32 devices in a mesh: dp: 2 (over core), blk: 4 (over y, x), hd: 4 (over z).
Axes of the slice: x: 2, y: 2, z: 4, core: 2. Of those that a mesh axis runs over, the one named last changes fastest.
Arguments:
- hidden_in: bfloat16 [2, 2048, 2048], P('dp', ('blk', 'hd')), may hold values from -6 to 6
- gain_attn: bfloat16 [2048], P(('dp', 'blk', 'hd')), may hold values from 0.25 to 1.75
- shift_attn: bfloat16 [2048], P(('dp', 'blk', 'hd')), may hold values from -3 to 3
- gain_mlp: bfloat16 [2048], P(('dp', 'blk', 'hd')), may hold values from 0.25 to 1.75
- shift_mlp: bfloat16 [2048], P(('dp', 'blk', 'hd')), may hold values from -3 to 3
- qkv_weight: bfloat16 [2048, 6144], P(('dp', 'blk', 'hd')), may hold values from -0.125 to 0.125
- qkv_bias: bfloat16 [6144], P(('dp', 'blk', 'hd')), may hold values from -3 to 3
- dense_weight: bfloat16 [2048, 2048], P(('dp', 'blk', 'hd')), may hold values from -1.5 to 1.5
- up_weight: bfloat16 [2048, 8192], P(('dp', 'blk', 'hd')), may hold values from -0.125 to 0.125
- up_bias: bfloat16 [8192], P(('dp', 'blk', 'hd')), may hold values from -3 to 3
- down_weight: bfloat16 [2048, 8192], P(('dp', 'blk', 'hd')), may hold values from -0.0625 to 0.0625
- out_bias: bfloat16 [2048], P(('dp', 'blk', 'hd')), may hold values from -3 to 3
- cotangent: bfloat16 [2, 2048, 2048], P('dp', ('blk', 'hd')), may hold values from -6 to 6
Outputs:
- output: bfloat16 [2, 2048, 2048], P('dp', ('blk', 'hd'))
- grad_hidden: float32 [2, 2048, 2048], P('dp', ('blk', 'hd'))
- grad_gain_attn: float32 [2048], P(('dp', 'blk', 'hd'))
- grad_shift_attn: float32 [2048], P(('dp', 'blk', 'hd'))
- grad_gain_mlp: float32 [2048], P(('dp', 'blk', 'hd'))
- grad_shift_mlp: float32 [2048], P(('dp', 'blk', 'hd'))
- grad_qkv_weight: float32 [2048, 6144], P(('dp', 'blk', 'hd'))
- grad_qkv_bias: float32 [6144], P(('dp', 'blk', 'hd'))
- grad_dense_weight: float32 [2048, 2048], P(('dp', 'blk', 'hd'))
- grad_up_weight: float32 [2048, 8192], P(('dp', 'blk', 'hd'))
- grad_up_bias: float32 [8192], P(('dp', 'blk', 'hd'))
- grad_down_weight: float32 [2048, 8192], P(('dp', 'blk', 'hd'))
- grad_out_bias: float32 [2048], P(('dp', 'blk', 'hd'))
The draws below stay inside these ranges and needn't reach their ends.
All inputs are finite; a program needn't handle non-finite values.
Results may differ from the reference program's by a relative error of at most 0.011.
Values may be sent and summed in bfloat16 or wider, within the bound.
No kernel may reach another device: no remote copies, remote signals or barrier semaphores. Data moves between devices by JAX's collectives and lax.ppermute only.
A program may use at most 640 MiB of HBM per device.

```python
import jax
import jax.numpy as jnp
from jax import lax

D = 2048
HEADS = 8
HS = 256
ROT = 64
FF = 8192
LEN = 2048
SEQS = 2


def block_levels(stream_key, dims, split, least, largest):
    def one(axis_at, blocks):
        steps = jax.random.uniform(jax.random.fold_in(jax.random.fold_in(stream_key, 6), axis_at), (blocks,), jnp.float32, least / len(split), largest / len(split))
        return jnp.repeat(jnp.exp(steps), dims[axis_at] // blocks).reshape((-1,) + (1,) * (len(dims) - axis_at - 1))

    gain = one(*split[0])
    for cut in split[1:]:
        gain = gain * one(*cut)
    return gain


def gaussian(key, shape, deviation, reach, split=(), held_as=jnp.bfloat16):
    values = deviation * jax.random.normal(key, shape, jnp.float32)
    if split:
        values = values * block_levels(key, shape, split, -0.22, 0.18)
    return jnp.clip(values, -reach, reach).astype(held_as)


def setup_inputs(seed: int = 0) -> dict:
    streams_of = jax.random.split(jax.random.key(seed), 14)
    return {
        "hidden_in": gaussian(streams_of[0], (SEQS, LEN, D), 1.0, 6.0, ((0, 2), (1, 16))),
        "gain_attn": jnp.clip(1.0 + 0.15 * jax.random.normal(streams_of[1], (D,), jnp.float32), 0.25, 1.75).astype(jnp.bfloat16),
        "shift_attn": gaussian(streams_of[2], (D,), 0.5, 3.0, ((0, 32),)),
        "gain_mlp": jnp.clip(1.0 + 0.15 * jax.random.normal(streams_of[3], (D,), jnp.float32), 0.25, 1.75).astype(jnp.bfloat16),
        "shift_mlp": gaussian(streams_of[4], (D,), 0.5, 3.0, ((0, 32),)),
        "qkv_weight": gaussian(streams_of[5], (D, 3 * D), D ** -0.5, 0.125, ((0, 32),)),
        "qkv_bias": gaussian(streams_of[6], (3 * D,), 0.5, 3.0, ((0, 32),)),
        "dense_weight": gaussian(streams_of[7], (D, D), (D // 128) ** -0.5, 1.5, ((0, 32),)),
        "up_weight": gaussian(streams_of[8], (D, FF), D ** -0.5, 0.125, ((0, 32),)),
        "up_bias": gaussian(streams_of[9], (FF,), 0.5, 3.0, ((0, 32),)),
        "down_weight": gaussian(streams_of[10], (D, FF), FF ** -0.5, 0.0625, ((0, 32),)),
        "out_bias": gaussian(streams_of[11], (D,), 0.5, 3.0, ((0, 32),)),
        "cotangent": gaussian(streams_of[12], (SEQS, LEN, D), 1.0, 6.0, ((0, 2), (1, 16))),
    }


@jax.custom_vjp
def low(v):
    return lax.optimization_barrier(v.astype(jnp.bfloat16)).astype(jnp.float32)

@jax.custom_vjp
def low_back(v):
    return v

def low_keep(v):
    return (low(v), None)

def low_pass(kept, grad):
    return (grad,)

def back_keep(v):
    return (v, None)

def back_low(kept, grad):
    return (low(grad),)
low.defvjp(low_keep, low_pass)
low_back.defvjp(back_keep, back_low)
epsilon = 1e-05
highest = lax.Precision.HIGHEST

def rotary_tables(positions):
    half_rot = ROT // 2
    frequency = 10000.0 ** (-(2.0 * jnp.arange(half_rot, dtype=jnp.float32)) / ROT)
    angles = positions[:, None] * frequency[None, :]
    return (jnp.cos(angles), jnp.sin(angles))

def rotate(values_in, cosine, sine):
    half_rot = ROT // 2
    first_half = values_in[..., :half_rot]
    second_half = values_in[..., half_rot:ROT]
    return jnp.concatenate([first_half * cosine - second_half * sine, second_half * cosine + first_half * sine, values_in[..., ROT:]], axis=-1)

def attention(query_rows, key_rows, value_rows):
    block_rows = min(512, LEN)
    blocks = LEN // block_rows
    scaling = HS ** (-0.5)
    key_places = jnp.arange(LEN, dtype=jnp.int32)

    def one_block(operands):
        query_block, first_row = operands
        scores = jnp.einsum('qhd,khd->hqk', query_block, key_rows, precision=highest)
        scores = low_back(scores * scaling)
        query_places = first_row + jnp.arange(block_rows, dtype=jnp.int32)
        visible = key_places[None, :] <= query_places[:, None]
        scores = jnp.where(visible[None], scores, -1e+30)
        weights = jax.nn.softmax(scores, axis=-1)
        return jnp.einsum('hqk,khd->qhd', low(weights), value_rows, precision=highest)
    stacked = query_rows.reshape(blocks, block_rows, HEADS, HS)
    firsts = jnp.arange(blocks, dtype=jnp.int32) * block_rows
    return lax.map(jax.checkpoint(one_block), (stacked, firsts)).reshape(LEN, HEADS, HS)

def layer(hidden, params):
    gain_attn, shift_attn, gain_mlp, shift_mlp, qkv_weight, qkv_bias, dense_weight, up_weight, up_bias, down_weight, out_bias = params
    average = lax.optimization_barrier(jnp.mean(hidden, axis=-1, keepdims=True))
    centered = hidden - average
    variance = lax.optimization_barrier(jnp.mean(centered * centered, axis=-1, keepdims=True))
    normed = centered * lax.rsqrt(variance + epsilon)
    attn_in = low(normed * gain_attn + shift_attn)
    mlp_in = low(normed * gain_mlp + shift_mlp)
    project = low_back(jnp.dot(attn_in, qkv_weight, precision=highest) + qkv_bias).reshape(LEN, 3, HEADS, HS)
    cosine, sine = rotary_tables(jnp.arange(LEN, dtype=jnp.float32))
    cosine = cosine[:, None, :]
    sine = sine[:, None, :]
    query_rows = low(low_back(rotate(project[:, 0], cosine, sine)))
    key_rows = low(low_back(rotate(project[:, 1], cosine, sine)))
    value_rows = low(low_back(project[:, 2]))
    attended = low(low_back(attention(query_rows, key_rows, value_rows).reshape(LEN, D)))
    hidden_pre = low_back(jnp.dot(mlp_in, up_weight, precision=highest) + up_bias)
    activated = low(jax.nn.gelu(hidden_pre, approximate=False))
    attn_out = jnp.dot(attended, dense_weight.T, precision=highest)
    mlp_out = jnp.dot(activated, down_weight.T, precision=highest)
    return hidden + attn_out + mlp_out + out_bias

def reference(hidden_in, gain_attn, shift_attn, gain_mlp, shift_mlp, qkv_weight, qkv_bias, dense_weight, up_weight, up_bias, down_weight, out_bias, cotangent):
    params = tuple((member.astype(jnp.float32) for member in (gain_attn, shift_attn, gain_mlp, shift_mlp, qkv_weight, qkv_bias, dense_weight, up_weight, up_bias, down_weight, out_bias)))

    def one_sequence(totals, operands):
        sequence, seq_grad = operands
        result, pullback = jax.vjp(layer, sequence.astype(jnp.float32), params)
        grad_input, grad_params = pullback(seq_grad.astype(jnp.float32))
        return (jax.tree.map(jnp.add, totals, grad_params), (result.astype(jnp.bfloat16), grad_input))
    initial = tuple((jnp.zeros_like(member) for member in params))
    totals, (output, grad_hidden) = lax.scan(one_sequence, initial, (hidden_in, cotangent))
    return (output, grad_hidden, totals[0], totals[1], totals[2], totals[3], totals[4], totals[5], totals[6], totals[7], totals[8], totals[9], totals[10])
```

```python
import jax
import jax.numpy as jnp
from jax import lax
from jax.sharding import Mesh, PartitionSpec as P

D = 2048
HEADS = 8
HS = 256
ROT = 64

TP = ("bl", "hd")
RP = ("dp", "bh")
ALL = ("dp", "bh", "bl", "hd")

epsilon = 1e-05
contract_last = (((1,), (1,)), ((), ()))
contract_first = (((0,), (0,)), ((), ()))
f32 = jnp.float32
bf16 = jnp.bfloat16


def rotary_tables(positions):
    half_rot = ROT // 2
    frequency = 10000.0 ** (-(2.0 * jnp.arange(half_rot, dtype=f32)) / ROT)
    angles = positions[:, None] * frequency[None, :]
    return (jnp.cos(angles), jnp.sin(angles))


def rotate(values_in, cosine, sine):
    half_rot = ROT // 2
    first_half = values_in[..., :half_rot]
    second_half = values_in[..., half_rot:ROT]
    return jnp.concatenate(
        [
            first_half * cosine - second_half * sine,
            second_half * cosine + first_half * sine,
            values_in[..., ROT:],
        ],
        axis=-1,
    )


def mm(a, b):
    return jnp.dot(a, b, preferred_element_type=f32)


def mm_nt(a, b):
    return lax.dot_general(a, b, contract_last, preferred_element_type=f32)


def mm_tn(a, b):
    return lax.dot_general(a, b, contract_first, preferred_element_type=f32)


def spread(shard):
    mine = lax.all_to_all(shard, TP, split_axis=1, concat_axis=0, tiled=True)
    return lax.all_gather(mine[:, 0], RP, axis=0, tiled=True)


def collect(partial):
    summed = lax.psum_scatter(partial.astype(bf16), RP, scatter_dimension=0, tiled=True)
    tp = lax.axis_size(TP)
    summed = summed.reshape(tp, summed.shape[0] // tp, summed.shape[1])
    return lax.all_to_all(summed, TP, split_axis=0, concat_axis=0, tiled=True).astype(f32)


def per_device(
    hidden_in,
    gain_attn,
    shift_attn,
    gain_mlp,
    shift_mlp,
    qkv_weight,
    qkv_bias,
    dense_weight,
    up_weight,
    up_bias,
    down_weight,
    out_bias,
    cotangent,
):
    seq_count, sub_len, _ = hidden_in.shape
    tp = lax.axis_size(TP)
    n_dev = lax.axis_size(ALL)
    t = lax.axis_index(TP)
    bh = lax.axis_index("bh")
    rows = qkv_weight.shape[0]
    ff = up_weight.shape[1]
    ffl = ff // tp
    scaling = HS ** (-0.5)
    group_len = sub_len * tp

    hidden_own = hidden_in.reshape(sub_len, D)
    g_own = cotangent.reshape(sub_len, D)
    smalls = jnp.concatenate(
        [gain_attn, shift_attn, gain_mlp, shift_mlp, out_bias, qkv_bias, up_bias]
    )
    smalls = lax.all_gather(smalls, ALL, axis=0, tiled=False).reshape(n_dev, -1).astype(f32)
    vecs = [smalls[:, i * rows : (i + 1) * rows].reshape(D) for i in range(5)]
    g_attn, s_attn, g_mlp, s_mlp, b_out = vecs
    nq = qkv_bias.shape[0]
    b_qkv = smalls[:, 5 * rows : 5 * rows + nq].reshape(3, HEADS, HS)
    b_up = smalls[:, 5 * rows + nq :].reshape(tp, ffl)
    b_qkv = lax.dynamic_index_in_dim(b_qkv, t, 1, keepdims=False).reshape(3 * HS)
    b_up = lax.dynamic_index_in_dim(b_up, t, 0, keepdims=False)

    x_all = lax.all_gather(hidden_own, TP, axis=0, tiled=True)
    w_up = spread(up_weight.reshape(rows, tp, ffl))
    w_qkv = spread(
        qkv_weight.reshape(rows, 3, HEADS, HS).transpose(0, 2, 1, 3).reshape(rows, HEADS, 3 * HS)
    )
    g_all = lax.all_gather(g_own, TP, axis=0, tiled=True)
    w_down = spread(down_weight.reshape(rows, tp, ffl))
    w_dense = spread(dense_weight.reshape(rows, HEADS, HS))

    hidden = x_all.astype(f32)
    average = jnp.mean(hidden, axis=1, keepdims=True)
    centered = hidden - average
    inverse = lax.rsqrt(jnp.mean(centered * centered, axis=1, keepdims=True) + epsilon)
    normed = centered * inverse
    attn_in = (normed * g_attn + s_attn).astype(bf16)
    mlp_in = (normed * g_mlp + s_mlp).astype(bf16)

    hidden_pre = mm(mlp_in, w_up) + b_up
    normal_cdf = 0.5 * (1.0 + lax.erf(hidden_pre * 0.7071067811865476))
    normal_density = jnp.exp(-0.5 * hidden_pre * hidden_pre) * 0.3989422804014327
    activated = (hidden_pre * normal_cdf).astype(bf16)
    grad_act = mm(g_all, w_down)
    grad_pre_up = (grad_act * (normal_cdf + hidden_pre * normal_density)).astype(bf16)
    down_term = mm_tn(g_all, activated)
    up_term = mm_tn(mlp_in, grad_pre_up)
    up_bias_term = jnp.sum(grad_pre_up.astype(f32), axis=0)

    project = mm(attn_in, w_qkv) + b_qkv
    query_places = bh * group_len + jnp.arange(group_len, dtype=jnp.int32)
    cosine, sine = rotary_tables(query_places.astype(f32))
    query = rotate(project[:, :HS], cosine, sine).astype(bf16)
    key = rotate(project[:, HS : 2 * HS], cosine, sine)
    kv = jnp.concatenate([key, project[:, 2 * HS :]], axis=1).astype(bf16)
    kv_all = lax.all_gather(kv, "bh", axis=0, tiled=True)
    key_all = kv_all[:, :HS]
    value_all = kv_all[:, HS:]
    visible = jnp.arange(kv_all.shape[0], dtype=jnp.int32)[None, :] <= query_places[:, None]
    scores = jnp.where(visible, mm_nt(query, key_all) * scaling, -1e30)
    row_max = jnp.max(scores, axis=1, keepdims=True)
    weights = jnp.exp(scores - row_max)
    weights = weights / jnp.sum(weights, axis=1, keepdims=True)
    weights_low = weights.astype(bf16)
    attended = mm(weights_low, value_all).astype(bf16)
    grad_att = mm(g_all, w_dense).astype(bf16)
    weight_grad = mm_nt(grad_att, value_all)
    row_delta = jnp.sum(weights * weight_grad, axis=1, keepdims=True)
    score_grad = (weights * (weight_grad - row_delta)).astype(bf16)
    grad_query = (mm(score_grad, key_all) * scaling).astype(bf16).astype(f32)
    grad_kv = jnp.concatenate(
        [mm_tn(score_grad, query) * scaling, mm_tn(weights_low, grad_att)], axis=1
    ).astype(bf16)
    grad_kv = lax.psum_scatter(grad_kv, "bh", scatter_dimension=0, tiled=True).astype(f32)
    grad_project = jnp.concatenate(
        [
            rotate(grad_query, cosine, -sine),
            rotate(grad_kv[:, :HS], cosine, -sine),
            grad_kv[:, HS:],
        ],
        axis=1,
    ).astype(bf16)
    qkv_bias_term = jnp.sum(grad_project.astype(f32), axis=0)
    dense_term = mm_tn(g_all, attended)
    qkv_term = mm_tn(attn_in, grad_project)

    projected = mm_nt(attended, w_dense) + mm_nt(activated, w_down)
    projected = lax.psum_scatter(
        projected.astype(bf16), TP, scatter_dimension=0, tiled=True
    ).astype(f32)
    output = (hidden_own.astype(f32) + projected + b_out).astype(bf16)

    grad_attn_in = mm_nt(grad_project, w_qkv)
    grad_mlp_in = mm_nt(grad_pre_up, w_up)
    terms = [
        jnp.sum(grad_attn_in * normed, axis=0),
        jnp.sum(grad_attn_in, axis=0),
        jnp.sum(grad_mlp_in * normed, axis=0),
        jnp.sum(grad_mlp_in, axis=0),
        jnp.sum(g_own.astype(f32), axis=0),
    ]
    grad_normed = (grad_attn_in * g_attn + grad_mlp_in * g_mlp).astype(bf16)
    grad_normed = lax.psum_scatter(grad_normed, TP, scatter_dimension=0, tiled=True).astype(f32)
    own = hidden_own.astype(f32)
    own_centered = own - jnp.mean(own, axis=1, keepdims=True)
    own_inverse = lax.rsqrt(
        jnp.mean(own_centered * own_centered, axis=1, keepdims=True) + epsilon
    )
    own_normed = own_centered * own_inverse
    grad_hidden = g_own.astype(f32) + own_inverse * (
        grad_normed
        - jnp.mean(grad_normed, axis=1, keepdims=True)
        - own_normed * jnp.mean(grad_normed * own_normed, axis=1, keepdims=True)
    )

    qkv_bias_full = lax.dynamic_update_slice(
        jnp.zeros((3, HEADS, HS), f32), qkv_bias_term.reshape(3, 1, HS), (0, t, 0)
    )
    up_bias_full = lax.dynamic_update_slice(
        jnp.zeros((tp, ffl), f32), up_bias_term.reshape(1, ffl), (t, 0)
    )
    small_terms = jnp.concatenate(
        [term.reshape(n_dev, rows) for term in terms]
        + [qkv_bias_full.reshape(n_dev, nq), up_bias_full.reshape(n_dev, ff // n_dev)],
        axis=1,
    )
    small = lax.all_to_all(small_terms, ALL, split_axis=0, concat_axis=0, tiled=True)
    small = jnp.sum(small, axis=0)
    down_grad = collect(down_term).transpose(1, 0, 2).reshape(rows, ff)
    up_grad = collect(up_term).transpose(1, 0, 2).reshape(rows, ff)
    dense_grad = collect(dense_term).transpose(1, 0, 2).reshape(rows, D)
    qkv_grad = (
        collect(qkv_term)
        .reshape(tp, rows, 3, HS)
        .transpose(1, 2, 0, 3)
        .reshape(rows, 3 * D)
    )
    return (
        output.reshape(seq_count, sub_len, D),
        grad_hidden.reshape(seq_count, sub_len, D),
        small[0 * rows : 1 * rows],
        small[1 * rows : 2 * rows],
        small[2 * rows : 3 * rows],
        small[3 * rows : 4 * rows],
        qkv_grad,
        small[5 * rows : 5 * rows + nq],
        dense_grad,
        up_grad,
        small[5 * rows + nq :],
        down_grad,
        small[4 * rows : 5 * rows],
    )


def solution(mesh):
    dp, blk, hd = (mesh.shape[name] for name in ("dp", "blk", "hd"))
    low = HEADS // hd
    inner = Mesh(mesh.devices.reshape(dp, blk // low, low, hd), ALL)
    token = P("dp", ("bh", "bl", "hd"), None)
    vector = P(ALL)
    matrix = P(ALL, None)
    return jax.shard_map(
        per_device,
        mesh=inner,
        in_specs=(
            token, vector, vector, vector, vector, matrix, vector,
            matrix, matrix, vector, matrix, vector, token,
        ),
        out_specs=(
            token, token, vector, vector, vector, vector, matrix, vector,
            matrix, matrix, vector, matrix, vector,
        ),
        check_vma=False,
    )
```

```python
import functools

import jax
import jax.numpy as jnp
from jax import lax
from jax.experimental import pallas as pl
from jax.experimental.pallas import tpu as pltpu
from jax.sharding import Mesh, PartitionSpec as P

D = 2048
HEADS = 8
HS = 256
ROT = 64

TP = ("bl", "hd")
RP = ("dp", "bh")
ALL = ("dp", "bh", "bl", "hd")

epsilon = 1e-05
contract_last = (((1,), (1,)), ((), ()))
f32 = jnp.float32
bf16 = jnp.bfloat16


def rotary_tables(positions):
    half_rot = ROT // 2
    frequency = 10000.0 ** (-(2.0 * jnp.arange(half_rot, dtype=f32)) / ROT)
    angles = positions[:, None] * frequency[None, :]
    cosine, sine = jnp.cos(angles), jnp.sin(angles)
    none = jnp.zeros_like(sine)
    rest = jnp.ones((positions.shape[0], 128 - ROT), f32)
    return (
        jnp.concatenate([cosine, cosine, rest], axis=1),
        jnp.concatenate([-sine, none, 0.0 * rest], axis=1),
        jnp.concatenate([none, sine, 0.0 * rest], axis=1),
    )


def mm(a, b):
    return jnp.dot(a, b, preferred_element_type=f32)


def mm_nt(a, b):
    return lax.dot_general(a, b, contract_last, preferred_element_type=f32)


def mm_tn(a, b):
    return lax.dot_general(a, b, (((0,), (0,)), ((), ())), preferred_element_type=f32)


def join(*values):
    return lax.optimization_barrier(values)


def swap(value, axis, distance):
    size = lax.axis_size(axis)
    return lax.ppermute(value, axis, [(i, i ^ distance) for i in range(size)])


def gather_axis(value, axis):
    return [value] + [swap(value, axis, d) for d in range(1, lax.axis_size(axis))]


def gather_start(value):
    size = lax.axis_size("hd")
    return [swap(value, "hd", d) for d in range(1, 3 if size == 4 else size)]


def gather_end(value, near):
    if lax.axis_size("hd") == 4:
        near = [near[0], near[1], swap(near[1], "hd", 1)]
    return [value] + near


def gather_rest(value):
    value = value[None]
    for axis in reversed(RP):
        place, size = lax.axis_index(axis), lax.axis_size(axis)
        bit = 1
        while bit < size:
            other = swap(value, axis, bit)
            upper = (place & bit) != 0
            value = jnp.concatenate(
                [jnp.where(upper, other, value), jnp.where(upper, value, other)], axis=0
            )
            bit *= 2
    return value


def groups():
    size = lax.axis_size("hd")
    part = size // 4
    return [list(range(size - (g + 1) * part, size - g * part)) for g in range(4)]


def send_far(terms, ds):
    return {d: [swap(term[d], "bl", far + 1) for far, term in enumerate(terms)] for d in ds}


def add_far(own, received):
    return {
        d: sum((other.astype(f32) for other in others), own[d])
        for d, others in received.items()
    }


def send_near(blocks, handed):
    four = lax.axis_size("hd") == 4
    out = {}
    for d, block in blocks.items():
        if d == 0:
            continue
        if four and d == 2:
            block = block + handed[3].astype(f32)
        out[d] = swap(block.astype(bf16), "hd", 1 if four and d == 3 else d)
    return out


def add_near(own, received):
    four = lax.axis_size("hd") == 4
    for d, block in received.items():
        if not (four and d == 3):
            own = own + block.astype(f32)
    return own


def spread_group(shard):
    mine = lax.all_to_all(shard, TP, split_axis=0, concat_axis=0, tiled=True)
    return mine.reshape(-1, shard.shape[2])


def spread_rest(mine):
    return lax.all_gather(mine, RP, axis=0, tiled=True)


def pick(value, axis, distance):
    return lax.dynamic_index_in_dim(value, lax.axis_index(axis) ^ distance, 0, keepdims=False)


def collect_dp(partial):
    partial = partial.reshape(lax.axis_size("dp"), -1, partial.shape[1])
    others = [swap(pick(partial, "dp", d), "dp", d) for d in range(1, lax.axis_size("dp"))]
    return pick(partial, "dp", 0), others


def collect_bh(own, others):
    total = sum((other.astype(f32) for other in others), own.astype(f32)).astype(bf16)
    total = total.reshape(lax.axis_size("bh"), -1, own.shape[1])
    others = [swap(pick(total, "bh", d), "bh", d) for d in range(1, lax.axis_size("bh"))]
    return pick(total, "bh", 0), others


def add_others(own, others):
    return sum((other.astype(f32) for other in others), own.astype(f32)).astype(bf16)


def collect_rest(partial):
    return lax.psum_scatter(partial, RP, scatter_dimension=0, tiled=True)


def collect_group(mine):
    mine = mine.reshape(lax.axis_size(TP), -1, mine.shape[1])
    return lax.all_to_all(mine, TP, split_axis=0, concat_axis=0, tiled=True)


TILE = 256
KEYS = 2048


def call(kernel, outs, *ins, scratch=(), grid=(), in_specs=None, out_specs=None):
    vmem = pl.BlockSpec(memory_space=pltpu.VMEM)
    return pl.pallas_call(
        kernel,
        grid=grid,
        out_shape=[jax.ShapeDtypeStruct(shape, dtype) for shape, dtype in outs],
        in_specs=in_specs or [vmem] * len(ins),
        out_specs=out_specs or [vmem] * len(outs),
        scratch_shapes=list(scratch),
        compiler_params=pltpu.CompilerParams(vmem_limit_bytes=58 * 2**20),
        cost_estimate=pl.CostEstimate(flops=1, bytes_accessed=1, transcendentals=0),
    )(*ins)


def tiles(count, step):
    def body(i, _):
        step(pl.ds(pl.multiple_of(i * TILE, TILE), TILE))
        return 0

    lax.fori_loop(0, count // TILE, body, 0)


def turn(value, tables, sign):
    own, above, below = tables
    first = value[:, :128]
    turned = first * own + sign * (
        pltpu.roll(first, 96, 1) * above + pltpu.roll(first, 32, 1) * below
    )
    return jnp.concatenate([turned, value[:, 128:]], axis=1)


def statistics(block):
    average = jnp.mean(block, axis=1, keepdims=True)
    centered = block - average
    return average, lax.rsqrt(jnp.mean(centered * centered, axis=1, keepdims=True) + epsilon)


def project_kernel(count, *refs):
    x_refs, refs = refs[:count], refs[count:]
    vec_ref, w_ref, b_ref, own_ref, above_ref, below_ref, *refs = refs
    attn_ref, mlp_ref, q_ref, kv_ref, average_ref, inverse_ref = refs
    rows = x_refs[0].shape[0]
    for start in range(0, count * rows, TILE):
        for i in range(start // rows, (start + TILE) // rows):
            at = slice(i * rows, (i + 1) * rows)
            block = x_refs[i][...].astype(f32)
            average, inverse = statistics(block)
            average_ref[at, :] = average
            inverse_ref[at, :] = inverse
            normed = (block - average) * inverse
            attn_ref[at, :] = (normed * vec_ref[0:1, :] + vec_ref[1:2, :]).astype(bf16)
            mlp_ref[at, :] = (normed * vec_ref[2:3, :] + vec_ref[3:4, :]).astype(bf16)
        at = slice(start, start + TILE)
        project = mm(attn_ref[at, :], w_ref[:, : 3 * HS]) + b_ref[...]
        tables = own_ref[at, :], above_ref[at, :], below_ref[at, :]
        query = turn(project[:, :HS], tables, 1.0).astype(bf16)
        q_ref[at, :] = (query.astype(f32) * HS**-0.5).astype(bf16)
        kv_ref[at, :HS] = turn(project[:, HS : 2 * HS], tables, 1.0).astype(bf16)
        kv_ref[at, HS:] = project[:, 2 * HS :].astype(bf16)


def cotangent_kernel(count, *refs):
    g_refs, (w_ref, g_ref, out_ref) = refs[:count], refs[count:]
    rows = g_refs[0].shape[0]
    for i in range(count):
        g_ref[i * rows : (i + 1) * rows, :] = g_refs[i][...]

    def step(at):
        out_ref[at, :] = mm(g_ref[at, :], w_ref[:, 3 * HS :]).astype(bf16)

    tiles(g_ref.shape[0], step)


def forward_kernel(mlp_ref, w_ref, b_ref, act_ref, slope_ref):
    def step(at):
        value = mm(mlp_ref[at, :], w_ref[...]) + b_ref[...]
        cdf = 0.5 * (1.0 + lax.erf(value * 0.7071067811865476))
        density = jnp.exp(-0.5 * value * value) * 0.3989422804014327
        act_ref[at, :] = (value * cdf).astype(bf16)
        slope_ref[at, :] = cdf + value * density

    tiles(mlp_ref.shape[0], step)


def backward_kernel(g_ref, w_ref, slope_ref, out_ref, sum_ref):
    sum_ref[...] = jnp.zeros_like(sum_ref)

    def step(at):
        grad = (mm(g_ref[at, :], w_ref[...]) * slope_ref[at, :]).astype(bf16)
        out_ref[at, :] = grad
        sum_ref[...] += jnp.sum(grad.astype(f32), axis=0, keepdims=True)

    tiles(g_ref.shape[0], step)


def output_kernel(att_ref, act_ref, dense_ref, down_ref, *out_refs):
    start = 0
    for out_ref in (out_refs[-1],) + out_refs[:-1]:
        at = slice(start, start + out_ref.shape[0])
        start += out_ref.shape[0]
        term = mm_nt(att_ref[at, :], dense_ref[...]) + mm_nt(act_ref[at, :], down_ref[...])
        out_ref[...] = term.astype(out_ref.dtype)


def output_terms(attended, activated, w_heads, w_down, kinds):
    count, ffl = activated.shape
    return call(
        output_kernel,
        [((rows, D), dtype) for rows, dtype in kinds],
        attended, activated, w_heads, w_down,
        grid=(D // TILE,),
        in_specs=[
            pl.BlockSpec((count, HS), lambda i: (0, 0)),
            pl.BlockSpec((count, ffl), lambda i: (0, 0)),
            pl.BlockSpec((TILE, HS), lambda i: (i, 3)),
            pl.BlockSpec((TILE, ffl), lambda i: (i, 0)),
        ],
        out_specs=[pl.BlockSpec((rows, TILE), lambda i: (0, i)) for rows, _ in kinds],
    )


def turn_back_kernel(count, *refs):
    dq_ref, refs = refs[0], refs[1:]
    term_refs, (own_ref, above_ref, below_ref, out_ref, sum_ref) = refs[:count], refs[count:]
    sum_ref[...] = jnp.zeros_like(sum_ref)

    def step(at):
        tables = own_ref[at, :], above_ref[at, :], below_ref[at, :]
        grad = term_refs[0][at, :].astype(f32)
        for ref in term_refs[1:]:
            grad += ref[at, :].astype(f32)
        grad = grad.astype(bf16)
        out_ref[at, :HS] = turn(dq_ref[at, :].astype(f32), tables, -1.0).astype(bf16)
        out_ref[at, HS : 2 * HS] = turn(grad[:, :HS].astype(f32), tables, -1.0).astype(bf16)
        out_ref[at, 2 * HS :] = grad[:, HS:]
        sum_ref[...] += jnp.sum(out_ref[at, :].astype(f32), axis=0, keepdims=True)

    tiles(dq_ref.shape[0], step)


def input_kernel(count, parts, *refs):
    x_refs, refs = refs[:count], refs[count:]
    average_ref, inverse_ref, gp_ref, gu_ref, heads_ref, up_ref, vec_ref = refs[:7]
    out_refs, sum_ref = refs[7:-1], refs[-1]
    rows = x_refs[0].shape[0]
    sums = [0.0] * 4
    order = (out_refs[-1],) + out_refs[:-1]
    reach = count * rows // parts
    for start in range(0, count * rows, TILE):
        at = slice(start, start + TILE)
        attn = mm_nt(gp_ref[at, :], heads_ref[...])
        mlp = mm_nt(gu_ref[at, :], up_ref[...])
        block = jnp.concatenate(
            [x_refs[i][...].astype(f32) for i in range(start // rows, (start + TILE) // rows)],
            axis=0,
        )
        normed = (block - average_ref[at, :]) * inverse_ref[at, :]
        for i, term in enumerate((attn * normed, attn, mlp * normed, mlp)):
            sums[i] = sums[i] + jnp.sum(term, axis=0, keepdims=True)
        out = attn * vec_ref[0:1, :] + mlp * vec_ref[2:3, :]
        out_ref = order[start // reach]
        out_ref[start % reach : start % reach + TILE, :] = out.astype(out_ref.dtype)
    sum_ref[...] = jnp.concatenate(sums, axis=0)


def input_terms(x_blocks, average, inverse, grad_project, grad_pre_up, w_heads, w_up, vectors, kinds):
    count, ffl = grad_pre_up.shape
    whole = lambda rows, cols: pl.BlockSpec((rows, cols), lambda i: (0, 0))
    return call(
        functools.partial(input_kernel, len(x_blocks), len(kinds)),
        [((rows, D), dtype) for rows, dtype in kinds] + [((4, D), f32)],
        *x_blocks, average, inverse, grad_project, grad_pre_up, w_heads, w_up, vectors,
        grid=(D // TILE,),
        in_specs=[
            *[pl.BlockSpec((block.shape[0], TILE), lambda i: (0, i)) for block in x_blocks],
            whole(count, 1),
            whole(count, 1),
            whole(count, 3 * HS),
            whole(count, ffl),
            pl.BlockSpec((TILE, 3 * HS), lambda i: (i, 0)),
            pl.BlockSpec((TILE, ffl), lambda i: (i, 0)),
            pl.BlockSpec((vectors.shape[0], TILE), lambda i: (0, i)),
        ],
        out_specs=[
            *[pl.BlockSpec((rows, TILE), lambda i: (0, i)) for rows, _ in kinds],
            pl.BlockSpec((4, TILE), lambda i: (0, i)),
        ],
    )


def attention_kernel(q_ref, g_ref, kv_ref, qpos_ref, kpos_ref, o_ref, dq_ref, dkv_ref, sum_ref):
    count, tile = q_ref.shape[0], TILE
    keys = kv_ref[:, :HS]
    values = kv_ref[:, HS:]
    keys_turned = keys.T
    values_turned = values.T
    sum_ref[...] = jnp.zeros_like(sum_ref)

    def step(i, _):
        at = pl.ds(pl.multiple_of(i * tile, tile), tile)
        query = q_ref[at, :]
        grad = g_ref[at, :]
        scores = mm_nt(keys, query)
        scores = jnp.where(kpos_ref[...] <= qpos_ref[:, at], scores, -1e30)
        weights = jnp.exp(scores - jnp.max(scores, axis=0, keepdims=True))
        weights = weights * (1.0 / jnp.sum(weights, axis=0, keepdims=True))
        weights_low = weights.astype(bf16)
        o_ref[at, :] = mm(values_turned, weights_low).T.astype(bf16)
        sum_ref[:, HS:] += mm(weights_low, grad)
        weight_grad = mm_nt(values, grad)
        delta = jnp.sum(weights * weight_grad, axis=0, keepdims=True)
        score_grad = (weights * (weight_grad - delta)).astype(bf16)
        dq_ref[at, :] = (mm(keys_turned, score_grad).T * (HS**-0.5)).astype(bf16)
        sum_ref[:, :HS] += mm(score_grad, query)
        return 0

    lax.fori_loop(0, count // tile, step, 0)
    dkv_ref[...] = sum_ref[...].astype(bf16)


def long_attention_kernel(q_ref, g_ref, kv_ref, qpos_ref, kpos_ref, o_ref, dq_ref, dkv_ref, sum_ref):
    blocks = kv_ref.shape[0] // KEYS
    sum_ref[...] = jnp.zeros_like(sum_ref)

    def step(at):
        query = q_ref[at, :]
        grad = g_ref[at, :]

        def scores_of(j):
            here = pl.ds(pl.multiple_of(j * KEYS, KEYS), KEYS)
            scores = mm_nt(kv_ref[here, :HS], query)
            return here, jnp.where(kpos_ref[here, :] <= qpos_ref[:, at], scores, -1e30)

        def first(j, state):
            top, total = state
            _, scores = scores_of(j)
            higher = jnp.maximum(top, jnp.max(scores, axis=0, keepdims=True))
            now = jnp.sum(jnp.exp(scores - higher), axis=0, keepdims=True)
            return higher, total * jnp.exp(top - higher) + now

        row = (1, TILE)
        top, total = lax.fori_loop(
            0, blocks, first, (jnp.full(row, -1e30, f32), jnp.zeros(row, f32))
        )
        inverse = 1.0 / total

        def second(j, state):
            result, delta = state
            here, scores = scores_of(j)
            weights = jnp.exp(scores - top) * inverse
            values = kv_ref[here, HS:]
            weight_grad = mm_nt(values, grad)
            result = result + mm(values.T, weights.astype(bf16))
            return result, delta + jnp.sum(weights * weight_grad, axis=0, keepdims=True)

        result, delta = lax.fori_loop(
            0, blocks, second, (jnp.zeros((HS, TILE), f32), jnp.zeros(row, f32))
        )
        o_ref[at, :] = result.T.astype(bf16)

        def third(j, result):
            here, scores = scores_of(j)
            weights = jnp.exp(scores - top) * inverse
            weight_grad = mm_nt(kv_ref[here, HS:], grad)
            score_grad = (weights * (weight_grad - delta)).astype(bf16)
            sum_ref[here, HS:] += mm(weights.astype(bf16), grad)
            sum_ref[here, :HS] += mm(score_grad, query)
            return result + mm(kv_ref[here, :HS].T, score_grad)

        result = lax.fori_loop(0, blocks, third, jnp.zeros((HS, TILE), f32))
        dq_ref[at, :] = (result.T * (HS**-0.5)).astype(bf16)

    tiles(q_ref.shape[0], step)
    dkv_ref[...] = sum_ref[...].astype(bf16)


def per_device(
    hidden_in,
    gain_attn,
    shift_attn,
    gain_mlp,
    shift_mlp,
    qkv_weight,
    qkv_bias,
    dense_weight,
    up_weight,
    up_bias,
    down_weight,
    out_bias,
    cotangent,
):
    seq_count, sub_len, _ = hidden_in.shape
    tp, rp = lax.axis_size(TP), lax.axis_size(RP)
    n_dev = lax.axis_size(ALL)
    t = lax.axis_index(TP)
    bh, bh_size, bl_size = lax.axis_index("bh"), lax.axis_size("bh"), lax.axis_size("bl")
    rows = qkv_weight.shape[0]
    ff = up_weight.shape[1]
    ffl = ff // tp
    group_len = sub_len * tp
    reach = lax.axis_size("hd") * sub_len

    x_own = hidden_in.reshape(sub_len, D)
    g_own = cotangent.reshape(sub_len, D)
    smalls = jnp.concatenate(
        [
            vector.reshape(-1, rows)
            for vector in (
                gain_attn, shift_attn, gain_mlp, shift_mlp, out_bias, qkv_bias, up_bias
            )
        ],
        axis=0,
    )
    kinds = smalls.shape[0]
    smalls = gather_rest(smalls).reshape(-1, 4 * HS)
    extra = 8 * -(-smalls.shape[0] // 8)
    smalls = jnp.pad(smalls, ((0, extra - smalls.shape[0]), (0, 0)))
    heads_own = jnp.concatenate(
        [
            qkv_weight.reshape(rows, 3, HEADS, HS).transpose(2, 0, 1, 3).reshape(HEADS, rows, 3 * HS),
            dense_weight.reshape(rows, HEADS, HS).transpose(1, 0, 2),
        ],
        axis=2,
    )
    heads_own = jnp.concatenate(
        [heads_own, jnp.broadcast_to(smalls[None], (tp,) + smalls.shape)], axis=1
    )
    up_own = up_weight.reshape(rows, tp, ffl).transpose(1, 0, 2)
    down_own = down_weight.reshape(rows, tp, ffl).transpose(1, 0, 2)

    x_near = gather_start(x_own)
    x_side = gather_axis(x_own, "bl")
    g_side = gather_axis(g_own, "bl")
    x_near, x_side, g_side, heads_own = join(x_near, x_side, g_side, heads_own)
    m_heads = lax.all_to_all(heads_own, TP, split_axis=0, concat_axis=0, tiled=True)
    x_rows = [x_side] + [gather_axis(block, "bl") for block in x_near[:2]]
    x_near = gather_end(x_own, x_near)
    x_near, x_rows, m_heads, up_own, g_late = join(x_near, x_rows, m_heads, up_own, g_own)
    w_heads = spread_rest(m_heads[:, :rows].reshape(tp * rows, -1))
    x_rows += [gather_axis(block, "bl") for block in x_near[3:]]
    g_first = swap(g_late, "hd", 1)
    m_up = spread_group(up_own)
    smalls = m_heads[:, rows:].reshape(tp, -1)[:, : rp * kinds * rows]
    smalls = smalls.reshape(tp, rp, kinds, rows).transpose(1, 0, 2, 3).reshape(n_dev, kinds, rows)
    smalls = smalls.astype(f32)
    vectors = smalls[:, :5].transpose(1, 0, 2).reshape(5, D)
    nq = qkv_bias.shape[0] // rows
    b_qkv = smalls[:, 5 : 5 + nq].reshape(3, HEADS, HS)
    b_up = smalls[:, 5 + nq :].reshape(tp, ffl)
    b_qkv = lax.dynamic_index_in_dim(b_qkv, t, 1, keepdims=False).reshape(1, 3 * HS)
    b_up = lax.dynamic_index_in_dim(b_up, t, 0, keepdims=True)

    row = jnp.arange(group_len, dtype=jnp.int32)
    inside = ((row // sub_len) ^ t) * sub_len + row % sub_len
    query_places = bh * group_len + inside
    key_places = jnp.concatenate([(bh ^ d) * group_len + inside for d in range(bh_size)])
    tables = rotary_tables(query_places.astype(f32))

    x_rows, g_first, m_up, g_late, down_own, vectors, b_qkv, tables = join(
        x_rows, g_first, m_up, g_late, down_own, vectors, b_qkv, tables
    )
    w_up = spread_rest(m_up)
    x_blocks = [row[far] for far in range(bl_size) for row in x_rows]
    g_rows = [g_side, gather_axis(g_first, "bl")]
    m_down = spread_group(down_own)
    attn_in, mlp_in, query, kv, average, inverse = call(
        functools.partial(project_kernel, tp),
        [
            ((group_len, D), bf16),
            ((group_len, D), bf16),
            ((group_len, HS), bf16),
            ((group_len, 2 * HS), bf16),
            ((group_len, 1), f32),
            ((group_len, 1), f32),
        ],
        *x_blocks, vectors, w_heads, b_qkv, *tables,
    )
    g_rows, m_down, kv, mlp_in, g_late = join(g_rows, m_down, kv, mlp_in, g_late)
    w_down = spread_rest(m_down)
    kv_blocks = gather_axis(kv, "bh")
    hd_size = lax.axis_size("hd")
    g_near = [g_first] + [swap(g_late, "hd", d) for d in range(2, 3 if hd_size == 4 else hd_size)]
    g_near, kv_blocks, mlp_in = join(g_near, kv_blocks, mlp_in)
    g_near = gather_end(g_late, g_near)
    g_rows += [gather_axis(block, "bl") for block in g_near[2:]]
    activated, slope = call(
        forward_kernel, [((group_len, ffl), bf16), ((group_len, ffl), f32)], mlp_in, w_up, b_up
    )
    g_rows, activated, slope = join(g_rows, activated, slope)
    g_blocks = [row[far] for far in range(bl_size) for row in g_rows]
    g_all, grad_att = call(
        functools.partial(cotangent_kernel, tp),
        [((group_len, D), bf16), ((group_len, HS), bf16)],
        *g_blocks, w_heads,
    )
    down_half = collect_dp(mm_tn(g_all, activated).astype(bf16))
    kv_all = jnp.concatenate(kv_blocks, axis=0)
    down_half, grad_att, kv_all = join(down_half, grad_att, kv_all)
    down_mine = collect_bh(*down_half)
    attended, grad_query, grad_kv = call(
        attention_kernel if kv_all.shape[0] <= KEYS else long_attention_kernel,
        [
            ((group_len, HS), bf16),
            ((group_len, HS), bf16),
            ((kv_all.shape[0], 2 * HS), bf16),
        ],
        query, grad_att, kv_all, query_places[None, :], key_places[:, None],
        scratch=[pltpu.VMEM((kv_all.shape[0], 2 * HS), f32)],
    )
    attended, grad_query, grad_kv, down_mine = join(attended, grad_query, grad_kv, down_mine)
    grad_kv = grad_kv.reshape(bh_size, group_len, 2 * HS)
    grad_kv = [grad_kv[0]] + [swap(grad_kv[d], "bh", d) for d in range(1, bh_size)]
    down_grad = collect_group(add_others(*down_mine))
    kinds = [(reach, bf16)] * (bl_size - 1) + [(reach, f32)]
    *out_far, out_own = [
        term.reshape(-1, sub_len, D)
        for term in output_terms(attended, activated, w_heads, w_down, kinds)
    ]
    grad_pre_up, up_bias_term = call(
        backward_kernel, [((group_len, ffl), bf16), ((1, ffl), f32)], g_all, w_down, slope
    )
    up_term = mm_tn(mlp_in, grad_pre_up).astype(bf16)
    grad_kv, down_grad, grad_pre_up, up_term, out_far, out_own = join(
        grad_kv, down_grad, grad_pre_up, up_term, out_far, out_own
    )
    parts = groups()
    up_mine = collect_rest(up_term)
    far = send_far(out_far, parts[0])
    grad_project, qkv_bias_term = call(
        functools.partial(turn_back_kernel, bh_size),
        [((group_len, 3 * HS), bf16), ((1, 3 * HS), f32)],
        grad_query, *grad_kv, *tables,
    )
    qkv_term = mm_tn(attn_in, grad_project).astype(bf16)
    dense_term = mm_tn(g_all, attended).astype(bf16)
    far, qkv_term, dense_term, grad_project, out_far = join(
        far, qkv_term, dense_term, grad_project, out_far
    )
    qkv_half, dense_half = collect_dp(qkv_term), collect_dp(dense_term)
    handed = send_near(add_far(out_own, far), {})
    far = send_far(out_far, parts[1])
    *in_far, in_own, sums = input_terms(
        x_blocks, average, inverse, grad_project, grad_pre_up, w_heads, w_up, vectors, kinds
    )
    in_far = [term.reshape(-1, sub_len, D) for term in in_far]
    in_own = in_own.reshape(-1, sub_len, D)
    qkv_half, dense_half, handed, far, in_far, in_own, out_far = join(
        qkv_half, dense_half, handed, far, in_far, in_own, out_far
    )
    qkv_mine, dense_mine = collect_bh(*qkv_half), collect_bh(*dense_half)
    near = handed | send_near(add_far(out_own, far), handed)
    far = send_far(out_far, parts[2] + parts[3])
    qkv_mine, dense_mine, near, far, in_far = join(qkv_mine, dense_mine, near, far, in_far)
    heads_grad = collect_group(
        jnp.concatenate([add_others(*qkv_mine), add_others(*dense_mine)], axis=1)
    )
    rest = add_far(out_own, far)
    near = near | send_near(rest, {})
    far = send_far(in_far, parts[0] + parts[1])
    projected = rest[0]
    down_grad = down_grad.astype(f32).transpose(1, 0, 2).reshape(rows, ff)
    heads_grad, near, far, in_far, down_grad, up_mine, projected = join(
        heads_grad, near, far, in_far, down_grad, up_mine, projected
    )
    output = (x_own.astype(f32) + add_near(projected, near) + vectors[4:5]).astype(bf16)
    up_grad = collect_group(up_mine)
    upper = add_far(in_own, far)
    handed = send_near({d: upper[d] for d in parts[0]}, {})
    far = send_far(in_far, parts[2] + parts[3])
    heads_grad = heads_grad.astype(f32)
    dense_grad = heads_grad[:, :, 3 * HS :].transpose(1, 0, 2).reshape(rows, D)
    qkv_grad = (
        heads_grad[:, :, : 3 * HS]
        .reshape(tp, rows, 3, HS)
        .transpose(1, 2, 0, 3)
        .reshape(rows, 3 * D)
    )
    sums = jnp.concatenate([sums, jnp.sum(g_own.astype(f32), axis=0, keepdims=True)], axis=0)
    qkv_bias_full = lax.dynamic_update_slice(
        jnp.zeros((3, HEADS, HS), f32), qkv_bias_term.reshape(3, 1, HS), (0, t, 0)
    )
    up_bias_full = lax.dynamic_update_slice(jnp.zeros((tp, ffl), f32), up_bias_term, (t, 0))
    small_terms = jnp.concatenate(
        [
            sums.reshape(5, n_dev, rows).transpose(1, 0, 2),
            qkv_bias_full.reshape(n_dev, nq, rows),
            up_bias_full.reshape(n_dev, -1, rows),
        ],
        axis=1,
    )
    upper = {d: upper[d] for d in parts[1]}
    up_grad, handed, far, output, dense_grad, qkv_grad, small_terms, upper = join(
        up_grad, handed, far, output, dense_grad, qkv_grad, small_terms, upper
    )
    lower = add_far(in_own, far)
    near = handed | send_near(upper | lower, handed)
    small = lax.all_to_all(small_terms, ALL, split_axis=0, concat_axis=0, tiled=True)
    up_grad = up_grad.astype(f32).transpose(1, 0, 2).reshape(rows, ff)
    near, small, up_grad = join(near, small, up_grad)
    grad_normed = add_near(lower[0], near)
    small = jnp.sum(small, axis=0)
    own = x_own.astype(f32)
    own_average, own_inverse = statistics(own)
    own_normed = (own - own_average) * own_inverse
    grad_hidden = g_own.astype(f32) + own_inverse * (
        grad_normed
        - jnp.mean(grad_normed, axis=1, keepdims=True)
        - own_normed * jnp.mean(grad_normed * own_normed, axis=1, keepdims=True)
    )
    return (
        output.reshape(seq_count, sub_len, D),
        grad_hidden.reshape(seq_count, sub_len, D),
        small[0],
        small[1],
        small[2],
        small[3],
        qkv_grad,
        small[5 : 5 + nq].reshape(-1),
        dense_grad,
        up_grad,
        small[5 + nq :].reshape(-1),
        down_grad,
        small[4],
    )


def solution(mesh):
    dp, blk, hd = (mesh.shape[name] for name in ("dp", "blk", "hd"))
    low = HEADS // hd
    inner = Mesh(mesh.devices.reshape(dp, blk // low, low, hd), ALL)
    token = P("dp", ("bh", "bl", "hd"), None)
    vector = P(ALL)
    matrix = P(ALL, None)
    return jax.shard_map(
        per_device,
        mesh=inner,
        in_specs=(
            token, vector, vector, vector, vector, matrix, vector,
            matrix, matrix, vector, matrix, vector, token,
        ),
        out_specs=(
            token, token, vector, vector, vector, vector, matrix, vector,
            matrix, matrix, vector, matrix, vector,
        ),
        check_vma=False,
    )
```

```python
import functools

import jax
import jax.numpy as jnp
from jax import lax
from jax.experimental import pallas as pl
from jax.experimental.pallas import tpu as pltpu
from jax.sharding import Mesh, PartitionSpec as P

D = 2048
HEADS = 8
HS = 256
ROT = 64

TP = ("bl", "hd")
RP = ("dp", "bh")
ALL = ("dp", "bh", "bl", "hd")

epsilon = 1e-05
contract_last = (((1,), (1,)), ((), ()))
f32 = jnp.float32
bf16 = jnp.bfloat16


def rotary_tables(positions):
    half_rot = ROT // 2
    frequency = 10000.0 ** (-(2.0 * jnp.arange(half_rot, dtype=f32)) / ROT)
    angles = positions[:, None] * frequency[None, :]
    cosine, sine = jnp.cos(angles), jnp.sin(angles)
    none = jnp.zeros_like(sine)
    rest = jnp.ones((positions.shape[0], 128 - ROT), f32)
    return (
        jnp.concatenate([cosine, cosine, rest], axis=1),
        jnp.concatenate([-sine, none, 0.0 * rest], axis=1),
        jnp.concatenate([none, sine, 0.0 * rest], axis=1),
    )


def mm(a, b):
    return jnp.dot(a, b, preferred_element_type=f32)


def mm_nt(a, b):
    return lax.dot_general(a, b, contract_last, preferred_element_type=f32)


class Order:
    def __init__(self, token):
        self.token = token

    def join(self, *values):
        self.token, values = lax.optimization_barrier((self.token, values))
        return values


def swap(value, axis, distance):
    size = lax.axis_size(axis)
    return lax.ppermute(value, axis, [(i, i ^ distance) for i in range(size)])


def gather_axis(value, axis):
    return [value] + [swap(value, axis, d) for d in range(1, lax.axis_size(axis))]


def gather_start(value):
    size = lax.axis_size("hd")
    return [swap(value, "hd", d) for d in range(1, 3 if size == 4 else size)]


def gather_end(value, near):
    if lax.axis_size("hd") == 4:
        near = [near[0], near[1], swap(near[1], "hd", 1)]
    return [value] + near


def gather_rest(value):
    value = value[None]
    for axis in reversed(RP):
        place, size = lax.axis_index(axis), lax.axis_size(axis)
        bit = 1
        while bit < size:
            other = swap(value, axis, bit)
            upper = (place & bit) != 0
            value = jnp.concatenate(
                [jnp.where(upper, other, value), jnp.where(upper, value, other)], axis=0
            )
            bit *= 2
    return value


def hand_on(value, distance):
    if lax.axis_size("hd") == 4 and distance == 3:
        distance = 1
    return swap(value, "hd", distance)


def spread_group(shard):
    mine = lax.all_to_all(shard, TP, split_axis=0, concat_axis=0, tiled=True)
    return mine.reshape(-1, shard.shape[2])


def spread_rest(mine):
    return lax.all_gather(mine, RP, axis=0, tiled=True)


def collect_group(mine):
    mine = mine.reshape(lax.axis_size(TP), -1, mine.shape[1])
    return lax.all_to_all(mine, TP, split_axis=0, concat_axis=0, tiled=True)


TILE = 256
KEYS = 2048


def call(kernel, outs, *ins, scratch=(), grid=(), in_specs=None, out_specs=None):
    vmem = pl.BlockSpec(memory_space=pltpu.VMEM)
    return pl.pallas_call(
        kernel,
        grid=grid,
        out_shape=[jax.ShapeDtypeStruct(shape, dtype) for shape, dtype in outs],
        in_specs=in_specs or [vmem] * len(ins),
        out_specs=out_specs or [vmem] * len(outs),
        scratch_shapes=list(scratch),
        compiler_params=pltpu.CompilerParams(vmem_limit_bytes=58 * 2**20),
        cost_estimate=pl.CostEstimate(flops=1, bytes_accessed=1, transcendentals=0),
    )(*ins)


def tiles(count, step):
    def body(i, _):
        step(pl.ds(pl.multiple_of(i * TILE, TILE), TILE))
        return 0

    lax.fori_loop(0, count // TILE, body, 0)


def add_kernel(counts, *refs):
    start = 0
    ins = refs[: sum(count for count, _ in counts)]
    outs = refs[len(ins) :]
    for count, parts in counts:
        group, ins = ins[:count], ins[count:]
        here, outs = outs[:parts], outs[parts:]
        start = 0
        for out_ref in here:
            at = slice(start, start + out_ref.shape[0])
            start += out_ref.shape[0]
            total = group[0][at, :].astype(f32)
            for ref in group[1:]:
                total += ref[at, :].astype(f32)
            out_ref[...] = total.astype(out_ref.dtype)


def add(*groups):
    counts, outs, ins = [], [], []
    for arrays, dtype, parts in groups:
        rows, cols = arrays[0].shape
        counts.append((len(arrays), parts))
        outs += [((rows // parts, cols), dtype)] * parts
        ins += arrays
    sums = call(functools.partial(add_kernel, counts), outs, *ins)
    result = []
    for _, parts in counts:
        result.append(list(sums[:parts]))
        sums = sums[parts:]
    return result


def turn(value, tables, sign):
    own, above, below = tables
    first = value[:, :128]
    turned = first * own + sign * (
        pltpu.roll(first, 96, 1) * above + pltpu.roll(first, 32, 1) * below
    )
    return jnp.concatenate([turned, value[:, 128:]], axis=1)


def statistics(block):
    average = jnp.mean(block, axis=1, keepdims=True)
    centered = block - average
    return average, lax.rsqrt(jnp.mean(centered * centered, axis=1, keepdims=True) + epsilon)


def project_kernel(count, *refs):
    x_refs, refs = refs[:count], refs[count:]
    vec_ref, w_ref, b_ref, own_ref, above_ref, below_ref, *refs = refs
    attn_ref, mlp_ref, q_ref, kv_ref, average_ref, inverse_ref = refs
    rows = x_refs[0].shape[0]
    for start in range(0, count * rows, TILE):
        for i in range(start // rows, (start + TILE) // rows):
            at = slice(i * rows, (i + 1) * rows)
            block = x_refs[i][...].astype(f32)
            average, inverse = statistics(block)
            average_ref[at, :] = average
            inverse_ref[at, :] = inverse
            normed = (block - average) * inverse
            attn_ref[at, :] = (normed * vec_ref[0:1, :] + vec_ref[1:2, :]).astype(bf16)
            mlp_ref[at, :] = (normed * vec_ref[2:3, :] + vec_ref[3:4, :]).astype(bf16)
        at = slice(start, start + TILE)
        project = mm(attn_ref[at, :], w_ref[...]) + b_ref[...]
        tables = own_ref[at, :], above_ref[at, :], below_ref[at, :]
        query = turn(project[:, :HS], tables, 1.0).astype(bf16)
        q_ref[at, :] = (query.astype(f32) * HS**-0.5).astype(bf16)
        kv_ref[at, :HS] = turn(project[:, HS : 2 * HS], tables, 1.0).astype(bf16)
        kv_ref[at, HS:] = project[:, 2 * HS :].astype(bf16)


def cotangent_kernel(count, *refs):
    g_refs, (w_ref, g_ref, out_ref) = refs[:count], refs[count:]
    rows = g_refs[0].shape[0]
    for i in range(count):
        g_ref[i * rows : (i + 1) * rows, :] = g_refs[i][...]

    def step(at):
        out_ref[at, :] = mm(g_ref[at, :], w_ref[...]).astype(bf16)

    tiles(g_ref.shape[0], step)


def forward_kernel(mlp_ref, w_ref, b_ref, act_ref, slope_ref):
    def step(at):
        value = mm(mlp_ref[at, :], w_ref[...]) + b_ref[...]
        cdf = 0.5 * (1.0 + lax.erf(value * 0.7071067811865476))
        density = jnp.exp(-0.5 * value * value) * 0.3989422804014327
        act_ref[at, :] = (value * cdf).astype(bf16)
        slope_ref[at, :] = cdf + value * density

    tiles(mlp_ref.shape[0], step)


def forward(mlp_in, w_up, b_up):
    count, ffl = mlp_in.shape[0], w_up.shape[1]
    columns = pl.BlockSpec((count, TILE), lambda i: (0, i))
    return call(
        forward_kernel,
        [((count, ffl), bf16), ((count, ffl), f32)],
        mlp_in, w_up, b_up,
        grid=(ffl // TILE,),
        in_specs=[
            pl.BlockSpec((count, D), lambda i: (0, 0)),
            pl.BlockSpec((D, TILE), lambda i: (0, i)),
            pl.BlockSpec((1, TILE), lambda i: (0, i)),
        ],
        out_specs=[columns, columns],
    )


def backward_kernel(g_ref, w_ref, slope_ref, out_ref, sum_ref):
    grad = (mm(g_ref[...], w_ref[...]) * slope_ref[...]).astype(bf16)
    out_ref[...] = grad
    sum_ref[...] = jnp.sum(grad.astype(f32), axis=0, keepdims=True)


def backward(g_all, w_down, slope):
    count, ffl = slope.shape
    columns = pl.BlockSpec((count, TILE), lambda i: (0, i))
    return call(
        backward_kernel,
        [((count, ffl), bf16), ((1, ffl), f32)],
        g_all, w_down, slope,
        grid=(ffl // TILE,),
        in_specs=[
            pl.BlockSpec((count, D), lambda i: (0, 0)),
            pl.BlockSpec((D, TILE), lambda i: (0, i)),
            columns,
        ],
        out_specs=[columns, pl.BlockSpec((1, TILE), lambda i: (0, i))],
    )


def weight_kernel(steps, place_ref, *refs):
    pairs, (far_ref, own_ref) = refs[:-2], refs[-2:]

    def store(out_ref):
        start = 0
        for lhs_ref, rhs_ref in zip(pairs[::2], pairs[1::2]):
            cols = slice(start, start + rhs_ref.shape[1])
            start += rhs_ref.shape[1]
            out_ref[:, cols] = mm(lhs_ref[...].T, rhs_ref[...]).astype(bf16)

    pl.when(pl.program_id(0) < steps)(lambda: store(far_ref))
    pl.when(pl.program_id(0) >= steps)(lambda: store(own_ref))


def weight_terms(*pairs):
    bh = lax.axis_size("bh")
    part = D // (2 * bh)
    tile = min(2 * TILE, part)
    per = part // tile
    steps = bh * per
    place = jnp.stack([lax.axis_index("dp"), lax.axis_index("bh")]).astype(jnp.int32)

    def lhs_at(i, place_ref):
        core = place_ref[0] ^ jnp.where(i < steps, 1, 0)
        block = place_ref[1] ^ (i % steps // per)
        return (0, (core * bh + block) * per + i % per)

    count = pairs[0].shape[0]
    cols = sum(rhs.shape[1] for rhs in pairs[1::2])
    specs = []
    for rhs in pairs[1::2]:
        specs.append(pl.BlockSpec((count, tile), lhs_at))
        specs.append(pl.BlockSpec(rhs.shape, lambda i, place_ref: (0, 0)))
    return pl.pallas_call(
        functools.partial(weight_kernel, steps),
        grid_spec=pltpu.PrefetchScalarGridSpec(
            num_scalar_prefetch=1,
            grid=(2 * steps,),
            in_specs=specs,
            out_specs=[
                pl.BlockSpec((tile, cols), lambda i, place_ref: (jnp.minimum(i, steps - 1), 0)),
                pl.BlockSpec((tile, cols), lambda i, place_ref: (jnp.maximum(i - steps, 0), 0)),
            ],
        ),
        out_shape=[jax.ShapeDtypeStruct((D // 2, cols), bf16)] * 2,
        compiler_params=pltpu.CompilerParams(vmem_limit_bytes=58 * 2**20),
        cost_estimate=pl.CostEstimate(flops=1, bytes_accessed=1, transcendentals=0),
    )(place, *pairs)


def output_kernel(att_ref, act_ref, dense_ref, down_ref, *out_refs):
    term = mm_nt(att_ref[...], dense_ref[...]) + mm_nt(act_ref[...], down_ref[...])
    rows = out_refs[0].shape[0]
    for i, out_ref in enumerate(out_refs):
        out_ref[...] = term[i * rows : (i + 1) * rows].astype(out_ref.dtype)


def output_terms(attended, activated, w_heads, w_down, part, count, rows, dtype):
    ffl, wide = activated.shape[1], 4 * TILE if count * rows <= 512 else 2 * TILE
    return call(
        output_kernel,
        [((rows, D), dtype)] * count,
        attended, activated, w_heads, w_down,
        grid=(D // wide,),
        in_specs=[
            pl.BlockSpec((count * rows, HS), lambda i: (part, 0)),
            pl.BlockSpec((count * rows, ffl), lambda i: (part, 0)),
            pl.BlockSpec((wide, HS), lambda i: (i, 3)),
            pl.BlockSpec((wide, ffl), lambda i: (i, 0)),
        ],
        out_specs=[pl.BlockSpec((rows, wide), lambda i: (0, i))] * count,
    )


def turn_back_kernel(count, *refs):
    dq_ref, refs = refs[0], refs[1:]
    term_refs, (own_ref, above_ref, below_ref, out_ref, sum_ref) = refs[:count], refs[count:]
    sum_ref[...] = jnp.zeros_like(sum_ref)

    def step(at):
        tables = own_ref[at, :], above_ref[at, :], below_ref[at, :]
        grad = term_refs[0][at, :].astype(f32)
        for ref in term_refs[1:]:
            grad += ref[at, :].astype(f32)
        grad = grad.astype(bf16)
        out_ref[at, :HS] = turn(dq_ref[at, :].astype(f32), tables, -1.0).astype(bf16)
        out_ref[at, HS : 2 * HS] = turn(grad[:, :HS].astype(f32), tables, -1.0).astype(bf16)
        out_ref[at, 2 * HS :] = grad[:, HS:]
        sum_ref[...] += jnp.sum(out_ref[at, :].astype(f32), axis=0, keepdims=True)

    tiles(dq_ref.shape[0], step)


def input_kernel(count, *refs):
    x_refs, refs = refs[:count], refs[count:]
    average_ref, inverse_ref, gp_ref, gu_ref, heads_ref, up_ref, vec_ref = refs[:7]
    out_refs, sum_ref = refs[7:-1], refs[-1]
    rows = x_refs[0].shape[0]
    sums = [0.0] * 4
    for start in range(0, count * rows, TILE):
        at = slice(start, start + TILE)
        attn = mm_nt(gp_ref[at, :], heads_ref[...])
        mlp = mm_nt(gu_ref[at, :], up_ref[...])
        block = jnp.concatenate(
            [x_refs[i][...].astype(f32) for i in range(start // rows, (start + TILE) // rows)],
            axis=0,
        )
        normed = (block - average_ref[at, :]) * inverse_ref[at, :]
        for i, term in enumerate((attn * normed, attn, mlp * normed, mlp)):
            sums[i] = sums[i] + jnp.sum(term, axis=0, keepdims=True)
        out = attn * vec_ref[0:1, :] + mlp * vec_ref[2:3, :]
        for i in range(0, TILE, rows):
            out_ref = out_refs[(start + i) // rows]
            out_ref[...] = out[i : i + rows].astype(out_ref.dtype)
    sum_ref[...] = jnp.concatenate(sums, axis=0)


def input_terms(x_blocks, average, inverse, grad_project, grad_pre_up, w_heads, w_up, vectors, own):
    count, ffl = grad_pre_up.shape
    whole = lambda rows, cols: pl.BlockSpec((rows, cols), lambda i: (0, 0))
    block = pl.BlockSpec((x_blocks[0].shape[0], TILE), lambda i: (0, i))
    *terms, sums = call(
        functools.partial(input_kernel, len(x_blocks)),
        [(x.shape, f32 if i < own else bf16) for i, x in enumerate(x_blocks)] + [((4, D), f32)],
        *x_blocks, average, inverse, grad_project, grad_pre_up, w_heads, w_up, vectors,
        grid=(D // TILE,),
        in_specs=[
            *[block] * len(x_blocks),
            whole(count, 1),
            whole(count, 1),
            whole(count, 3 * HS),
            whole(count, ffl),
            pl.BlockSpec((TILE, 3 * HS), lambda i: (i, 0)),
            pl.BlockSpec((TILE, ffl), lambda i: (i, 0)),
            pl.BlockSpec((vectors.shape[0], TILE), lambda i: (0, i)),
        ],
        out_specs=[*[block] * len(x_blocks), pl.BlockSpec((4, TILE), lambda i: (0, i))],
    )
    return terms, sums


def attention_kernel(count, q_ref, g_ref, qpos_ref, kpos_ref, *refs):
    kv_refs, (o_ref, dq_ref), refs = refs[:count], refs[count : count + 2], refs[count + 2 :]
    dkv_refs, sum_ref = refs[:-1], refs[-1]
    keys = jnp.concatenate([ref[:, :HS] for ref in kv_refs], axis=0)
    values = jnp.concatenate([ref[:, HS:] for ref in kv_refs], axis=0)
    keys_turned = keys.T
    values_turned = values.T
    sum_ref[...] = jnp.zeros_like(sum_ref)

    def step(at):
        query = q_ref[at, :]
        grad = g_ref[at, :]
        scores = mm_nt(keys, query)
        scores = jnp.where(kpos_ref[...] <= qpos_ref[:, at], scores, -1e30)
        weights = jnp.exp(scores - jnp.max(scores, axis=0, keepdims=True))
        weights = weights * (1.0 / jnp.sum(weights, axis=0, keepdims=True))
        weights_low = weights.astype(bf16)
        o_ref[at, :] = mm(values_turned, weights_low).T.astype(bf16)
        sum_ref[:, HS:] += mm(weights_low, grad)
        weight_grad = mm_nt(values, grad)
        delta = jnp.sum(weights * weight_grad, axis=0, keepdims=True)
        score_grad = (weights * (weight_grad - delta)).astype(bf16)
        dq_ref[at, :] = (mm(keys_turned, score_grad).T * (HS**-0.5)).astype(bf16)
        sum_ref[:, :HS] += mm(score_grad, query)

    tiles(q_ref.shape[0], step)
    start = 0
    for ref in dkv_refs:
        ref[...] = sum_ref[start : start + ref.shape[0], :].astype(bf16)
        start += ref.shape[0]


def long_attention_kernel(q_ref, g_ref, kv_ref, qpos_ref, kpos_ref, o_ref, dq_ref, dkv_ref, sum_ref):
    blocks = kv_ref.shape[0] // KEYS
    sum_ref[...] = jnp.zeros_like(sum_ref)

    def step(at):
        query = q_ref[at, :]
        grad = g_ref[at, :]

        def scores_of(j):
            here = pl.ds(pl.multiple_of(j * KEYS, KEYS), KEYS)
            scores = mm_nt(kv_ref[here, :HS], query)
            return here, jnp.where(kpos_ref[here, :] <= qpos_ref[:, at], scores, -1e30)

        def first(j, state):
            top, total = state
            _, scores = scores_of(j)
            higher = jnp.maximum(top, jnp.max(scores, axis=0, keepdims=True))
            now = jnp.sum(jnp.exp(scores - higher), axis=0, keepdims=True)
            return higher, total * jnp.exp(top - higher) + now

        row = (1, TILE)
        top, total = lax.fori_loop(
            0, blocks, first, (jnp.full(row, -1e30, f32), jnp.zeros(row, f32))
        )
        inverse = 1.0 / total

        def second(j, state):
            result, delta = state
            here, scores = scores_of(j)
            weights = jnp.exp(scores - top) * inverse
            values = kv_ref[here, HS:]
            weight_grad = mm_nt(values, grad)
            result = result + mm(values.T, weights.astype(bf16))
            return result, delta + jnp.sum(weights * weight_grad, axis=0, keepdims=True)

        result, delta = lax.fori_loop(
            0, blocks, second, (jnp.zeros((HS, TILE), f32), jnp.zeros(row, f32))
        )
        o_ref[at, :] = result.T.astype(bf16)

        def third(j, result):
            here, scores = scores_of(j)
            weights = jnp.exp(scores - top) * inverse
            weight_grad = mm_nt(kv_ref[here, HS:], grad)
            score_grad = (weights * (weight_grad - delta)).astype(bf16)
            sum_ref[here, HS:] += mm(weights.astype(bf16), grad)
            sum_ref[here, :HS] += mm(score_grad, query)
            return result + mm(kv_ref[here, :HS].T, score_grad)

        result = lax.fori_loop(0, blocks, third, jnp.zeros((HS, TILE), f32))
        dq_ref[at, :] = (result.T * (HS**-0.5)).astype(bf16)

    tiles(q_ref.shape[0], step)
    dkv_ref[...] = sum_ref[...].astype(bf16)


def attention(query, grad, kv_blocks, qpos, kpos):
    count, total = len(kv_blocks), kpos.shape[0]
    low = (query.shape, bf16)
    scratch = [pltpu.VMEM((total, 2 * HS), f32)]
    if total <= KEYS:
        attended, grad_query, *grad_kv = call(
            functools.partial(attention_kernel, count),
            [low, low] + [(block.shape, bf16) for block in kv_blocks],
            query, grad, qpos, kpos, *kv_blocks,
            scratch=scratch,
        )
        return attended, grad_query, grad_kv
    kv_all = jnp.concatenate(kv_blocks, axis=0)
    attended, grad_query, grad_kv = call(
        long_attention_kernel, [low, low, (kv_all.shape, bf16)], query, grad, kv_all, qpos, kpos,
        scratch=scratch,
    )
    return attended, grad_query, jnp.split(grad_kv, count, axis=0)


def per_device(
    hidden_in,
    gain_attn,
    shift_attn,
    gain_mlp,
    shift_mlp,
    qkv_weight,
    qkv_bias,
    dense_weight,
    up_weight,
    up_bias,
    down_weight,
    out_bias,
    cotangent,
):
    seq_count, sub_len, _ = hidden_in.shape
    tp, rp = lax.axis_size(TP), lax.axis_size(RP)
    n_dev = lax.axis_size(ALL)
    t = lax.axis_index(TP)
    bh, bh_size, bl_size = lax.axis_index("bh"), lax.axis_size("bh"), lax.axis_size("bl")
    rows = qkv_weight.shape[0]
    ff = up_weight.shape[1]
    ffl = ff // tp
    group_len = sub_len * tp

    vmem = pl.BlockSpec(memory_space=pltpu.VMEM)
    x_own = hidden_in.reshape(sub_len, D)
    join = Order(out_bias).join
    g_own = cotangent.reshape(sub_len, D)
    smalls = jnp.concatenate(
        [
            vector.reshape(-1, rows)
            for vector in (
                gain_attn, shift_attn, gain_mlp, shift_mlp, out_bias, qkv_bias, up_bias
            )
        ],
        axis=0,
    )
    kinds = smalls.shape[0]
    smalls = gather_rest(smalls).reshape(-1, 4 * HS)
    extra = 8 * -(-smalls.shape[0] // 8)
    smalls = jnp.pad(smalls, ((0, extra - smalls.shape[0]), (0, 0)))
    heads_own = jnp.concatenate(
        [
            qkv_weight.reshape(rows, 3, HEADS, HS).transpose(2, 0, 1, 3).reshape(HEADS, rows, 3 * HS),
            dense_weight.reshape(rows, HEADS, HS).transpose(1, 0, 2),
        ],
        axis=2,
    )
    heads_own = jnp.concatenate(
        [heads_own, jnp.broadcast_to(smalls[None], (tp,) + smalls.shape)], axis=1
    )
    up_own = up_weight.reshape(rows, tp, ffl).transpose(1, 0, 2)
    down_own = down_weight.reshape(rows, tp, ffl).transpose(1, 0, 2)

    x_near = gather_start(x_own)
    x_side = gather_axis(x_own, "bl")
    g_side = gather_axis(g_own, "bl")
    x_near, x_side, g_side, heads_own = join(x_near, x_side, g_side, heads_own)
    m_heads = lax.all_to_all(heads_own, TP, split_axis=0, concat_axis=0, tiled=True)
    x_rows = [x_side] + [gather_axis(block, "bl") for block in x_near[:2]]
    x_near = gather_end(x_own, x_near)
    row = jnp.arange(group_len, dtype=jnp.int32)
    inside = ((row // sub_len) ^ t) * sub_len + row % sub_len
    query_places = bh * group_len + inside
    key_places = jnp.concatenate([(bh ^ d) * group_len + inside for d in range(bh_size)])
    tables = rotary_tables(query_places.astype(f32))
    x_near, x_rows, m_heads, up_own, g_late, tables, query_places, key_places = join(
        x_near, x_rows, m_heads, up_own, g_own, tables, query_places[None, :], key_places[:, None]
    )
    w_heads = spread_rest(m_heads[:, :rows].reshape(tp * rows, -1))
    x_rows += [gather_axis(block, "bl") for block in x_near[3:]]
    g_first = swap(g_late, "hd", 1)
    m_up = spread_group(up_own)
    smalls = m_heads[:, rows:].reshape(tp, -1)[:, : rp * kinds * rows]
    smalls = smalls.reshape(tp, rp, kinds, rows).transpose(1, 0, 2, 3).reshape(n_dev, kinds, rows)
    smalls = smalls.astype(f32)
    vectors = smalls[:, :5].transpose(1, 0, 2).reshape(5, D)
    nq = qkv_bias.shape[0] // rows
    b_qkv = smalls[:, 5 : 5 + nq].reshape(3, HEADS, HS)
    b_up = smalls[:, 5 + nq :].reshape(tp, ffl)
    b_qkv = lax.dynamic_index_in_dim(b_qkv, t, 1, keepdims=False).reshape(1, 3 * HS)
    b_up = lax.dynamic_index_in_dim(b_up, t, 0, keepdims=True)

    x_rows, g_first, m_up, g_late, down_own, vectors, b_qkv, b_up = join(
        x_rows, g_first, m_up, g_late, down_own, vectors, b_qkv, b_up
    )
    w_up = spread_rest(m_up)
    x_blocks = [row[far] for far in range(bl_size) for row in x_rows]
    g_rows = [g_side, gather_axis(g_first, "bl")]
    hd_size = lax.axis_size("hd")
    four = hd_size == 4
    g_near = [g_first] + [swap(g_late, "hd", d) for d in range(2, 3 if hd_size == 4 else hd_size)]
    attn_in, mlp_in, query, kv, average, inverse = call(
        functools.partial(project_kernel, tp),
        [
            ((group_len, D), bf16),
            ((group_len, D), bf16),
            ((group_len, HS), bf16),
            ((group_len, 2 * HS), bf16),
            ((group_len, 1), f32),
            ((group_len, 1), f32),
        ],
        *x_blocks, vectors, w_heads, b_qkv, *tables,
        grid=(1,),
        in_specs=[vmem] * (tp + 1) + [pl.BlockSpec((D, 3 * HS), lambda i: (0, 0))] + [vmem] * 4,
    )
    g_rows, g_near, kv, mlp_in, g_late, down_own = join(
        g_rows, g_near, kv, mlp_in, g_late, down_own
    )
    g_near = gather_end(g_late, g_near)
    g_rows += [gather_axis(block, "bl") for block in g_near[2:3]]
    g_rows, g_near, kv, down_own, mlp_in = join(g_rows, g_near, kv, down_own, mlp_in)
    g_rows += [gather_axis(block, "bl") for block in g_near[3:]]
    kv_blocks = gather_axis(kv, "bh")
    m_down = spread_group(down_own)
    activated, slope = forward(mlp_in, w_up, b_up)
    g_rows, kv_blocks, m_down, activated, slope = join(g_rows, kv_blocks, m_down, activated, slope)
    w_down = spread_rest(m_down)
    g_blocks = [row[far] for far in range(bl_size) for row in g_rows]
    g_all, grad_att = call(
        functools.partial(cotangent_kernel, tp),
        [((group_len, D), bf16), ((group_len, HS), bf16)],
        *g_blocks, w_heads,
        grid=(1,),
        in_specs=[vmem] * tp + [pl.BlockSpec((D, HS), lambda i: (0, 3))],
    )
    down_far, down_own = weight_terms(g_all, activated)
    down_far, down_own, grad_att = join(down_far, down_own, grad_att)
    down_far = swap(down_far, "dp", 1)
    down_far, grad_att = join(down_far, grad_att)
    ((down_mine),) = add(([down_far, down_own], bf16, bh_size))
    down_mine, grad_att = join(down_mine, grad_att)
    down_others = [swap(down_mine[d], "bh", d) for d in range(1, bh_size)]
    attended, grad_query, grad_kv = attention(
        query, grad_att, kv_blocks, query_places, key_places
    )
    hd_terms = (hd_size, sub_len)
    out_far = [
        output_terms(attended, activated, w_heads, w_down, far, *hd_terms, bf16)
        for far in range(1, bl_size)
    ]
    down_others, out_far, attended, grad_kv, slope = join(
        down_others, out_far, attended, grad_kv, slope
    )
    part = hd_size // 4
    parts = [range(hd_size - (g + 1) * part, hd_size - g * part) for g in range(4)]

    def over_bl(terms, ds):
        return {d: [swap(term[d], "bl", f + 1) for f, term in enumerate(terms)] for d in ds}

    def sums_of(own, received, ds, handed=()):
        return [
            ([own[d], *received[d], *(handed if d == 2 else ())], f32 if d == 0 else bf16, 1)
            for d in ds
        ]

    ((down_last,),) = add(([down_mine[0], *down_others], bf16, 1))
    down_last, attended, slope = join(down_last, attended, slope)
    kv_others = [swap(grad_kv[d], "bh", d) for d in range(1, bh_size)]
    down_grad = collect_group(down_last)
    received = over_bl(out_far, parts[0])
    grad_pre_up, up_bias_term = backward(g_all, w_down, slope)
    out_own = output_terms(attended, activated, w_heads, w_down, 0, *hd_terms, f32)
    up_far, up_own = weight_terms(mlp_in, grad_pre_up)
    kv_others, down_grad, received, grad_pre_up, out_own, up_far, up_own, out_far = join(
        kv_others, down_grad, received, grad_pre_up, out_own, up_far, up_own, out_far
    )
    out = dict(zip(parts[0], add(*sums_of(out_own, received, parts[0]))))
    out, kv_others, up_far = join(out, kv_others, up_far)
    out_near = {d: hand_on(out[d][0], d) for d in parts[0]}
    received = over_bl(out_far, [*parts[1], *parts[2]])
    up_far = swap(up_far, "dp", 1)
    grad_project, qkv_bias_term = call(
        functools.partial(turn_back_kernel, bh_size),
        [((group_len, 3 * HS), bf16), ((1, 3 * HS), f32)],
        grad_query, grad_kv[0], *kv_others, *tables,
    )
    heads_far, heads_own = weight_terms(attn_in, grad_project, g_all, attended)
    out_near, received, up_far, grad_project, heads_far, heads_own, out_far = join(
        out_near, received, up_far, grad_project, heads_far, heads_own, out_far
    )
    middle = [*parts[1], *parts[2]]
    up_mine, *out = add(
        ([up_far, up_own], bf16, bh_size),
        *sums_of(out_own, received, middle, [out_near[3]] if four else []),
    )
    up_mine, out, grad_project, heads_far = join(up_mine, out, grad_project, heads_far)
    out_near |= {d: hand_on(term, d) for d, (term,) in zip(middle, out)}
    received = over_bl(out_far, parts[3])
    up_others = [swap(up_mine[d], "bh", d) for d in range(1, bh_size)]
    heads_far = swap(heads_far, "dp", 1)
    in_terms, sums = input_terms(
        x_blocks, average, inverse, grad_project, grad_pre_up, w_heads, w_up, vectors, hd_size
    )
    out_near, received, up_others, heads_far, in_terms = join(
        out_near, received, up_others, heads_far, in_terms
    )
    in_own = in_terms[:hd_size]
    in_far = [in_terms[f * hd_size : (f + 1) * hd_size] for f in range(1, bl_size)]
    (up_last,), heads_mine = add(
        ([up_mine[0], *up_others], bf16, 1), ([heads_far, heads_own], bf16, bh_size)
    )
    up_last, heads_mine, in_far = join(up_last, heads_mine, in_far)
    up_grad = collect_group(up_last)
    heads_others = [swap(heads_mine[d], "bh", d) for d in range(1, bh_size)]
    received_in = over_bl(in_far, parts[0])
    sums = jnp.concatenate([sums, jnp.sum(g_own.astype(f32), axis=0, keepdims=True)], axis=0)
    qkv_bias_full = lax.dynamic_update_slice(
        jnp.zeros((3, HEADS, HS), f32), qkv_bias_term.reshape(3, 1, HS), (0, t, 0)
    )
    up_bias_full = lax.dynamic_update_slice(jnp.zeros((tp, ffl), f32), up_bias_term, (t, 0))
    small_terms = jnp.concatenate(
        [
            sums.reshape(5, n_dev, rows).transpose(1, 0, 2),
            qkv_bias_full.reshape(n_dev, nq, rows),
            up_bias_full.reshape(n_dev, -1, rows),
        ],
        axis=1,
    )
    up_grad, heads_others, received_in, small_terms, in_far, in_own = join(
        up_grad, heads_others, received_in, small_terms, in_far, in_own
    )
    (heads_last,), *ins = add(
        ([heads_mine[0], *heads_others], bf16, 1), *sums_of(in_own, received_in, parts[0])
    )
    heads_last, ins, in_far = join(heads_last, ins, in_far)
    heads_grad = collect_group(heads_last)
    in_near = {d: hand_on(term, d) for d, (term,) in zip(parts[0], ins)}
    received_in = over_bl(in_far, middle)
    down_grad = down_grad.astype(f32).transpose(1, 0, 2).reshape(rows, ff)
    up_grad = up_grad.astype(f32).transpose(1, 0, 2).reshape(rows, ff)
    heads_grad, in_near, received_in, down_grad, up_grad, in_far, in_own, small_terms = join(
        heads_grad, in_near, received_in, down_grad, up_grad, in_far, in_own, small_terms
    )
    ins = add(*sums_of(in_own, received_in, middle, [in_near[3]] if four else []))
    ins, in_far, small_terms, heads_grad = join(ins, in_far, small_terms, heads_grad)
    in_near |= {d: hand_on(term, d) for d, (term,) in zip(middle, ins)}
    received_in = over_bl(in_far, parts[3])
    small = lax.all_to_all(small_terms, ALL, split_axis=0, concat_axis=0, tiled=True)
    heads_grad = heads_grad.astype(f32)
    dense_grad = heads_grad[:, :, 3 * HS :].transpose(1, 0, 2).reshape(rows, D)
    qkv_grad = (
        heads_grad[:, :, : 3 * HS]
        .reshape(tp, rows, 3, HS)
        .transpose(1, 2, 0, 3)
        .reshape(rows, 3 * D)
    )

    def total(own, received, near):
        rest = {d: sum((x.astype(f32) for x in received[d]), own[d]) for d in received}
        near = near | {d: hand_on(rest[d].astype(bf16), d) for d in rest if d}
        straight = [d for d in range(1, hd_size) if not (four and d == 3)]
        return sum((near[d].astype(f32) for d in straight), rest[0])

    projected = total(out_own, received, out_near)
    output = (x_own.astype(f32) + projected + vectors[4:5]).astype(bf16)
    in_near, received_in, small, dense_grad, qkv_grad, output, in_own = join(
        in_near, received_in, small, dense_grad, qkv_grad, output, in_own
    )
    small = jnp.sum(small, axis=0)
    grad_normed = total(in_own, received_in, in_near)
    own = x_own.astype(f32)
    own_average, own_inverse = statistics(own)
    own_normed = (own - own_average) * own_inverse
    grad_hidden = g_own.astype(f32) + own_inverse * (
        grad_normed
        - jnp.mean(grad_normed, axis=1, keepdims=True)
        - own_normed * jnp.mean(grad_normed * own_normed, axis=1, keepdims=True)
    )
    return (
        output.reshape(seq_count, sub_len, D),
        grad_hidden.reshape(seq_count, sub_len, D),
        small[0],
        small[1],
        small[2],
        small[3],
        qkv_grad,
        small[5 : 5 + nq].reshape(-1),
        dense_grad,
        up_grad,
        small[5 + nq :].reshape(-1),
        down_grad,
        small[4],
    )


def solution(mesh):
    dp, blk, hd = (mesh.shape[name] for name in ("dp", "blk", "hd"))
    low = HEADS // hd
    inner = Mesh(mesh.devices.reshape(dp, blk // low, low, hd), ALL)
    token = P("dp", ("bh", "bl", "hd"), None)
    vector = P(ALL)
    matrix = P(ALL, None)
    return jax.shard_map(
        per_device,
        mesh=inner,
        in_specs=(
            token, vector, vector, vector, vector, matrix, vector,
            matrix, matrix, vector, matrix, vector, token,
        ),
        out_specs=(
            token, token, vector, vector, vector, vector, matrix, vector,
            matrix, matrix, vector, matrix, vector,
        ),
        check_vma=False,
    )
```

```python
import functools

import jax
import jax.numpy as jnp
from jax import lax
from jax.experimental import pallas as pl
from jax.experimental.pallas import tpu as pltpu
from jax.sharding import Mesh, PartitionSpec as P

D = 2048
HEADS = 8
HS = 256
ROT = 64

TP = ("bl", "hd")
RP = ("dp", "bh")
ALL = ("dp", "bh", "bl", "hd")

epsilon = 1e-05
contract_last = (((1,), (1,)), ((), ()))
f32 = jnp.float32
bf16 = jnp.bfloat16


def rotary_tables(positions):
    half_rot = ROT // 2
    frequency = 10000.0 ** (-(2.0 * jnp.arange(half_rot, dtype=f32)) / ROT)
    angles = positions[:, None] * frequency[None, :]
    cosine, sine = jnp.cos(angles), jnp.sin(angles)
    none = jnp.zeros_like(sine)
    rest = jnp.ones((positions.shape[0], 128 - ROT), f32)
    return (
        jnp.concatenate([cosine, cosine, rest], axis=1),
        jnp.concatenate([-sine, none, 0.0 * rest], axis=1),
        jnp.concatenate([none, sine, 0.0 * rest], axis=1),
    )


def mm(a, b):
    return jnp.dot(a, b, preferred_element_type=f32)


def mm_nt(a, b):
    return lax.dot_general(a, b, contract_last, preferred_element_type=f32)


class Order:
    def __init__(self, token):
        self.token = token

    def join(self, *values):
        self.token, values = lax.optimization_barrier((self.token, values))
        return values


def swap(value, axis, distance):
    size = lax.axis_size(axis)
    return lax.ppermute(value, axis, [(i, i ^ distance) for i in range(size)])


def gather_axis(value, axis):
    return [value] + [swap(value, axis, d) for d in range(1, lax.axis_size(axis))]


def gather_start(value):
    size = lax.axis_size("hd")
    return [swap(value, "hd", d) for d in range(1, 3 if size == 4 else size)]


def gather_end(value, near):
    if lax.axis_size("hd") == 4:
        near = [near[0], near[1], swap(near[1], "hd", 1)]
    return [value] + near


def gather_rest(value):
    place, size = lax.axis_index(RP), lax.axis_size(RP)
    blocks = jnp.stack([value] + [swap(value, RP, d) for d in range(1, size)])
    bit = 1
    while bit < size:
        pairs = blocks.reshape((size // (2 * bit), 2, bit) + value.shape)
        turned = jnp.stack([pairs[:, 1], pairs[:, 0]], axis=1).reshape(blocks.shape)
        blocks = jnp.where((place & bit) != 0, turned, blocks)
        bit *= 2
    return blocks


def hand_on(value, distance):
    if lax.axis_size("hd") == 4 and distance == 3:
        distance = 1
    return swap(value, "hd", distance)


def spread_group(shard):
    mine = lax.all_to_all(shard, TP, split_axis=0, concat_axis=0, tiled=True)
    return mine.reshape(-1, shard.shape[2])


def spread_rest(mine):
    return lax.all_gather(mine, RP, axis=0, tiled=True)


def collect_rest(terms):
    return lax.psum_scatter(terms, RP, scatter_dimension=0, tiled=True)


def collect_group(mine):
    mine = mine.reshape(lax.axis_size(TP), -1, mine.shape[1])
    return lax.all_to_all(mine, TP, split_axis=0, concat_axis=0, tiled=True)


TILE = 256
KEYS = 2048


def call(kernel, outs, *ins, scratch=(), grid=(), in_specs=None, out_specs=None):
    vmem = pl.BlockSpec(memory_space=pltpu.VMEM)
    return pl.pallas_call(
        kernel,
        grid=grid,
        out_shape=[jax.ShapeDtypeStruct(shape, dtype) for shape, dtype in outs],
        in_specs=in_specs or [vmem] * len(ins),
        out_specs=out_specs or [vmem] * len(outs),
        scratch_shapes=list(scratch),
        compiler_params=pltpu.CompilerParams(vmem_limit_bytes=58 * 2**20),
        cost_estimate=pl.CostEstimate(flops=1, bytes_accessed=1, transcendentals=0),
    )(*ins)


def tiles(count, step):
    def body(i, _):
        step(pl.ds(pl.multiple_of(i * TILE, TILE), TILE))
        return 0

    lax.fori_loop(0, count // TILE, body, 0)


def add(*groups):
    return [
        [sum((x.astype(f32) for x in arrays[1:]), arrays[0].astype(f32)).astype(dtype)]
        for arrays, dtype, _ in groups
    ]


def turn(value, tables, sign):
    own, above, below = tables
    first = value[:, :128]
    turned = first * own + sign * (
        pltpu.roll(first, 96, 1) * above + pltpu.roll(first, 32, 1) * below
    )
    return jnp.concatenate([turned, value[:, 128:]], axis=1)


def statistics(block):
    average = jnp.mean(block, axis=1, keepdims=True)
    centered = block - average
    return average, lax.rsqrt(jnp.mean(centered * centered, axis=1, keepdims=True) + epsilon)


def project_kernel(count, *refs):
    x_refs, refs = refs[:count], refs[count:]
    vec_ref, w_ref, b_ref, own_ref, above_ref, below_ref, *refs = refs
    attn_ref, mlp_ref, q_ref, kv_ref, average_ref, inverse_ref = refs
    rows = x_refs[0].shape[0]
    for start in range(0, count * rows, TILE):
        for i in range(start // rows, (start + TILE) // rows):
            at = slice(i * rows, (i + 1) * rows)
            block = x_refs[i][...].astype(f32)
            average, inverse = statistics(block)
            average_ref[at, :] = average
            inverse_ref[at, :] = inverse
            normed = (block - average) * inverse
            attn_ref[at, :] = (normed * vec_ref[0:1, :] + vec_ref[1:2, :]).astype(bf16)
            mlp_ref[at, :] = (normed * vec_ref[2:3, :] + vec_ref[3:4, :]).astype(bf16)
        at = slice(start, start + TILE)
        project = mm(attn_ref[at, :], w_ref[...]) + b_ref[...]
        tables = own_ref[at, :], above_ref[at, :], below_ref[at, :]
        query = turn(project[:, :HS], tables, 1.0).astype(bf16)
        q_ref[at, :] = (query.astype(f32) * HS**-0.5).astype(bf16)
        kv_ref[at, :HS] = turn(project[:, HS : 2 * HS], tables, 1.0).astype(bf16)
        kv_ref[at, HS:] = project[:, 2 * HS :].astype(bf16)


def cotangent_kernel(count, *refs):
    g_refs, (w_ref, g_ref, out_ref) = refs[:count], refs[count:]
    rows = g_refs[0].shape[0]
    for i in range(count):
        g_ref[i * rows : (i + 1) * rows, :] = g_refs[i][...]

    def step(at):
        out_ref[at, :] = mm(g_ref[at, :], w_ref[...]).astype(bf16)

    tiles(g_ref.shape[0], step)


def forward_kernel(mlp_ref, w_ref, b_ref, act_ref, slope_ref):
    def step(at):
        value = mm(mlp_ref[at, :], w_ref[...]) + b_ref[...]
        cdf = 0.5 * (1.0 + lax.erf(value * 0.7071067811865476))
        density = jnp.exp(-0.5 * value * value) * 0.3989422804014327
        act_ref[at, :] = (value * cdf).astype(bf16)
        slope_ref[at, :] = cdf + value * density

    tiles(mlp_ref.shape[0], step)


def forward(mlp_in, w_up, b_up):
    count, ffl = mlp_in.shape[0], w_up.shape[1]
    columns = pl.BlockSpec((count, TILE), lambda i: (0, i))
    return call(
        forward_kernel,
        [((count, ffl), bf16), ((count, ffl), f32)],
        mlp_in, w_up, b_up,
        grid=(ffl // TILE,),
        in_specs=[
            pl.BlockSpec((count, D), lambda i: (0, 0)),
            pl.BlockSpec((D, TILE), lambda i: (0, i)),
            pl.BlockSpec((1, TILE), lambda i: (0, i)),
        ],
        out_specs=[columns, columns],
    )


def backward_kernel(g_ref, w_ref, slope_ref, out_ref, sum_ref):
    grad = (mm(g_ref[...], w_ref[...]) * slope_ref[...]).astype(bf16)
    out_ref[...] = grad
    sum_ref[...] = jnp.sum(grad.astype(f32), axis=0, keepdims=True)


def backward(g_all, w_down, slope):
    count, ffl = slope.shape
    columns = pl.BlockSpec((count, TILE), lambda i: (0, i))
    return call(
        backward_kernel,
        [((count, ffl), bf16), ((1, ffl), f32)],
        g_all, w_down, slope,
        grid=(ffl // TILE,),
        in_specs=[
            pl.BlockSpec((count, D), lambda i: (0, 0)),
            pl.BlockSpec((D, TILE), lambda i: (0, i)),
            columns,
        ],
        out_specs=[columns, pl.BlockSpec((1, TILE), lambda i: (0, i))],
    )


def weight_kernel(*refs):
    pairs, out_ref = refs[:-1], refs[-1]
    start = 0
    for lhs_ref, rhs_ref in zip(pairs[::2], pairs[1::2]):
        cols = slice(start, start + rhs_ref.shape[1])
        start += rhs_ref.shape[1]
        out_ref[:, cols] = mm(lhs_ref[...].T, rhs_ref[...]).astype(bf16)


def weight_terms(*pairs):
    count = pairs[0].shape[0]
    cols = sum(rhs.shape[1] for rhs in pairs[1::2])
    specs = []
    for rhs in pairs[1::2]:
        specs.append(pl.BlockSpec((count, 2 * TILE), lambda i: (0, i)))
        specs.append(pl.BlockSpec(rhs.shape, lambda i: (0, 0)))
    return call(
        weight_kernel,
        [((D, cols), bf16)],
        *pairs,
        grid=(D // (2 * TILE),),
        in_specs=specs,
        out_specs=[pl.BlockSpec((2 * TILE, cols), lambda i: (i, 0))],
    )[0]


def weight_half_kernel(per, place_ref, lhs_ref, rhs_ref, *out_refs):
    term = mm(lhs_ref[...].T, rhs_ref[...]).astype(bf16)
    for d, out_ref in enumerate(out_refs):

        @pl.when(pl.program_id(0) // per == d)
        def _(out_ref=out_ref):
            out_ref[...] = term


def weight_half(lhs, rhs, other):
    bh = lax.axis_size("bh")
    part = D // (2 * bh)
    tile = min(2 * TILE, part)
    per = part // tile
    place = jnp.stack([lax.axis_index("dp") ^ other, lax.axis_index("bh")]).astype(jnp.int32)
    count, cols = rhs.shape

    def lhs_at(i, place_ref):
        return (0, (place_ref[0] * bh + (place_ref[1] ^ (i // per))) * per + i % per)

    def out_at(d):
        return lambda i, place_ref: (jnp.clip(i - d * per, 0, per - 1), 0)

    return pl.pallas_call(
        functools.partial(weight_half_kernel, per),
        grid_spec=pltpu.PrefetchScalarGridSpec(
            num_scalar_prefetch=1,
            grid=(bh * per,),
            in_specs=[
                pl.BlockSpec((count, tile), lhs_at),
                pl.BlockSpec((count, cols), lambda i, place_ref: (0, 0)),
            ],
            out_specs=[pl.BlockSpec((tile, cols), out_at(d)) for d in range(bh)],
        ),
        out_shape=[jax.ShapeDtypeStruct((part, cols), bf16)] * bh,
        compiler_params=pltpu.CompilerParams(vmem_limit_bytes=58 * 2**20),
        cost_estimate=pl.CostEstimate(flops=1, bytes_accessed=1, transcendentals=0),
    )(place, lhs, rhs)


def output_kernel(att_ref, act_ref, dense_ref, down_ref, *out_refs):
    term = mm_nt(att_ref[...], dense_ref[...]) + mm_nt(act_ref[...], down_ref[...])
    rows = out_refs[0].shape[0]
    for i, out_ref in enumerate(out_refs):
        out_ref[...] = term[i * rows : (i + 1) * rows].astype(out_ref.dtype)


def output_terms(attended, activated, w_heads, w_down, part, count, rows, dtype):
    ffl, wide = activated.shape[1], 4 * TILE if count * rows <= 512 else 2 * TILE
    return call(
        output_kernel,
        [((rows, D), dtype)] * count,
        attended, activated, w_heads, w_down,
        grid=(D // wide,),
        in_specs=[
            pl.BlockSpec((count * rows, HS), lambda i: (part, 0)),
            pl.BlockSpec((count * rows, ffl), lambda i: (part, 0)),
            pl.BlockSpec((wide, HS), lambda i: (i, 3)),
            pl.BlockSpec((wide, ffl), lambda i: (i, 0)),
        ],
        out_specs=[pl.BlockSpec((rows, wide), lambda i: (0, i))] * count,
    )


def turn_back_kernel(count, *refs):
    dq_ref, refs = refs[0], refs[1:]
    term_refs, (own_ref, above_ref, below_ref, out_ref, sum_ref) = refs[:count], refs[count:]
    sum_ref[...] = jnp.zeros_like(sum_ref)

    def step(at):
        tables = own_ref[at, :], above_ref[at, :], below_ref[at, :]
        grad = term_refs[0][at, :].astype(f32)
        for ref in term_refs[1:]:
            grad += ref[at, :].astype(f32)
        grad = grad.astype(bf16)
        out_ref[at, :HS] = turn(dq_ref[at, :].astype(f32), tables, -1.0).astype(bf16)
        out_ref[at, HS : 2 * HS] = turn(grad[:, :HS].astype(f32), tables, -1.0).astype(bf16)
        out_ref[at, 2 * HS :] = grad[:, HS:]
        sum_ref[...] += jnp.sum(out_ref[at, :].astype(f32), axis=0, keepdims=True)

    tiles(dq_ref.shape[0], step)


def input_kernel(count, *refs):
    x_refs, refs = refs[:count], refs[count:]
    average_ref, inverse_ref, gp_ref, gu_ref, heads_ref, up_ref, vec_ref = refs[:7]
    out_refs, sum_ref = refs[7:-1], refs[-1]
    rows = x_refs[0].shape[0]
    sums = [0.0] * 4
    for start in range(0, count * rows, TILE):
        at = slice(start, start + TILE)
        attn = mm_nt(gp_ref[at, :], heads_ref[...])
        mlp = mm_nt(gu_ref[at, :], up_ref[...])
        block = jnp.concatenate(
            [x_refs[i][...].astype(f32) for i in range(start // rows, (start + TILE) // rows)],
            axis=0,
        )
        normed = (block - average_ref[at, :]) * inverse_ref[at, :]
        for i, term in enumerate((attn * normed, attn, mlp * normed, mlp)):
            sums[i] = sums[i] + jnp.sum(term, axis=0, keepdims=True)
        out = attn * vec_ref[0:1, :] + mlp * vec_ref[2:3, :]
        for i in range(0, TILE, rows):
            out_ref = out_refs[(start + i) // rows]
            out_ref[...] = out[i : i + rows].astype(out_ref.dtype)
    sum_ref[...] = jnp.concatenate(sums, axis=0)


def input_terms(x_blocks, average, inverse, grad_project, grad_pre_up, w_heads, w_up, vectors, own):
    count, ffl = grad_pre_up.shape
    whole = lambda rows, cols: pl.BlockSpec((rows, cols), lambda i: (0, 0))
    block = pl.BlockSpec((x_blocks[0].shape[0], TILE), lambda i: (0, i))
    *terms, sums = call(
        functools.partial(input_kernel, len(x_blocks)),
        [(x.shape, f32 if i < own else bf16) for i, x in enumerate(x_blocks)] + [((4, D), f32)],
        *x_blocks, average, inverse, grad_project, grad_pre_up, w_heads, w_up, vectors,
        grid=(D // TILE,),
        in_specs=[
            *[block] * len(x_blocks),
            whole(count, 1),
            whole(count, 1),
            whole(count, 3 * HS),
            whole(count, ffl),
            pl.BlockSpec((TILE, 3 * HS), lambda i: (i, 0)),
            pl.BlockSpec((TILE, ffl), lambda i: (i, 0)),
            pl.BlockSpec((vectors.shape[0], TILE), lambda i: (0, i)),
        ],
        out_specs=[*[block] * len(x_blocks), pl.BlockSpec((4, TILE), lambda i: (0, i))],
    )
    return terms, sums


def places(block, start, shape, dim, sizes, t):
    rows, tp = sizes
    index = start + lax.broadcasted_iota(jnp.int32, shape, dim)
    device = index // rows
    block = block ^ (device // tp)
    return (block * tp + (t ^ (device % tp))) * rows + index % rows


def attention_kernel(count, sizes, place_ref, q_ref, g_ref, *refs):
    kv_refs, (o_ref, dq_ref), refs = refs[:count], refs[count : count + 2], refs[count + 2 :]
    dkv_refs, sum_ref = refs[:-1], refs[-1]
    t, block, tile = place_ref[0], place_ref[1], 2 * TILE
    keys = jnp.concatenate([ref[:, :HS] for ref in kv_refs], axis=0)
    values = jnp.concatenate([ref[:, HS:] for ref in kv_refs], axis=0)
    keys_turned = keys.T
    values_turned = values.T
    key_places = places(block, 0, (keys.shape[0], 1), 0, sizes, t)
    sum_ref[...] = jnp.zeros_like(sum_ref)
    for start in range(0, q_ref.shape[0], tile):
        at = slice(start, start + tile)
        query = q_ref[at, :]
        grad = g_ref[at, :]
        visible = key_places <= places(block, start, (1, tile), 1, sizes, t)
        scores = jnp.where(visible, mm_nt(keys, query), -1e30)
        weights = jnp.exp(scores - jnp.max(scores, axis=0, keepdims=True))
        weights = weights * (1.0 / jnp.sum(weights, axis=0, keepdims=True))
        weights_low = weights.astype(bf16)
        result = mm(values_turned, weights_low)
        o_ref[at, :] = result.T.astype(bf16)
        sum_ref[:, HS:] += mm(weights_low, grad)
        delta = jnp.sum(result * grad.T.astype(f32), axis=0, keepdims=True)
        score_grad = (weights * (mm_nt(values, grad) - delta)).astype(bf16)
        dq_ref[at, :] = (mm(keys_turned, score_grad).T * (HS**-0.5)).astype(bf16)
        sum_ref[:, :HS] += mm(score_grad, query)
    start = 0
    for ref in dkv_refs:
        ref[...] = sum_ref[start : start + ref.shape[0], :].astype(bf16)
        start += ref.shape[0]


def long_attention_kernel(sizes, place_ref, q_ref, g_ref, kv_ref, o_ref, dq_ref, dkv_ref, sum_ref):
    blocks = kv_ref.shape[0] // KEYS
    t, block = place_ref[0], place_ref[1]
    sum_ref[...] = jnp.zeros_like(sum_ref)

    def step(at):
        query = q_ref[at, :]
        grad = g_ref[at, :]
        query_places = places(block, at.start, (1, TILE), 1, sizes, t)

        def scores_of(j):
            here = pl.ds(pl.multiple_of(j * KEYS, KEYS), KEYS)
            visible = places(block, j * KEYS, (KEYS, 1), 0, sizes, t) <= query_places
            return here, jnp.where(visible, mm_nt(kv_ref[here, :HS], query), -1e30)

        def first(j, state):
            top, total = state
            _, scores = scores_of(j)
            higher = jnp.maximum(top, jnp.max(scores, axis=0, keepdims=True))
            now = jnp.sum(jnp.exp(scores - higher), axis=0, keepdims=True)
            return higher, total * jnp.exp(top - higher) + now

        row = (1, TILE)
        top, total = lax.fori_loop(
            0, blocks, first, (jnp.full(row, -1e30, f32), jnp.zeros(row, f32))
        )
        inverse = 1.0 / total

        def second(j, result):
            here, scores = scores_of(j)
            weights = jnp.exp(scores - top) * inverse
            return result + mm(kv_ref[here, HS:].T, weights.astype(bf16))

        result = lax.fori_loop(0, blocks, second, jnp.zeros((HS, TILE), f32))
        o_ref[at, :] = result.T.astype(bf16)
        delta = jnp.sum(result * grad.T.astype(f32), axis=0, keepdims=True)

        def third(j, result):
            here, scores = scores_of(j)
            weights = jnp.exp(scores - top) * inverse
            weight_grad = mm_nt(kv_ref[here, HS:], grad)
            score_grad = (weights * (weight_grad - delta)).astype(bf16)
            sum_ref[here, HS:] += mm(weights.astype(bf16), grad)
            sum_ref[here, :HS] += mm(score_grad, query)
            return result + mm(kv_ref[here, :HS].T, score_grad)

        result = lax.fori_loop(0, blocks, third, jnp.zeros((HS, TILE), f32))
        dq_ref[at, :] = (result.T * (HS**-0.5)).astype(bf16)

    tiles(q_ref.shape[0], step)
    dkv_ref[...] = sum_ref[...].astype(bf16)


def attention(query, grad, kv_blocks, sizes):
    place = jnp.stack([lax.axis_index(TP), lax.axis_index("bh")]).astype(jnp.int32)
    count, total = len(kv_blocks), sum(block.shape[0] for block in kv_blocks)
    low = (query.shape, bf16)
    scratch = [pltpu.VMEM((total, 2 * HS), f32)]
    vmem = pl.BlockSpec(memory_space=pltpu.VMEM)
    smem = pl.BlockSpec(memory_space=pltpu.SMEM)
    if total <= KEYS:
        attended, grad_query, *grad_kv = call(
            functools.partial(attention_kernel, count, sizes),
            [low, low] + [(block.shape, bf16) for block in kv_blocks],
            place, query, grad, *kv_blocks,
            scratch=scratch,
            in_specs=[smem] + [vmem] * (2 + count),
        )
        return attended, grad_query, grad_kv
    kv_all = jnp.concatenate(kv_blocks, axis=0)
    attended, grad_query, grad_kv = call(
        functools.partial(long_attention_kernel, sizes),
        [low, low, (kv_all.shape, bf16)],
        place, query, grad, kv_all,
        scratch=scratch,
        in_specs=[smem] + [vmem] * 3,
    )
    return attended, grad_query, jnp.split(grad_kv, count, axis=0)


def per_device(
    hidden_in,
    gain_attn,
    shift_attn,
    gain_mlp,
    shift_mlp,
    qkv_weight,
    qkv_bias,
    dense_weight,
    up_weight,
    up_bias,
    down_weight,
    out_bias,
    cotangent,
):
    seq_count, sub_len, _ = hidden_in.shape
    tp, rp = lax.axis_size(TP), lax.axis_size(RP)
    n_dev = lax.axis_size(ALL)
    t = lax.axis_index(TP)
    bh, bh_size, bl_size = lax.axis_index("bh"), lax.axis_size("bh"), lax.axis_size("bl")
    rows = qkv_weight.shape[0]
    ff = up_weight.shape[1]
    ffl = ff // tp
    group_len = sub_len * tp

    vmem = pl.BlockSpec(memory_space=pltpu.VMEM)
    x_own = hidden_in.reshape(sub_len, D)
    join = Order(out_bias).join
    g_own = cotangent.reshape(sub_len, D)
    smalls = jnp.concatenate(
        [
            vector.reshape(-1, rows)
            for vector in (
                gain_attn, shift_attn, gain_mlp, shift_mlp, out_bias, qkv_bias, up_bias
            )
        ],
        axis=0,
    )
    kinds = smalls.shape[0]
    count = kinds * rows
    smalls = jnp.pad(smalls.reshape(1, count), ((0, 7), (0, 4 * HS - count)))
    heads_own = jnp.concatenate(
        [
            qkv_weight.reshape(rows, 3, HEADS, HS).transpose(2, 0, 1, 3).reshape(HEADS, rows, 3 * HS),
            dense_weight.reshape(rows, HEADS, HS).transpose(1, 0, 2),
        ],
        axis=2,
    )
    heads_own = jnp.concatenate(
        [heads_own, jnp.broadcast_to(smalls[None], (tp,) + smalls.shape)], axis=1
    )
    up_own = up_weight.reshape(rows, tp, ffl).transpose(1, 0, 2)
    down_own = down_weight.reshape(rows, tp, ffl).transpose(1, 0, 2)

    x_near = gather_start(x_own)
    x_side = gather_axis(x_own, "bl")
    g_side = gather_axis(g_own, "bl")
    x_near, x_side, g_side, heads_own = join(x_near, x_side, g_side, heads_own)
    m_heads = lax.all_to_all(heads_own, TP, split_axis=0, concat_axis=0, tiled=True)
    x_rows = [x_side] + [gather_axis(block, "bl") for block in x_near[:2]]
    x_near = gather_end(x_own, x_near)
    row = jnp.arange(group_len, dtype=jnp.int32)
    inside = ((row // sub_len) ^ t) * sub_len + row % sub_len
    query_places = bh * group_len + inside
    tables = rotary_tables(query_places.astype(f32))
    x_near, x_rows, m_heads, up_own, g_late, tables = join(
        x_near, x_rows, m_heads, up_own, g_own, tables
    )
    w_heads = spread_rest(m_heads[:, :rows].reshape(tp * rows, -1))
    x_rows += [gather_axis(block, "bl") for block in x_near[3:]]
    g_first = swap(g_late, "hd", 1)
    m_up = spread_group(up_own)
    smalls = gather_rest(m_heads[:, rows, :count]).reshape(n_dev, kinds, rows).astype(f32)
    vectors = smalls[:, :5].transpose(1, 0, 2).reshape(5, D)
    nq = qkv_bias.shape[0] // rows
    b_qkv = smalls[:, 5 : 5 + nq].reshape(3, HEADS, HS)
    b_up = smalls[:, 5 + nq :].reshape(tp, ffl)
    b_qkv = lax.dynamic_index_in_dim(b_qkv, t, 1, keepdims=False).reshape(1, 3 * HS)
    b_up = lax.dynamic_index_in_dim(b_up, t, 0, keepdims=True)

    x_rows, g_first, m_up, g_late, down_own, vectors, b_qkv, b_up = join(
        x_rows, g_first, m_up, g_late, down_own, vectors, b_qkv, b_up
    )
    w_up = spread_rest(m_up)
    x_blocks = [row[far] for far in range(bl_size) for row in x_rows]
    g_rows = [g_side, gather_axis(g_first, "bl")]
    hd_size = lax.axis_size("hd")
    four = hd_size == 4
    g_near = [g_first] + [swap(g_late, "hd", d) for d in range(2, 3 if hd_size == 4 else hd_size)]
    attn_in, mlp_in, query, kv, average, inverse = call(
        functools.partial(project_kernel, tp),
        [
            ((group_len, D), bf16),
            ((group_len, D), bf16),
            ((group_len, HS), bf16),
            ((group_len, 2 * HS), bf16),
            ((group_len, 1), f32),
            ((group_len, 1), f32),
        ],
        *x_blocks, vectors, w_heads, b_qkv, *tables,
        grid=(1,),
        in_specs=[vmem] * (tp + 1) + [pl.BlockSpec((D, 3 * HS), lambda i: (0, 0))] + [vmem] * 4,
    )
    g_rows, g_near, kv, mlp_in, g_late, down_own = join(
        g_rows, g_near, kv, mlp_in, g_late, down_own
    )
    g_near = gather_end(g_late, g_near)
    g_rows += [gather_axis(block, "bl") for block in g_near[2:3]]
    g_rows, g_near, kv, down_own, mlp_in = join(g_rows, g_near, kv, down_own, mlp_in)
    g_rows += [gather_axis(block, "bl") for block in g_near[3:]]
    kv_blocks = gather_axis(kv, "bh")
    m_down = spread_group(down_own)
    activated, slope = forward(mlp_in, w_up, b_up)
    g_rows, kv_blocks, m_down, activated, slope = join(g_rows, kv_blocks, m_down, activated, slope)
    w_down = spread_rest(m_down)
    g_blocks = [row[far] for far in range(bl_size) for row in g_rows]
    g_all, grad_att = call(
        functools.partial(cotangent_kernel, tp),
        [((group_len, D), bf16), ((group_len, HS), bf16)],
        *g_blocks, w_heads,
        grid=(1,),
        in_specs=[vmem] * tp + [pl.BlockSpec((D, HS), lambda i: (0, 3))],
    )
    down_far = weight_half(g_all, activated, 1)
    down_far, grad_att, g_all = join(down_far, grad_att, g_all)
    down_far = [swap(terms, "dp", 1) for terms in reversed(down_far)][::-1]
    down_own = weight_half(g_all, activated, 0)
    down_far, down_own, grad_att = join(down_far, down_own, grad_att)
    down_sent = add(*[([down_far[d], down_own[d]], bf16, 1) for d in range(1, bh_size)])
    down_sent, grad_att = join(down_sent, grad_att)
    down_others = [swap(sent[0], "bh", d + 1) for d, sent in enumerate(down_sent)]
    attended, grad_query, grad_kv = attention(query, grad_att, kv_blocks, (sub_len, tp))
    hd_terms = (hd_size, sub_len)
    out_far = [
        output_terms(attended, activated, w_heads, w_down, far, *hd_terms, bf16)
        for far in range(1, bl_size)
    ]
    out_own = output_terms(attended, activated, w_heads, w_down, 0, *hd_terms, f32)
    down_others, out_far, attended, grad_kv, slope, out_own = join(
        down_others, out_far, attended, grad_kv, slope, out_own
    )
    part = hd_size // 4
    parts = [range(hd_size - (g + 1) * part, hd_size - g * part) for g in range(4)]

    def over_bl(terms, ds):
        return {d: [swap(term[d], "bl", f + 1) for f, term in enumerate(terms)] for d in ds}

    def sums_of(own, received, ds, handed=()):
        return [
            ([own[d], *received[d], *(handed if d == 2 else ())], f32 if d == 0 else bf16, 1)
            for d in ds
        ]

    ((down_last,),) = add(([down_far[0], down_own[0], *down_others], bf16, 1))
    down_last, attended, slope = join(down_last, attended, slope)
    kv_others = [swap(grad_kv[d], "bh", d) for d in range(1, bh_size)]
    down_grad = collect_group(down_last)
    received = over_bl(out_far, parts[0])
    grad_pre_up, up_bias_term = backward(g_all, w_down, slope)
    up_terms = weight_terms(mlp_in, grad_pre_up)
    kv_others, down_grad, received, grad_pre_up, out_far, up_terms = join(
        kv_others, down_grad, received, grad_pre_up, out_far, up_terms
    )
    up_mine = collect_rest(up_terms)
    out = dict(zip(parts[0], add(*sums_of(out_own, received, parts[0]))))
    out, kv_others = join(out, kv_others)
    out_near = {d: hand_on(out[d][0], d) for d in parts[0]}
    middle = [*parts[1], *parts[2]]
    received = over_bl(out_far, middle)
    grad_project, qkv_bias_term = call(
        functools.partial(turn_back_kernel, bh_size),
        [((group_len, 3 * HS), bf16), ((1, 3 * HS), f32)],
        grad_query, grad_kv[0], *kv_others, *tables,
    )
    in_terms, sums = input_terms(
        x_blocks, average, inverse, grad_project, grad_pre_up, w_heads, w_up, vectors, hd_size
    )
    in_own = in_terms[:hd_size]
    in_far = [in_terms[f * hd_size : (f + 1) * hd_size] for f in range(1, bl_size)]
    out_near, received, out_far, in_far, grad_project = join(
        out_near, received, out_far, in_far, grad_project
    )
    out = add(*sums_of(out_own, received, middle, [out_near[3]] if four else []))
    out, in_far, grad_project = join(out, in_far, grad_project)
    out_near |= {d: hand_on(term, d) for d, (term,) in zip(middle, out)}
    received = over_bl(out_far, parts[3])
    received_in = over_bl(in_far, parts[0])
    heads_terms = weight_terms(attn_in, grad_project, g_all, attended)
    out_near, received, received_in, heads_terms, up_mine, in_far = join(
        out_near, received, received_in, heads_terms, up_mine, in_far
    )
    heads_mine = collect_rest(heads_terms)
    ins = add(*sums_of(in_own, received_in, parts[0]))
    ins, up_mine, in_far = join(ins, up_mine, in_far)
    up_grad = collect_group(up_mine)
    in_near = {d: hand_on(term, d) for d, (term,) in zip(parts[0], ins)}
    received_in = over_bl(in_far, middle)
    sums = jnp.concatenate([sums, jnp.sum(g_own.astype(f32), axis=0, keepdims=True)], axis=0)
    qkv_bias_full = lax.dynamic_update_slice(
        jnp.zeros((3, HEADS, HS), f32), qkv_bias_term.reshape(3, 1, HS), (0, t, 0)
    )
    up_bias_full = lax.dynamic_update_slice(jnp.zeros((tp, ffl), f32), up_bias_term, (t, 0))
    small_terms = jnp.concatenate(
        [
            sums.reshape(5, n_dev, rows).transpose(1, 0, 2),
            qkv_bias_full.reshape(n_dev, nq, rows),
            up_bias_full.reshape(n_dev, -1, rows),
        ],
        axis=1,
    )
    up_grad, in_near, received_in, small_terms, in_far = join(
        up_grad, in_near, received_in, small_terms, in_far
    )
    ins = add(*sums_of(in_own, received_in, middle, [in_near[3]] if four else []))
    ins, in_far, heads_mine, small_terms = join(ins, in_far, heads_mine, small_terms)
    heads_grad = collect_group(heads_mine)
    received_in = over_bl(in_far, parts[3])
    down_grad = down_grad.astype(f32).transpose(1, 0, 2).reshape(rows, ff)
    up_grad = up_grad.astype(f32).transpose(1, 0, 2).reshape(rows, ff)
    heads_grad, received_in, down_grad, up_grad, ins, small_terms = join(
        heads_grad, received_in, down_grad, up_grad, ins, small_terms
    )
    in_near |= {d: hand_on(term, d) for d, (term,) in zip(middle, ins)}
    small = lax.all_to_all(small_terms, ALL, split_axis=0, concat_axis=0, tiled=True)
    heads_grad = heads_grad.astype(f32)
    dense_grad = heads_grad[:, :, 3 * HS :].transpose(1, 0, 2).reshape(rows, D)
    qkv_grad = (
        heads_grad[:, :, : 3 * HS]
        .reshape(tp, rows, 3, HS)
        .transpose(1, 2, 0, 3)
        .reshape(rows, 3 * D)
    )

    def total(own, received, near):
        rest = {d: sum((x.astype(f32) for x in received[d]), own[d]) for d in received}
        near = near | {d: hand_on(rest[d].astype(bf16), d) for d in rest if d}
        straight = [d for d in range(1, hd_size) if not (four and d == 3)]
        return sum((near[d].astype(f32) for d in straight), rest[0])

    projected = total(out_own, received, out_near)
    output = (x_own.astype(f32) + projected + vectors[4:5]).astype(bf16)
    in_near, received_in, small, dense_grad, qkv_grad, output, in_own = join(
        in_near, received_in, small, dense_grad, qkv_grad, output, in_own
    )
    small = jnp.sum(small, axis=0)
    grad_normed = total(in_own, received_in, in_near)
    own = x_own.astype(f32)
    own_average, own_inverse = statistics(own)
    own_normed = (own - own_average) * own_inverse
    grad_hidden = g_own.astype(f32) + own_inverse * (
        grad_normed
        - jnp.mean(grad_normed, axis=1, keepdims=True)
        - own_normed * jnp.mean(grad_normed * own_normed, axis=1, keepdims=True)
    )
    return (
        output.reshape(seq_count, sub_len, D),
        grad_hidden.reshape(seq_count, sub_len, D),
        small[0],
        small[1],
        small[2],
        small[3],
        qkv_grad,
        small[5 : 5 + nq].reshape(-1),
        dense_grad,
        up_grad,
        small[5 + nq :].reshape(-1),
        down_grad,
        small[4],
    )


def solution(mesh):
    dp, blk, hd = (mesh.shape[name] for name in ("dp", "blk", "hd"))
    low = HEADS // hd
    inner = Mesh(mesh.devices.reshape(dp, blk // low, low, hd), ALL)
    token = P("dp", ("bh", "bl", "hd"), None)
    vector = P(ALL)
    matrix = P(ALL, None)
    return jax.shard_map(
        per_device,
        mesh=inner,
        in_specs=(
            token, vector, vector, vector, vector, matrix, vector,
            matrix, matrix, vector, matrix, vector, token,
        ),
        out_specs=(
            token, token, vector, vector, vector, vector, matrix, vector,
            matrix, matrix, vector, matrix, vector,
        ),
        check_vma=False,
    )
```

```python
import functools

import jax
import jax.numpy as jnp
from jax import lax
from jax.experimental import pallas as pl
from jax.experimental.pallas import tpu as pltpu
from jax.sharding import Mesh, PartitionSpec as P

D = 2048
HEADS = 8
HS = 256
ROT = 64

TP = ("bl", "hd")
RP = ("dp", "bh")
ALL = ("dp", "bh", "bl", "hd")

epsilon = 1e-05
contract_last = (((1,), (1,)), ((), ()))
f32 = jnp.float32
bf16 = jnp.bfloat16


def rotary_tables(positions):
    half_rot = ROT // 2
    frequency = 10000.0 ** (-(2.0 * jnp.arange(half_rot, dtype=f32)) / ROT)
    angles = positions[:, None] * frequency[None, :]
    cosine, sine = jnp.cos(angles), jnp.sin(angles)
    none = jnp.zeros_like(sine)
    rest = jnp.ones((positions.shape[0], 128 - ROT), f32)
    return (
        jnp.concatenate([cosine, cosine, rest], axis=1),
        jnp.concatenate([-sine, none, 0.0 * rest], axis=1),
        jnp.concatenate([none, sine, 0.0 * rest], axis=1),
    )


def mm(a, b):
    return jnp.dot(a, b, preferred_element_type=f32)


def mm_nt(a, b):
    return lax.dot_general(a, b, contract_last, preferred_element_type=f32)


class Order:
    def __init__(self, token):
        self.token = token

    def join(self, *values):
        self.token, values = lax.optimization_barrier((self.token, values))
        return values


def swap(value, axis, distance):
    size = lax.axis_size(axis)
    return lax.ppermute(value, axis, [(i, i ^ distance) for i in range(size)])


def gather_axis(value, axis):
    return [value] + [swap(value, axis, d) for d in range(1, lax.axis_size(axis))]


def gather_start(value):
    size = lax.axis_size("hd")
    return [swap(value, "hd", d) for d in range(1, 3 if size == 4 else size)]


def gather_end(value, near):
    if lax.axis_size("hd") == 4:
        near = [near[0], near[1], swap(near[1], "hd", 1)]
    return [value] + near


def gather_rest(value):
    place, size = lax.axis_index(RP), lax.axis_size(RP)
    blocks = jnp.stack([value] + [swap(value, RP, d) for d in range(1, size)])
    bit = 1
    while bit < size:
        pairs = blocks.reshape((size // (2 * bit), 2, bit) + value.shape)
        turned = jnp.stack([pairs[:, 1], pairs[:, 0]], axis=1).reshape(blocks.shape)
        blocks = jnp.where((place & bit) != 0, turned, blocks)
        bit *= 2
    return blocks


def hand_on(value, distance):
    if lax.axis_size("hd") == 4 and distance == 3:
        distance = 1
    return swap(value, "hd", distance)


def exchange(terms, axis, dim):
    place, size = lax.axis_index(axis), lax.axis_size(axis)
    pick = lambda d: lax.dynamic_index_in_dim(terms, place ^ d, dim, keepdims=False)
    return [pick(0)] + [swap(pick(d), axis, d) for d in range(1, size)]


def spread_group(shard):
    mine = lax.all_to_all(shard, TP, split_axis=0, concat_axis=0, tiled=True)
    return mine.reshape(-1, shard.shape[2])


def spread_rest(mine):
    return lax.all_gather(mine, RP, axis=0, tiled=True)


def collect_rest(terms):
    return lax.psum_scatter(terms, RP, scatter_dimension=0, tiled=True)


def collect_group(mine):
    mine = mine.reshape(lax.axis_size(TP), -1, mine.shape[1])
    return lax.all_to_all(mine, TP, split_axis=0, concat_axis=0, tiled=True)


TILE = 256
KEYS = 2048


def call(kernel, outs, *ins, scratch=(), grid=(), in_specs=None, out_specs=None):
    vmem = pl.BlockSpec(memory_space=pltpu.VMEM)
    return pl.pallas_call(
        kernel,
        grid=grid,
        out_shape=[jax.ShapeDtypeStruct(shape, dtype) for shape, dtype in outs],
        in_specs=in_specs or [vmem] * len(ins),
        out_specs=out_specs or [vmem] * len(outs),
        scratch_shapes=list(scratch),
        compiler_params=pltpu.CompilerParams(vmem_limit_bytes=58 * 2**20),
        cost_estimate=pl.CostEstimate(flops=1, bytes_accessed=1, transcendentals=0),
    )(*ins)


def tiles(count, step):
    def body(i, _):
        step(pl.ds(pl.multiple_of(i * TILE, TILE), TILE))
        return 0

    lax.fori_loop(0, count // TILE, body, 0)


def add(*groups):
    return [
        [sum((x.astype(f32) for x in arrays[1:]), arrays[0].astype(f32)).astype(dtype)]
        for arrays, dtype, _ in groups
    ]


def turn(value, tables, sign):
    own, above, below = tables
    first = value[:, :128]
    turned = first * own + sign * (
        pltpu.roll(first, 96, 1) * above + pltpu.roll(first, 32, 1) * below
    )
    return jnp.concatenate([turned, value[:, 128:]], axis=1)


def statistics(block):
    average = jnp.mean(block, axis=1, keepdims=True)
    centered = block - average
    return average, lax.rsqrt(jnp.mean(centered * centered, axis=1, keepdims=True) + epsilon)


def project_kernel(count, *refs):
    x_refs, refs = refs[:count], refs[count:]
    vec_ref, w_ref, b_ref, own_ref, above_ref, below_ref, *refs = refs
    attn_ref, mlp_ref, q_ref, kv_ref, average_ref, inverse_ref = refs
    rows = x_refs[0].shape[0]
    for start in range(0, count * rows, TILE):
        for i in range(start // rows, (start + TILE) // rows):
            at = slice(i * rows, (i + 1) * rows)
            block = x_refs[i][...].astype(f32)
            average, inverse = statistics(block)
            average_ref[at, :] = average
            inverse_ref[at, :] = inverse
            normed = (block - average) * inverse
            attn_ref[at, :] = (normed * vec_ref[0:1, :] + vec_ref[1:2, :]).astype(bf16)
            mlp_ref[at, :] = (normed * vec_ref[2:3, :] + vec_ref[3:4, :]).astype(bf16)
        at = slice(start, start + TILE)
        project = mm(attn_ref[at, :], w_ref[...]) + b_ref[...]
        tables = own_ref[at, :], above_ref[at, :], below_ref[at, :]
        query = turn(project[:, :HS], tables, 1.0).astype(bf16)
        q_ref[at, :] = (query.astype(f32) * HS**-0.5).astype(bf16)
        kv_ref[at, :HS] = turn(project[:, HS : 2 * HS], tables, 1.0).astype(bf16)
        kv_ref[at, HS:] = project[:, 2 * HS :].astype(bf16)


def cotangent_kernel(count, *refs):
    g_refs, (w_ref, g_ref, out_ref) = refs[:count], refs[count:]
    rows = g_refs[0].shape[0]
    for i in range(count):
        g_ref[i * rows : (i + 1) * rows, :] = g_refs[i][...]

    def step(at):
        out_ref[at, :] = mm(g_ref[at, :], w_ref[...]).astype(bf16)

    tiles(g_ref.shape[0], step)


def forward_kernel(mlp_ref, w_ref, b_ref, act_ref, slope_ref):
    def step(at):
        value = mm(mlp_ref[at, :], w_ref[...]) + b_ref[...]
        cdf = 0.5 * (1.0 + lax.erf(value * 0.7071067811865476))
        density = jnp.exp(-0.5 * value * value) * 0.3989422804014327
        act_ref[at, :] = (value * cdf).astype(bf16)
        slope_ref[at, :] = cdf + value * density

    tiles(mlp_ref.shape[0], step)


def forward(mlp_in, w_up, b_up):
    count, ffl = mlp_in.shape[0], w_up.shape[1]
    columns = pl.BlockSpec((count, TILE), lambda i: (0, i))
    return call(
        forward_kernel,
        [((count, ffl), bf16), ((count, ffl), f32)],
        mlp_in, w_up, b_up,
        grid=(ffl // TILE,),
        in_specs=[
            pl.BlockSpec((count, D), lambda i: (0, 0)),
            pl.BlockSpec((D, TILE), lambda i: (0, i)),
            pl.BlockSpec((1, TILE), lambda i: (0, i)),
        ],
        out_specs=[columns, columns],
    )


def backward_kernel(g_ref, w_ref, slope_ref, out_ref, sum_ref):
    grad = (mm(g_ref[...], w_ref[...]) * slope_ref[...]).astype(bf16)
    out_ref[...] = grad
    sum_ref[...] = jnp.sum(grad.astype(f32), axis=0, keepdims=True)


def backward(g_all, w_down, slope):
    count, ffl = slope.shape
    columns = pl.BlockSpec((count, TILE), lambda i: (0, i))
    return call(
        backward_kernel,
        [((count, ffl), bf16), ((1, ffl), f32)],
        g_all, w_down, slope,
        grid=(ffl // TILE,),
        in_specs=[
            pl.BlockSpec((count, D), lambda i: (0, 0)),
            pl.BlockSpec((D, TILE), lambda i: (0, i)),
            columns,
        ],
        out_specs=[columns, pl.BlockSpec((1, TILE), lambda i: (0, i))],
    )


def weight_kernel(*refs):
    pairs, out_ref = refs[:-1], refs[-1]
    start = 0
    for lhs_ref, rhs_ref in zip(pairs[::2], pairs[1::2]):
        cols = slice(start, start + rhs_ref.shape[1])
        start += rhs_ref.shape[1]
        out_ref[:, cols] = mm(lhs_ref[...].T, rhs_ref[...]).astype(bf16)


def weight_terms(*pairs):
    count = pairs[0].shape[0]
    cols = sum(rhs.shape[1] for rhs in pairs[1::2])
    specs = []
    for rhs in pairs[1::2]:
        specs.append(pl.BlockSpec((count, 2 * TILE), lambda i: (0, i)))
        specs.append(pl.BlockSpec(rhs.shape, lambda i: (0, 0)))
    return call(
        weight_kernel,
        [((D, cols), bf16)],
        *pairs,
        grid=(D // (2 * TILE),),
        in_specs=specs,
        out_specs=[pl.BlockSpec((2 * TILE, cols), lambda i: (i, 0))],
    )[0]


def weight_half_kernel(per, place_ref, lhs_ref, rhs_ref, *out_refs):
    term = mm(lhs_ref[...].T, rhs_ref[...]).astype(bf16)
    for d, out_ref in enumerate(out_refs):

        @pl.when(pl.program_id(0) // per == d)
        def _(out_ref=out_ref):
            out_ref[...] = term


def weight_half(lhs, rhs, other):
    bh = lax.axis_size("bh")
    part = D // (2 * bh)
    tile = min(2 * TILE, part)
    per = part // tile
    place = jnp.stack([lax.axis_index("dp") ^ other, lax.axis_index("bh")]).astype(jnp.int32)
    count, cols = rhs.shape

    def lhs_at(i, place_ref):
        return (0, (place_ref[0] * bh + (place_ref[1] ^ (i // per))) * per + i % per)

    def out_at(d):
        return lambda i, place_ref: (jnp.clip(i - d * per, 0, per - 1), 0)

    return pl.pallas_call(
        functools.partial(weight_half_kernel, per),
        grid_spec=pltpu.PrefetchScalarGridSpec(
            num_scalar_prefetch=1,
            grid=(bh * per,),
            in_specs=[
                pl.BlockSpec((count, tile), lhs_at),
                pl.BlockSpec((count, cols), lambda i, place_ref: (0, 0)),
            ],
            out_specs=[pl.BlockSpec((tile, cols), out_at(d)) for d in range(bh)],
        ),
        out_shape=[jax.ShapeDtypeStruct((part, cols), bf16)] * bh,
        compiler_params=pltpu.CompilerParams(vmem_limit_bytes=58 * 2**20),
        cost_estimate=pl.CostEstimate(flops=1, bytes_accessed=1, transcendentals=0),
    )(place, lhs, rhs)


def output_kernel(att_ref, act_ref, dense_ref, down_ref, *out_refs):
    term = mm_nt(att_ref[...], dense_ref[...]) + mm_nt(act_ref[...], down_ref[...])
    rows = out_refs[0].shape[0]
    for i, out_ref in enumerate(out_refs):
        out_ref[...] = term[i * rows : (i + 1) * rows].astype(out_ref.dtype)


def output_terms(attended, activated, w_heads, w_down, part, count, rows, dtype):
    ffl, wide = activated.shape[1], 4 * TILE if count * rows <= 512 else 2 * TILE
    return call(
        output_kernel,
        [((rows, D), dtype)] * count,
        attended, activated, w_heads, w_down,
        grid=(D // wide,),
        in_specs=[
            pl.BlockSpec((count * rows, HS), lambda i: (part, 0)),
            pl.BlockSpec((count * rows, ffl), lambda i: (part, 0)),
            pl.BlockSpec((wide, HS), lambda i: (i, 3)),
            pl.BlockSpec((wide, ffl), lambda i: (i, 0)),
        ],
        out_specs=[pl.BlockSpec((rows, wide), lambda i: (0, i))] * count,
    )


def turn_back_kernel(count, *refs):
    dq_ref, refs = refs[0], refs[1:]
    term_refs, (own_ref, above_ref, below_ref, out_ref, sum_ref) = refs[:count], refs[count:]
    sum_ref[...] = jnp.zeros_like(sum_ref)

    def step(at):
        tables = own_ref[at, :], above_ref[at, :], below_ref[at, :]
        grad = term_refs[0][at, :].astype(f32)
        for ref in term_refs[1:]:
            grad += ref[at, :].astype(f32)
        grad = grad.astype(bf16)
        out_ref[at, :HS] = turn(dq_ref[at, :].astype(f32), tables, -1.0).astype(bf16)
        out_ref[at, HS : 2 * HS] = turn(grad[:, :HS].astype(f32), tables, -1.0).astype(bf16)
        out_ref[at, 2 * HS :] = grad[:, HS:]
        sum_ref[...] += jnp.sum(out_ref[at, :].astype(f32), axis=0, keepdims=True)

    tiles(dq_ref.shape[0], step)


def input_kernel(count, *refs):
    x_refs, refs = refs[:count], refs[count:]
    average_ref, inverse_ref, gp_ref, gu_ref, heads_ref, up_ref, vec_ref = refs[:7]
    out_refs, sum_ref = refs[7:-1], refs[-1]
    rows = x_refs[0].shape[0]
    sums = [0.0] * 4
    for start in range(0, count * rows, TILE):
        at = slice(start, start + TILE)
        attn = mm_nt(gp_ref[at, :], heads_ref[...])
        mlp = mm_nt(gu_ref[at, :], up_ref[...])
        block = jnp.concatenate(
            [x_refs[i][...].astype(f32) for i in range(start // rows, (start + TILE) // rows)],
            axis=0,
        )
        normed = (block - average_ref[at, :]) * inverse_ref[at, :]
        for i, term in enumerate((attn * normed, attn, mlp * normed, mlp)):
            sums[i] = sums[i] + jnp.sum(term, axis=0, keepdims=True)
        out = attn * vec_ref[0:1, :] + mlp * vec_ref[2:3, :]
        for i in range(0, TILE, rows):
            out_ref = out_refs[(start + i) // rows]
            out_ref[...] = out[i : i + rows].astype(out_ref.dtype)
    sum_ref[...] = jnp.concatenate(sums, axis=0)


def input_terms(x_blocks, average, inverse, grad_project, grad_pre_up, w_heads, w_up, vectors, own):
    count, ffl = grad_pre_up.shape
    whole = lambda rows, cols: pl.BlockSpec((rows, cols), lambda i: (0, 0))
    block = pl.BlockSpec((x_blocks[0].shape[0], TILE), lambda i: (0, i))
    *terms, sums = call(
        functools.partial(input_kernel, len(x_blocks)),
        [(x.shape, f32 if i < own else bf16) for i, x in enumerate(x_blocks)] + [((4, D), f32)],
        *x_blocks, average, inverse, grad_project, grad_pre_up, w_heads, w_up, vectors,
        grid=(D // TILE,),
        in_specs=[
            *[block] * len(x_blocks),
            whole(count, 1),
            whole(count, 1),
            whole(count, 3 * HS),
            whole(count, ffl),
            pl.BlockSpec((TILE, 3 * HS), lambda i: (i, 0)),
            pl.BlockSpec((TILE, ffl), lambda i: (i, 0)),
            pl.BlockSpec((vectors.shape[0], TILE), lambda i: (0, i)),
        ],
        out_specs=[*[block] * len(x_blocks), pl.BlockSpec((4, TILE), lambda i: (0, i))],
    )
    return terms, sums


def places(block, start, shape, dim, sizes, t):
    rows, tp = sizes
    index = start + lax.broadcasted_iota(jnp.int32, shape, dim)
    device = index // rows
    block = block ^ (device // tp)
    return (block * tp + (t ^ (device % tp))) * rows + index % rows


def attention_kernel(count, sizes, place_ref, q_ref, g_ref, *refs):
    kv_refs, (o_ref, dq_ref), refs = refs[:count], refs[count : count + 2], refs[count + 2 :]
    dkv_refs, sum_ref = refs[:-1], refs[-1]
    t, block, tile = place_ref[0], place_ref[1], 2 * TILE
    keys = jnp.concatenate([ref[:, :HS] for ref in kv_refs], axis=0)
    values = jnp.concatenate([ref[:, HS:] for ref in kv_refs], axis=0)
    keys_turned = keys.T
    values_turned = values.T
    key_places = places(block, 0, (keys.shape[0], 1), 0, sizes, t)
    sum_ref[...] = jnp.zeros_like(sum_ref)
    for start in range(0, q_ref.shape[0], tile):
        at = slice(start, start + tile)
        query = q_ref[at, :]
        grad = g_ref[at, :]
        visible = key_places <= places(block, start, (1, tile), 1, sizes, t)
        scores = jnp.where(visible, mm_nt(keys, query), -1e30)
        weights = jnp.exp(scores - jnp.max(scores, axis=0, keepdims=True))
        weights = weights * (1.0 / jnp.sum(weights, axis=0, keepdims=True))
        weights_low = weights.astype(bf16)
        result = mm(values_turned, weights_low)
        o_ref[at, :] = result.T.astype(bf16)
        sum_ref[:, HS:] += mm(weights_low, grad)
        delta = jnp.sum(result * grad.T.astype(f32), axis=0, keepdims=True)
        score_grad = (weights * (mm_nt(values, grad) - delta)).astype(bf16)
        dq_ref[at, :] = (mm(keys_turned, score_grad).T * (HS**-0.5)).astype(bf16)
        sum_ref[:, :HS] += mm(score_grad, query)
    start = 0
    for ref in dkv_refs:
        ref[...] = sum_ref[start : start + ref.shape[0], :].astype(bf16)
        start += ref.shape[0]


def long_attention_kernel(sizes, place_ref, q_ref, g_ref, kv_ref, o_ref, dq_ref, dkv_ref, sum_ref):
    blocks = kv_ref.shape[0] // KEYS
    t, block = place_ref[0], place_ref[1]
    sum_ref[...] = jnp.zeros_like(sum_ref)

    def step(at):
        query = q_ref[at, :]
        grad = g_ref[at, :]
        query_places = places(block, at.start, (1, TILE), 1, sizes, t)

        def scores_of(j):
            here = pl.ds(pl.multiple_of(j * KEYS, KEYS), KEYS)
            visible = places(block, j * KEYS, (KEYS, 1), 0, sizes, t) <= query_places
            return here, jnp.where(visible, mm_nt(kv_ref[here, :HS], query), -1e30)

        def first(j, state):
            top, total = state
            _, scores = scores_of(j)
            higher = jnp.maximum(top, jnp.max(scores, axis=0, keepdims=True))
            now = jnp.sum(jnp.exp(scores - higher), axis=0, keepdims=True)
            return higher, total * jnp.exp(top - higher) + now

        row = (1, TILE)
        top, total = lax.fori_loop(
            0, blocks, first, (jnp.full(row, -1e30, f32), jnp.zeros(row, f32))
        )
        inverse = 1.0 / total

        def second(j, result):
            here, scores = scores_of(j)
            weights = jnp.exp(scores - top) * inverse
            return result + mm(kv_ref[here, HS:].T, weights.astype(bf16))

        result = lax.fori_loop(0, blocks, second, jnp.zeros((HS, TILE), f32))
        o_ref[at, :] = result.T.astype(bf16)
        delta = jnp.sum(result * grad.T.astype(f32), axis=0, keepdims=True)

        def third(j, result):
            here, scores = scores_of(j)
            weights = jnp.exp(scores - top) * inverse
            weight_grad = mm_nt(kv_ref[here, HS:], grad)
            score_grad = (weights * (weight_grad - delta)).astype(bf16)
            sum_ref[here, HS:] += mm(weights.astype(bf16), grad)
            sum_ref[here, :HS] += mm(score_grad, query)
            return result + mm(kv_ref[here, :HS].T, score_grad)

        result = lax.fori_loop(0, blocks, third, jnp.zeros((HS, TILE), f32))
        dq_ref[at, :] = (result.T * (HS**-0.5)).astype(bf16)

    tiles(q_ref.shape[0], step)
    dkv_ref[...] = sum_ref[...].astype(bf16)


def attention(query, grad, kv_blocks, sizes):
    place = jnp.stack([lax.axis_index(TP), lax.axis_index("bh")]).astype(jnp.int32)
    count, total = len(kv_blocks), sum(block.shape[0] for block in kv_blocks)
    low = (query.shape, bf16)
    scratch = [pltpu.VMEM((total, 2 * HS), f32)]
    vmem = pl.BlockSpec(memory_space=pltpu.VMEM)
    smem = pl.BlockSpec(memory_space=pltpu.SMEM)
    if total <= KEYS:
        attended, grad_query, *grad_kv = call(
            functools.partial(attention_kernel, count, sizes),
            [low, low] + [(block.shape, bf16) for block in kv_blocks],
            place, query, grad, *kv_blocks,
            scratch=scratch,
            in_specs=[smem] + [vmem] * (2 + count),
        )
        return attended, grad_query, grad_kv
    kv_all = jnp.concatenate(kv_blocks, axis=0)
    attended, grad_query, grad_kv = call(
        functools.partial(long_attention_kernel, sizes),
        [low, low, (kv_all.shape, bf16)],
        place, query, grad, kv_all,
        scratch=scratch,
        in_specs=[smem] + [vmem] * 3,
    )
    return attended, grad_query, jnp.split(grad_kv, count, axis=0)


def per_device(
    hidden_in,
    gain_attn,
    shift_attn,
    gain_mlp,
    shift_mlp,
    qkv_weight,
    qkv_bias,
    dense_weight,
    up_weight,
    up_bias,
    down_weight,
    out_bias,
    cotangent,
):
    seq_count, sub_len, _ = hidden_in.shape
    tp, rp = lax.axis_size(TP), lax.axis_size(RP)
    n_dev = lax.axis_size(ALL)
    t = lax.axis_index(TP)
    bh, bh_size, bl_size = lax.axis_index("bh"), lax.axis_size("bh"), lax.axis_size("bl")
    rows = qkv_weight.shape[0]
    ff = up_weight.shape[1]
    ffl = ff // tp
    group_len = sub_len * tp

    vmem = pl.BlockSpec(memory_space=pltpu.VMEM)
    x_own = hidden_in.reshape(sub_len, D)
    join = Order(out_bias).join
    g_own = cotangent.reshape(sub_len, D)
    smalls = jnp.concatenate(
        [
            vector.reshape(-1, rows)
            for vector in (
                gain_attn, shift_attn, gain_mlp, shift_mlp, out_bias, qkv_bias, up_bias
            )
        ],
        axis=0,
    )
    kinds = smalls.shape[0]
    count = kinds * rows
    smalls = jnp.pad(smalls.reshape(1, count), ((0, 7), (0, 4 * HS - count)))
    heads_own = jnp.concatenate(
        [
            qkv_weight.reshape(rows, 3, HEADS, HS).transpose(2, 0, 1, 3).reshape(HEADS, rows, 3 * HS),
            dense_weight.reshape(rows, HEADS, HS).transpose(1, 0, 2),
        ],
        axis=2,
    )
    heads_own = jnp.concatenate(
        [heads_own, jnp.broadcast_to(smalls[None], (tp,) + smalls.shape)], axis=1
    )
    up_own = up_weight.reshape(rows, tp, ffl).transpose(1, 0, 2)
    down_own = down_weight.reshape(rows, tp, ffl).transpose(1, 0, 2)

    x_near = gather_start(x_own)
    x_side = gather_axis(x_own, "bl")
    g_side = gather_axis(g_own, "bl")
    x_near, x_side, g_side, heads_own = join(x_near, x_side, g_side, heads_own)
    m_heads = lax.all_to_all(heads_own, TP, split_axis=0, concat_axis=0, tiled=True)
    x_rows = [x_side] + [gather_axis(block, "bl") for block in x_near[:2]]
    x_near = gather_end(x_own, x_near)
    row = jnp.arange(group_len, dtype=jnp.int32)
    inside = ((row // sub_len) ^ t) * sub_len + row % sub_len
    query_places = bh * group_len + inside
    tables = rotary_tables(query_places.astype(f32))
    x_near, x_rows, m_heads, up_own, g_late, tables, down_own = join(
        x_near, x_rows, m_heads, up_own, g_own, tables, down_own
    )
    w_heads = spread_rest(m_heads[:, :rows].reshape(tp * rows, -1))
    x_rows += [gather_axis(block, "bl") for block in x_near[3:]]
    g_first = swap(g_late, "hd", 1)
    m_up = spread_group(up_own)
    smalls = gather_rest(m_heads[:, rows, :count]).reshape(n_dev, kinds, rows).astype(f32)
    vectors = smalls[:, :5].transpose(1, 0, 2).reshape(5, D)
    nq = qkv_bias.shape[0] // rows
    b_qkv = smalls[:, 5 : 5 + nq].reshape(3, HEADS, HS)
    b_up = smalls[:, 5 + nq :].reshape(tp, ffl)
    b_qkv = lax.dynamic_index_in_dim(b_qkv, t, 1, keepdims=False).reshape(1, 3 * HS)
    b_up = lax.dynamic_index_in_dim(b_up, t, 0, keepdims=True)

    x_rows, g_first, m_up, g_late, down_own, vectors, b_qkv, b_up = join(
        x_rows, g_first, m_up, g_late, down_own, vectors, b_qkv, b_up
    )
    w_up = spread_rest(m_up)
    x_blocks = [row[far] for far in range(bl_size) for row in x_rows]
    g_rows = [g_side, gather_axis(g_first, "bl")]
    hd_size = lax.axis_size("hd")
    four = hd_size == 4
    g_near = [g_first] + [swap(g_late, "hd", d) for d in range(2, 3 if hd_size == 4 else hd_size)]
    attn_in, mlp_in, query, kv, average, inverse = call(
        functools.partial(project_kernel, tp),
        [
            ((group_len, D), bf16),
            ((group_len, D), bf16),
            ((group_len, HS), bf16),
            ((group_len, 2 * HS), bf16),
            ((group_len, 1), f32),
            ((group_len, 1), f32),
        ],
        *x_blocks, vectors, w_heads, b_qkv, *tables,
        grid=(1,),
        in_specs=[vmem] * (tp + 1) + [pl.BlockSpec((D, 3 * HS), lambda i: (0, 0))] + [vmem] * 4,
    )
    g_rows, g_near, kv, mlp_in, g_late, down_own = join(
        g_rows, g_near, kv, mlp_in, g_late, down_own
    )
    g_near = gather_end(g_late, g_near)
    g_rows += [gather_axis(block, "bl") for block in g_near[2:3]]
    g_rows, g_near, down_own, mlp_in = join(g_rows, g_near, down_own, mlp_in)
    g_rows += [gather_axis(block, "bl") for block in g_near[3:]]
    kv_blocks = gather_axis(kv, "bh")
    m_down = spread_group(down_own)
    activated, slope = forward(mlp_in, w_up, b_up)
    g_rows, kv_blocks, m_down, activated, slope = join(g_rows, kv_blocks, m_down, activated, slope)
    w_down = spread_rest(m_down)
    g_blocks = [row[far] for far in range(bl_size) for row in g_rows]
    g_all, grad_att = call(
        functools.partial(cotangent_kernel, tp),
        [((group_len, D), bf16), ((group_len, HS), bf16)],
        *g_blocks, w_heads,
        grid=(1,),
        in_specs=[vmem] * tp + [pl.BlockSpec((D, HS), lambda i: (0, 3))],
    )
    down_far = weight_half(g_all, activated, 1)
    down_far, grad_att, g_all = join(down_far, grad_att, g_all)
    down_far = [swap(terms, "dp", 1) for terms in reversed(down_far)][::-1]
    down_own = weight_half(g_all, activated, 0)
    down_far, down_own, grad_att = join(down_far, down_own, grad_att)
    down_sent = add(*[([down_far[d], down_own[d]], bf16, 1) for d in range(1, bh_size)])
    down_sent, grad_att = join(down_sent, grad_att)
    down_others = [swap(sent[0], "bh", d + 1) for d, sent in enumerate(down_sent)]
    attended, grad_query, grad_kv = attention(query, grad_att, kv_blocks, (sub_len, tp))
    hd_terms = (hd_size, sub_len)
    out_far = [
        output_terms(attended, activated, w_heads, w_down, far, *hd_terms, bf16)
        for far in range(1, bl_size)
    ]
    out_own = output_terms(attended, activated, w_heads, w_down, 0, *hd_terms, f32)
    down_others, out_far, attended, slope, out_own = join(
        down_others, out_far, attended, slope, out_own
    )
    part = hd_size // 4
    parts = [range(hd_size - (g + 1) * part, hd_size - g * part) for g in range(4)]

    def over_bl(terms, ds):
        return {d: [swap(term[d], "bl", f + 1) for f, term in enumerate(terms)] for d in ds}

    def sums_of(own, received, ds, handed=()):
        return [
            ([own[d], *received[d], *(handed if d == 2 else ())], f32 if d == 0 else bf16, 1)
            for d in ds
        ]

    ((down_last,),) = add(([down_far[0], down_own[0], *down_others], bf16, 1))
    down_last, attended, slope = join(down_last, attended, slope)
    kv_others = [swap(grad_kv[d], "bh", d) for d in range(1, bh_size)]
    down_grad = collect_group(down_last)
    received = over_bl(out_far, parts[0])
    grad_pre_up, up_bias_term = backward(g_all, w_down, slope)
    up_terms = weight_terms(mlp_in, grad_pre_up)
    kv_others, down_grad, received, grad_pre_up, out_far, up_terms = join(
        kv_others, down_grad, received, grad_pre_up, out_far, up_terms
    )
    up_mine = collect_rest(up_terms)
    out = dict(zip(parts[0], add(*sums_of(out_own, received, parts[0]))))
    out, kv_others = join(out, kv_others)
    out_near = {d: hand_on(out[d][0], d) for d in parts[0]}
    middle = [*parts[1], *parts[2]]
    received = over_bl(out_far, middle)
    grad_project, qkv_bias_term = call(
        functools.partial(turn_back_kernel, bh_size),
        [((group_len, 3 * HS), bf16), ((1, 3 * HS), f32)],
        grad_query, grad_kv[0], *kv_others, *tables,
    )
    in_terms, sums = input_terms(
        x_blocks, average, inverse, grad_project, grad_pre_up, w_heads, w_up, vectors, hd_size
    )
    in_own = in_terms[:hd_size]
    in_far = [in_terms[f * hd_size : (f + 1) * hd_size] for f in range(1, bl_size)]
    out_near, received, out_far, in_far, grad_project = join(
        out_near, received, out_far, in_far, grad_project
    )
    out = add(*sums_of(out_own, received, middle, [out_near[3]] if four else []))
    out, in_far, grad_project = join(out, in_far, grad_project)
    out_near |= {d: hand_on(term, d) for d, (term,) in zip(middle, out)}
    received = over_bl(out_far, parts[3])
    received_in = over_bl(in_far, parts[0])
    heads_terms = weight_terms(attn_in, grad_project, g_all, attended)
    sums = jnp.concatenate([sums, jnp.sum(g_own.astype(f32), axis=0, keepdims=True)], axis=0)
    qkv_bias_full = lax.dynamic_update_slice(
        jnp.zeros((3, HEADS, HS), f32), qkv_bias_term.reshape(3, 1, HS), (0, t, 0)
    )
    up_bias_full = lax.dynamic_update_slice(jnp.zeros((tp, ffl), f32), up_bias_term, (t, 0))
    small_terms = jnp.concatenate(
        [
            sums.reshape(5, n_dev, rows).transpose(1, 0, 2),
            qkv_bias_full.reshape(n_dev, nq, rows),
            up_bias_full.reshape(n_dev, -1, rows),
        ],
        axis=1,
    )
    out_near, received, received_in, heads_terms, up_mine, in_far, small = join(
        out_near, received, received_in, heads_terms, up_mine, in_far, small_terms
    )
    heads_mine = collect_rest(heads_terms)
    ins = add(*sums_of(in_own, received_in, parts[0]))
    ins, up_mine, in_far = join(ins, up_mine, in_far)
    up_grad = collect_group(up_mine)
    in_near = {d: hand_on(term, d) for d, (term,) in zip(parts[0], ins)}
    received_in = over_bl(in_far, middle)
    small = exchange(small.reshape(rp, bl_size, hd_size, kinds, rows), RP, 0)
    up_grad, in_near, received_in, small, in_far = join(
        up_grad, in_near, received_in, small, in_far
    )
    ins = add(*sums_of(in_own, received_in, middle, [in_near[3]] if four else []))
    in_far, heads_mine, small = join(in_far, heads_mine, small)
    heads_grad = collect_group(heads_mine)
    received_in = over_bl(in_far, parts[3])
    down_grad = down_grad.astype(f32).transpose(1, 0, 2).reshape(rows, ff)
    up_grad = up_grad.astype(f32).transpose(1, 0, 2).reshape(rows, ff)
    small = exchange(sum(small[1:], small[0]), "hd", 1)
    heads_grad, received_in, down_grad, up_grad, ins, small = join(
        heads_grad, received_in, down_grad, up_grad, ins, small
    )
    in_near |= {d: hand_on(term, d) for d, (term,) in zip(middle, ins)}
    small = exchange(sum(small[1:], small[0]), "bl", 0)
    heads_grad = heads_grad.astype(f32)
    dense_grad = heads_grad[:, :, 3 * HS :].transpose(1, 0, 2).reshape(rows, D)
    qkv_grad = (
        heads_grad[:, :, : 3 * HS]
        .reshape(tp, rows, 3, HS)
        .transpose(1, 2, 0, 3)
        .reshape(rows, 3 * D)
    )

    def total(own, received, near):
        rest = {d: sum((x.astype(f32) for x in received[d]), own[d]) for d in received}
        near = near | {d: hand_on(rest[d].astype(bf16), d) for d in rest if d}
        straight = [d for d in range(1, hd_size) if not (four and d == 3)]
        return sum((near[d].astype(f32) for d in straight), rest[0])

    projected = total(out_own, received, out_near)
    output = (x_own.astype(f32) + projected + vectors[4:5]).astype(bf16)
    in_near, received_in, small, dense_grad, qkv_grad, output, in_own = join(
        in_near, received_in, small, dense_grad, qkv_grad, output, in_own
    )
    small = sum(small[1:], small[0])
    grad_normed = total(in_own, received_in, in_near)
    own = x_own.astype(f32)
    own_average, own_inverse = statistics(own)
    own_normed = (own - own_average) * own_inverse
    grad_hidden = g_own.astype(f32) + own_inverse * (
        grad_normed
        - jnp.mean(grad_normed, axis=1, keepdims=True)
        - own_normed * jnp.mean(grad_normed * own_normed, axis=1, keepdims=True)
    )
    return (
        output.reshape(seq_count, sub_len, D),
        grad_hidden.reshape(seq_count, sub_len, D),
        small[0],
        small[1],
        small[2],
        small[3],
        qkv_grad,
        small[5 : 5 + nq].reshape(-1),
        dense_grad,
        up_grad,
        small[5 + nq :].reshape(-1),
        down_grad,
        small[4],
    )


def solution(mesh):
    dp, blk, hd = (mesh.shape[name] for name in ("dp", "blk", "hd"))
    low = HEADS // hd
    inner = Mesh(mesh.devices.reshape(dp, blk // low, low, hd), ALL)
    token = P("dp", ("bh", "bl", "hd"), None)
    vector = P(ALL)
    matrix = P(ALL, None)
    return jax.shard_map(
        per_device,
        mesh=inner,
        in_specs=(
            token, vector, vector, vector, vector, matrix, vector,
            matrix, matrix, vector, matrix, vector, token,
        ),
        out_specs=(
            token, token, vector, vector, vector, vector, matrix, vector,
            matrix, matrix, vector, matrix, vector,
        ),
        check_vma=False,
    )
```

```python
import functools

import jax
import jax.numpy as jnp
from jax import lax
from jax.experimental import pallas as pl
from jax.experimental.pallas import tpu as pltpu
from jax.sharding import Mesh, PartitionSpec as P

D = 2048
HEADS = 8
HS = 256
ROT = 64

TP = ("bl", "hd")
RP = ("dp", "bh")
ALL = ("dp", "bh", "bl", "hd")

epsilon = 1e-05
contract_last = (((1,), (1,)), ((), ()))
f32 = jnp.float32
bf16 = jnp.bfloat16


def rotary_tables(positions):
    half_rot = ROT // 2
    frequency = 10000.0 ** (-(2.0 * jnp.arange(half_rot, dtype=f32)) / ROT)
    angles = positions[:, None] * frequency[None, :]
    cosine, sine = jnp.cos(angles), jnp.sin(angles)
    none = jnp.zeros_like(sine)
    rest = jnp.ones((positions.shape[0], 128 - ROT), f32)
    return (
        jnp.concatenate([cosine, cosine, rest], axis=1),
        jnp.concatenate([-sine, none, 0.0 * rest], axis=1),
        jnp.concatenate([none, sine, 0.0 * rest], axis=1),
    )


def mm(a, b):
    return jnp.dot(a, b, preferred_element_type=f32)


def mm_nt(a, b):
    return lax.dot_general(a, b, contract_last, preferred_element_type=f32)


class Order:
    def __init__(self, token):
        self.token = token

    def join(self, *values):
        self.token, values = lax.optimization_barrier((self.token, values))
        return values


def swap(value, axis, distance):
    size = lax.axis_size(axis)
    return lax.ppermute(value, axis, [(i, i ^ distance) for i in range(size)])


def gather_axis(value, axis):
    return [value] + [swap(value, axis, d) for d in range(1, lax.axis_size(axis))]


def gather_start(value):
    size = lax.axis_size("hd")
    return [swap(value, "hd", d) for d in range(1, 3 if size == 4 else size)]


def gather_end(value, near):
    if lax.axis_size("hd") == 4:
        near = [near[0], near[1], swap(near[1], "hd", 1)]
    return [value] + near


def gather_rest(value):
    place, size = lax.axis_index(RP), lax.axis_size(RP)
    blocks = jnp.stack([value] + [swap(value, RP, d) for d in range(1, size)])
    bit = 1
    while bit < size:
        pairs = blocks.reshape((size // (2 * bit), 2, bit) + value.shape)
        turned = jnp.stack([pairs[:, 1], pairs[:, 0]], axis=1).reshape(blocks.shape)
        blocks = jnp.where((place & bit) != 0, turned, blocks)
        bit *= 2
    return blocks


def hand_on(value, distance):
    if lax.axis_size("hd") == 4 and distance == 3:
        distance = 1
    return swap(value, "hd", distance)


def exchange(terms, axis, dim):
    place, size = lax.axis_index(axis), lax.axis_size(axis)
    pick = lambda d: lax.dynamic_index_in_dim(terms, place ^ d, dim, keepdims=False)
    return [pick(0)] + [swap(pick(d), axis, d) for d in range(1, size)]


def spread_group(shard):
    mine = lax.all_to_all(shard, TP, split_axis=0, concat_axis=0, tiled=True)
    return mine.reshape(-1, shard.shape[2])


def spread_rest(mine):
    return lax.all_gather(mine, RP, axis=0, tiled=True)


def collect_rest(terms):
    return lax.psum_scatter(terms, RP, scatter_dimension=0, tiled=True)


def collect_group(mine):
    mine = mine.reshape(lax.axis_size(TP), -1, mine.shape[1])
    return lax.all_to_all(mine, TP, split_axis=0, concat_axis=0, tiled=True)


TILE = 256
KEYS = 2048


def call(kernel, outs, *ins, scratch=(), grid=(), in_specs=None, out_specs=None):
    vmem = pl.BlockSpec(memory_space=pltpu.VMEM)
    return pl.pallas_call(
        kernel,
        grid=grid,
        out_shape=[jax.ShapeDtypeStruct(shape, dtype) for shape, dtype in outs],
        in_specs=in_specs or [vmem] * len(ins),
        out_specs=out_specs or [vmem] * len(outs),
        scratch_shapes=list(scratch),
        compiler_params=pltpu.CompilerParams(vmem_limit_bytes=58 * 2**20),
        cost_estimate=pl.CostEstimate(flops=1, bytes_accessed=1, transcendentals=0),
    )(*ins)


def tiles(count, step):
    def body(i, _):
        step(pl.ds(pl.multiple_of(i * TILE, TILE), TILE))
        return 0

    lax.fori_loop(0, count // TILE, body, 0)


def add(*groups):
    return [
        [sum((x.astype(f32) for x in arrays[1:]), arrays[0].astype(f32)).astype(dtype)]
        for arrays, dtype, _ in groups
    ]


def turn(value, tables, sign):
    own, above, below = tables
    first = value[:, :128]
    turned = first * own + sign * (
        pltpu.roll(first, 96, 1) * above + pltpu.roll(first, 32, 1) * below
    )
    return jnp.concatenate([turned, value[:, 128:]], axis=1)


def statistics(block):
    average = jnp.mean(block, axis=1, keepdims=True)
    centered = block - average
    return average, lax.rsqrt(jnp.mean(centered * centered, axis=1, keepdims=True) + epsilon)


def project_kernel(count, *refs):
    x_refs, refs = refs[:count], refs[count:]
    vec_ref, w_ref, b_ref, own_ref, above_ref, below_ref, *refs = refs
    attn_ref, mlp_ref, q_ref, kv_ref, average_ref, inverse_ref = refs
    rows = x_refs[0].shape[0]
    for start in range(0, count * rows, TILE):
        for i in range(start // rows, (start + TILE) // rows):
            at = slice(i * rows, (i + 1) * rows)
            block = x_refs[i][...].astype(f32)
            average, inverse = statistics(block)
            average_ref[at, :] = average
            inverse_ref[at, :] = inverse
            normed = (block - average) * inverse
            attn_ref[at, :] = (normed * vec_ref[0:1, :] + vec_ref[1:2, :]).astype(bf16)
            mlp_ref[at, :] = (normed * vec_ref[2:3, :] + vec_ref[3:4, :]).astype(bf16)
        at = slice(start, start + TILE)
        project = mm(attn_ref[at, :], w_ref[...]) + b_ref[...]
        tables = own_ref[at, :], above_ref[at, :], below_ref[at, :]
        query = turn(project[:, :HS], tables, 1.0).astype(bf16)
        q_ref[at, :] = (query.astype(f32) * HS**-0.5).astype(bf16)
        kv_ref[at, :HS] = turn(project[:, HS : 2 * HS], tables, 1.0).astype(bf16)
        kv_ref[at, HS:] = project[:, 2 * HS :].astype(bf16)


def cotangent_kernel(count, *refs):
    g_refs, (w_ref, g_ref, out_ref) = refs[:count], refs[count:]
    rows = g_refs[0].shape[0]
    for i in range(count):
        g_ref[i * rows : (i + 1) * rows, :] = g_refs[i][...]

    def step(at):
        out_ref[at, :] = mm(g_ref[at, :], w_ref[...]).astype(bf16)

    tiles(g_ref.shape[0], step)


def forward_kernel(mlp_ref, w_ref, b_ref, act_ref, slope_ref):
    def step(at):
        value = mm(mlp_ref[at, :], w_ref[...]) + b_ref[...]
        cdf = 0.5 * (1.0 + lax.erf(value * 0.7071067811865476))
        density = jnp.exp(-0.5 * value * value) * 0.3989422804014327
        act_ref[at, :] = (value * cdf).astype(bf16)
        slope_ref[at, :] = cdf + value * density

    tiles(mlp_ref.shape[0], step)


def forward(mlp_in, w_up, b_up):
    count, ffl = mlp_in.shape[0], w_up.shape[1]
    columns = pl.BlockSpec((count, TILE), lambda i: (0, i))
    return call(
        forward_kernel,
        [((count, ffl), bf16), ((count, ffl), f32)],
        mlp_in, w_up, b_up,
        grid=(ffl // TILE,),
        in_specs=[
            pl.BlockSpec((count, D), lambda i: (0, 0)),
            pl.BlockSpec((D, TILE), lambda i: (0, i)),
            pl.BlockSpec((1, TILE), lambda i: (0, i)),
        ],
        out_specs=[columns, columns],
    )


def backward_kernel(g_ref, w_ref, slope_ref, out_ref, sum_ref):
    grad = (mm(g_ref[...], w_ref[...]) * slope_ref[...]).astype(bf16)
    out_ref[...] = grad
    sum_ref[...] = jnp.sum(grad.astype(f32), axis=0, keepdims=True)


def backward(g_all, w_down, slope):
    count, ffl = slope.shape
    columns = pl.BlockSpec((count, TILE), lambda i: (0, i))
    return call(
        backward_kernel,
        [((count, ffl), bf16), ((1, ffl), f32)],
        g_all, w_down, slope,
        grid=(ffl // TILE,),
        in_specs=[
            pl.BlockSpec((count, D), lambda i: (0, 0)),
            pl.BlockSpec((D, TILE), lambda i: (0, i)),
            columns,
        ],
        out_specs=[columns, pl.BlockSpec((1, TILE), lambda i: (0, i))],
    )


def weight_kernel(*refs):
    pairs, out_ref = refs[:-1], refs[-1]
    start = 0
    for lhs_ref, rhs_ref in zip(pairs[::2], pairs[1::2]):
        cols = slice(start, start + rhs_ref.shape[1])
        start += rhs_ref.shape[1]
        out_ref[:, cols] = mm(lhs_ref[...].T, rhs_ref[...]).astype(bf16)


def weight_terms(*pairs):
    count = pairs[0].shape[0]
    cols = sum(rhs.shape[1] for rhs in pairs[1::2])
    specs = []
    for rhs in pairs[1::2]:
        specs.append(pl.BlockSpec((count, 2 * TILE), lambda i: (0, i)))
        specs.append(pl.BlockSpec(rhs.shape, lambda i: (0, 0)))
    return call(
        weight_kernel,
        [((D, cols), bf16)],
        *pairs,
        grid=(D // (2 * TILE),),
        in_specs=specs,
        out_specs=[pl.BlockSpec((2 * TILE, cols), lambda i: (i, 0))],
    )[0]


def weight_half_kernel(per, place_ref, lhs_ref, rhs_ref, *out_refs):
    term = mm(lhs_ref[...].T, rhs_ref[...]).astype(bf16)
    for d, out_ref in enumerate(out_refs):

        @pl.when(pl.program_id(0) // per == d)
        def _(out_ref=out_ref):
            out_ref[...] = term


def weight_half(lhs, rhs, other):
    bh = lax.axis_size("bh")
    part = D // (2 * bh)
    tile = min(2 * TILE, part)
    per = part // tile
    place = jnp.stack([lax.axis_index("dp") ^ other, lax.axis_index("bh")]).astype(jnp.int32)
    count, cols = rhs.shape

    def lhs_at(i, place_ref):
        return (0, (place_ref[0] * bh + (place_ref[1] ^ (i // per))) * per + i % per)

    def out_at(d):
        return lambda i, place_ref: (jnp.clip(i - d * per, 0, per - 1), 0)

    return pl.pallas_call(
        functools.partial(weight_half_kernel, per),
        grid_spec=pltpu.PrefetchScalarGridSpec(
            num_scalar_prefetch=1,
            grid=(bh * per,),
            in_specs=[
                pl.BlockSpec((count, tile), lhs_at),
                pl.BlockSpec((count, cols), lambda i, place_ref: (0, 0)),
            ],
            out_specs=[pl.BlockSpec((tile, cols), out_at(d)) for d in range(bh)],
        ),
        out_shape=[jax.ShapeDtypeStruct((part, cols), bf16)] * bh,
        compiler_params=pltpu.CompilerParams(vmem_limit_bytes=58 * 2**20),
        cost_estimate=pl.CostEstimate(flops=1, bytes_accessed=1, transcendentals=0),
    )(place, lhs, rhs)


def output_kernel(att_ref, act_ref, dense_ref, down_ref, *out_refs):
    term = mm_nt(att_ref[...], dense_ref[...]) + mm_nt(act_ref[...], down_ref[...])
    rows = out_refs[0].shape[0]
    for i, out_ref in enumerate(out_refs):
        out_ref[...] = term[i * rows : (i + 1) * rows].astype(out_ref.dtype)


def output_terms(attended, activated, w_heads, w_down, part, count, rows, dtype):
    ffl, wide = activated.shape[1], 4 * TILE if count * rows <= 512 else 2 * TILE
    return call(
        output_kernel,
        [((rows, D), dtype)] * count,
        attended, activated, w_heads, w_down,
        grid=(D // wide,),
        in_specs=[
            pl.BlockSpec((count * rows, HS), lambda i: (part, 0)),
            pl.BlockSpec((count * rows, ffl), lambda i: (part, 0)),
            pl.BlockSpec((wide, HS), lambda i: (i, 3)),
            pl.BlockSpec((wide, ffl), lambda i: (i, 0)),
        ],
        out_specs=[pl.BlockSpec((rows, wide), lambda i: (0, i))] * count,
    )


def turn_back_kernel(count, *refs):
    dq_ref, refs = refs[0], refs[1:]
    term_refs, (own_ref, above_ref, below_ref, out_ref, sum_ref) = refs[:count], refs[count:]
    sum_ref[...] = jnp.zeros_like(sum_ref)

    def step(at):
        tables = own_ref[at, :], above_ref[at, :], below_ref[at, :]
        grad = term_refs[0][at, :].astype(f32)
        for ref in term_refs[1:]:
            grad += ref[at, :].astype(f32)
        grad = grad.astype(bf16)
        out_ref[at, :HS] = turn(dq_ref[at, :].astype(f32), tables, -1.0).astype(bf16)
        out_ref[at, HS : 2 * HS] = turn(grad[:, :HS].astype(f32), tables, -1.0).astype(bf16)
        out_ref[at, 2 * HS :] = grad[:, HS:]
        sum_ref[...] += jnp.sum(out_ref[at, :].astype(f32), axis=0, keepdims=True)

    tiles(dq_ref.shape[0], step)


def input_kernel(count, *refs):
    x_refs, refs = refs[:count], refs[count:]
    average_ref, inverse_ref, gp_ref, gu_ref, heads_ref, up_ref, vec_ref = refs[:7]
    out_refs, sum_ref = refs[7:-1], refs[-1]
    rows = x_refs[0].shape[0]
    sums = [0.0] * 4
    for start in range(0, count * rows, TILE):
        at = slice(start, start + TILE)
        attn = mm_nt(gp_ref[at, :], heads_ref[...])
        mlp = mm_nt(gu_ref[at, :], up_ref[...])
        block = jnp.concatenate(
            [x_refs[i][...].astype(f32) for i in range(start // rows, (start + TILE) // rows)],
            axis=0,
        )
        normed = (block - average_ref[at, :]) * inverse_ref[at, :]
        for i, term in enumerate((attn * normed, attn, mlp * normed, mlp)):
            sums[i] = sums[i] + jnp.sum(term, axis=0, keepdims=True)
        out = attn * vec_ref[0:1, :] + mlp * vec_ref[2:3, :]
        for i in range(0, TILE, rows):
            out_ref = out_refs[(start + i) // rows]
            out_ref[...] = out[i : i + rows].astype(out_ref.dtype)
    sum_ref[...] = jnp.concatenate(sums, axis=0)


def input_terms(x_blocks, average, inverse, grad_project, grad_pre_up, w_heads, w_up, vectors, own):
    count, ffl = grad_pre_up.shape
    whole = lambda rows, cols: pl.BlockSpec((rows, cols), lambda i: (0, 0))
    block = pl.BlockSpec((x_blocks[0].shape[0], TILE), lambda i: (0, i))
    *terms, sums = call(
        functools.partial(input_kernel, len(x_blocks)),
        [(x.shape, f32 if i < own else bf16) for i, x in enumerate(x_blocks)] + [((4, D), f32)],
        *x_blocks, average, inverse, grad_project, grad_pre_up, w_heads, w_up, vectors,
        grid=(D // TILE,),
        in_specs=[
            *[block] * len(x_blocks),
            whole(count, 1),
            whole(count, 1),
            whole(count, 3 * HS),
            whole(count, ffl),
            pl.BlockSpec((TILE, 3 * HS), lambda i: (i, 0)),
            pl.BlockSpec((TILE, ffl), lambda i: (i, 0)),
            pl.BlockSpec((vectors.shape[0], TILE), lambda i: (0, i)),
        ],
        out_specs=[*[block] * len(x_blocks), pl.BlockSpec((4, TILE), lambda i: (0, i))],
    )
    return terms, sums


def places(block, start, shape, dim, sizes, t):
    rows, tp = sizes
    index = start + lax.broadcasted_iota(jnp.int32, shape, dim)
    device = index // rows
    block = block ^ (device // tp)
    return (block * tp + (t ^ (device % tp))) * rows + index % rows


def attention_kernel(count, sizes, place_ref, q_ref, g_ref, *refs):
    kv_refs, (o_ref, dq_ref), refs = refs[:count], refs[count : count + 2], refs[count + 2 :]
    dkv_refs, sum_ref = refs[:-1], refs[-1]
    t, block, tile = place_ref[0], place_ref[1], 2 * TILE
    keys = jnp.concatenate([ref[:, :HS] for ref in kv_refs], axis=0)
    values = jnp.concatenate([ref[:, HS:] for ref in kv_refs], axis=0)
    keys_turned = keys.T
    values_turned = values.T
    key_places = places(block, 0, (keys.shape[0], 1), 0, sizes, t)
    sum_ref[...] = jnp.zeros_like(sum_ref)
    for start in range(0, q_ref.shape[0], tile):
        at = slice(start, start + tile)
        query = q_ref[at, :]
        grad = g_ref[at, :]
        visible = key_places <= places(block, start, (1, tile), 1, sizes, t)
        scores = jnp.where(visible, mm_nt(keys, query), -1e30)
        weights = jnp.exp(scores - jnp.max(scores, axis=0, keepdims=True))
        weights = weights * (1.0 / jnp.sum(weights, axis=0, keepdims=True))
        weights_low = weights.astype(bf16)
        result = mm(values_turned, weights_low)
        o_ref[at, :] = result.T.astype(bf16)
        sum_ref[:, HS:] += mm(weights_low, grad)
        delta = jnp.sum(result * grad.T.astype(f32), axis=0, keepdims=True)
        score_grad = (weights * (mm_nt(values, grad) - delta)).astype(bf16)
        dq_ref[at, :] = (mm(keys_turned, score_grad).T * (HS**-0.5)).astype(bf16)
        sum_ref[:, :HS] += mm(score_grad, query)
    start = 0
    for ref in dkv_refs:
        ref[...] = sum_ref[start : start + ref.shape[0], :].astype(bf16)
        start += ref.shape[0]


def long_attention_kernel(sizes, place_ref, q_ref, g_ref, kv_ref, o_ref, dq_ref, dkv_ref, sum_ref):
    blocks = kv_ref.shape[0] // KEYS
    t, block = place_ref[0], place_ref[1]
    sum_ref[...] = jnp.zeros_like(sum_ref)

    def step(at):
        query = q_ref[at, :]
        grad = g_ref[at, :]
        query_places = places(block, at.start, (1, TILE), 1, sizes, t)

        def scores_of(j):
            here = pl.ds(pl.multiple_of(j * KEYS, KEYS), KEYS)
            visible = places(block, j * KEYS, (KEYS, 1), 0, sizes, t) <= query_places
            return here, jnp.where(visible, mm_nt(kv_ref[here, :HS], query), -1e30)

        def first(j, state):
            top, total = state
            _, scores = scores_of(j)
            higher = jnp.maximum(top, jnp.max(scores, axis=0, keepdims=True))
            now = jnp.sum(jnp.exp(scores - higher), axis=0, keepdims=True)
            return higher, total * jnp.exp(top - higher) + now

        row = (1, TILE)
        top, total = lax.fori_loop(
            0, blocks, first, (jnp.full(row, -1e30, f32), jnp.zeros(row, f32))
        )
        inverse = 1.0 / total

        def second(j, result):
            here, scores = scores_of(j)
            weights = jnp.exp(scores - top) * inverse
            return result + mm(kv_ref[here, HS:].T, weights.astype(bf16))

        result = lax.fori_loop(0, blocks, second, jnp.zeros((HS, TILE), f32))
        o_ref[at, :] = result.T.astype(bf16)
        delta = jnp.sum(result * grad.T.astype(f32), axis=0, keepdims=True)

        def third(j, result):
            here, scores = scores_of(j)
            weights = jnp.exp(scores - top) * inverse
            weight_grad = mm_nt(kv_ref[here, HS:], grad)
            score_grad = (weights * (weight_grad - delta)).astype(bf16)
            sum_ref[here, HS:] += mm(weights.astype(bf16), grad)
            sum_ref[here, :HS] += mm(score_grad, query)
            return result + mm(kv_ref[here, :HS].T, score_grad)

        result = lax.fori_loop(0, blocks, third, jnp.zeros((HS, TILE), f32))
        dq_ref[at, :] = (result.T * (HS**-0.5)).astype(bf16)

    tiles(q_ref.shape[0], step)
    dkv_ref[...] = sum_ref[...].astype(bf16)


def attention(query, grad, kv_blocks, sizes):
    place = jnp.stack([lax.axis_index(TP), lax.axis_index("bh")]).astype(jnp.int32)
    count, total = len(kv_blocks), sum(block.shape[0] for block in kv_blocks)
    low = (query.shape, bf16)
    scratch = [pltpu.VMEM((total, 2 * HS), f32)]
    vmem = pl.BlockSpec(memory_space=pltpu.VMEM)
    smem = pl.BlockSpec(memory_space=pltpu.SMEM)
    if total <= KEYS:
        attended, grad_query, *grad_kv = call(
            functools.partial(attention_kernel, count, sizes),
            [low, low] + [(block.shape, bf16) for block in kv_blocks],
            place, query, grad, *kv_blocks,
            scratch=scratch,
            in_specs=[smem] + [vmem] * (2 + count),
        )
        return attended, grad_query, grad_kv
    kv_all = jnp.concatenate(kv_blocks, axis=0)
    attended, grad_query, grad_kv = call(
        functools.partial(long_attention_kernel, sizes),
        [low, low, (kv_all.shape, bf16)],
        place, query, grad, kv_all,
        scratch=scratch,
        in_specs=[smem] + [vmem] * 3,
    )
    return attended, grad_query, jnp.split(grad_kv, count, axis=0)


def per_device(
    hidden_in,
    gain_attn,
    shift_attn,
    gain_mlp,
    shift_mlp,
    qkv_weight,
    qkv_bias,
    dense_weight,
    up_weight,
    up_bias,
    down_weight,
    out_bias,
    cotangent,
):
    seq_count, sub_len, _ = hidden_in.shape
    tp, rp = lax.axis_size(TP), lax.axis_size(RP)
    n_dev = lax.axis_size(ALL)
    t = lax.axis_index(TP)
    bh, bh_size, bl_size = lax.axis_index("bh"), lax.axis_size("bh"), lax.axis_size("bl")
    rows = qkv_weight.shape[0]
    ff = up_weight.shape[1]
    ffl = ff // tp
    group_len = sub_len * tp

    vmem = pl.BlockSpec(memory_space=pltpu.VMEM)
    x_own = hidden_in.reshape(sub_len, D)
    join = Order(out_bias).join
    g_own = cotangent.reshape(sub_len, D)
    smalls = jnp.concatenate(
        [
            vector.reshape(-1, rows)
            for vector in (
                gain_attn, shift_attn, gain_mlp, shift_mlp, out_bias, qkv_bias, up_bias
            )
        ],
        axis=0,
    )
    kinds = smalls.shape[0]
    count = kinds * rows
    smalls = jnp.pad(smalls.reshape(1, count), ((0, 7), (0, 4 * HS - count)))
    heads_own = jnp.concatenate(
        [
            qkv_weight.reshape(rows, 3, HEADS, HS).transpose(2, 0, 1, 3).reshape(HEADS, rows, 3 * HS),
            dense_weight.reshape(rows, HEADS, HS).transpose(1, 0, 2),
        ],
        axis=2,
    )
    heads_own = jnp.concatenate(
        [heads_own, jnp.broadcast_to(smalls[None], (tp,) + smalls.shape)], axis=1
    )
    up_own = up_weight.reshape(rows, tp, ffl).transpose(1, 0, 2)
    down_own = down_weight.reshape(rows, tp, ffl).transpose(1, 0, 2)

    x_near = gather_start(x_own)
    x_side = gather_axis(x_own, "bl")
    g_side = gather_axis(g_own, "bl")
    x_near, x_side, g_side, heads_own, up_own, down_own = join(
        x_near, x_side, g_side, heads_own, up_own, down_own
    )
    m_heads = lax.all_to_all(heads_own, TP, split_axis=0, concat_axis=0, tiled=True)
    x_rows = [x_side, gather_axis(x_near[0], "bl")]
    x_second = x_near[1]
    x_left = gather_axis(x_second[: sub_len // 2], "bl")[1:]
    x_near = gather_end(x_own, x_near)
    row = jnp.arange(group_len, dtype=jnp.int32)
    inside = ((row // sub_len) ^ t) * sub_len + row % sub_len
    query_places = bh * group_len + inside
    tables = rotary_tables(query_places.astype(f32))
    x_near, x_rows, x_left, m_heads, up_own, g_late, tables, down_own, x_second = join(
        x_near, x_rows, x_left, m_heads, up_own, g_own, tables, down_own, x_second
    )
    x_right = gather_axis(x_second[sub_len // 2 :], "bl")[1:]
    w_heads = spread_rest(m_heads[:, :rows].reshape(tp * rows, -1))
    x_rows += [None] + [gather_axis(block, "bl") for block in x_near[3:]]
    g_first = swap(g_late, "hd", 1)
    m_up = spread_group(up_own)
    smalls = gather_rest(m_heads[:, rows, :count]).reshape(n_dev, kinds, rows).astype(f32)
    vectors = smalls[:, :5].transpose(1, 0, 2).reshape(5, D)
    nq = qkv_bias.shape[0] // rows
    b_qkv = smalls[:, 5 : 5 + nq].reshape(3, HEADS, HS)
    b_up = smalls[:, 5 + nq :].reshape(tp, ffl)
    b_qkv = lax.dynamic_index_in_dim(b_qkv, t, 1, keepdims=False).reshape(1, 3 * HS)
    b_up = lax.dynamic_index_in_dim(b_up, t, 0, keepdims=True)

    x_rows, x_right, g_first, m_up, g_late, down_own, vectors, b_qkv, b_up = join(
        x_rows, x_right, g_first, m_up, g_late, down_own, vectors, b_qkv, b_up
    )
    x_rows[2] = [x_second] + [
        jnp.concatenate(halves, axis=0) for halves in zip(x_left, x_right)
    ]
    w_up = spread_rest(m_up)
    x_blocks = [row[far] for far in range(bl_size) for row in x_rows]
    g_rows = [g_side, gather_axis(g_first, "bl")]
    hd_size = lax.axis_size("hd")
    four = hd_size == 4
    g_near = [g_first] + [swap(g_late, "hd", d) for d in range(2, 3 if hd_size == 4 else hd_size)]
    attn_in, mlp_in, query, kv, average, inverse = call(
        functools.partial(project_kernel, tp),
        [
            ((group_len, D), bf16),
            ((group_len, D), bf16),
            ((group_len, HS), bf16),
            ((group_len, 2 * HS), bf16),
            ((group_len, 1), f32),
            ((group_len, 1), f32),
        ],
        *x_blocks, vectors, w_heads, b_qkv, *tables,
        grid=(1,),
        in_specs=[vmem] * (tp + 1) + [pl.BlockSpec((D, 3 * HS), lambda i: (0, 0))] + [vmem] * 4,
    )
    g_rows, g_near, kv, mlp_in, g_late, down_own = join(
        g_rows, g_near, kv, mlp_in, g_late, down_own
    )
    g_near = gather_end(g_late, g_near)
    g_rows += [gather_axis(block, "bl") for block in g_near[2:3]]
    g_rows, g_near, down_own, mlp_in = join(g_rows, g_near, down_own, mlp_in)
    g_rows += [gather_axis(block, "bl") for block in g_near[3:]]
    kv_blocks = gather_axis(kv, "bh")
    m_down = spread_group(down_own)
    activated, slope = forward(mlp_in, w_up, b_up)
    g_rows, kv_blocks, m_down, activated, slope = join(g_rows, kv_blocks, m_down, activated, slope)
    w_down = spread_rest(m_down)
    g_blocks = [row[far] for far in range(bl_size) for row in g_rows]
    g_all, grad_att = call(
        functools.partial(cotangent_kernel, tp),
        [((group_len, D), bf16), ((group_len, HS), bf16)],
        *g_blocks, w_heads,
        grid=(1,),
        in_specs=[vmem] * tp + [pl.BlockSpec((D, HS), lambda i: (0, 3))],
    )
    down_far = weight_half(g_all, activated, 1)
    down_far, grad_att, g_all = join(down_far, grad_att, g_all)
    down_far = [swap(terms, "dp", 1) for terms in reversed(down_far)][::-1]
    down_own = weight_half(g_all, activated, 0)
    down_far, down_own, grad_att = join(down_far, down_own, grad_att)
    down_sent = add(*[([down_far[d], down_own[d]], bf16, 1) for d in range(1, bh_size)])
    down_sent, grad_att = join(down_sent, grad_att)
    down_others = [swap(sent[0], "bh", d + 1) for d, sent in enumerate(down_sent)]
    attended, grad_query, grad_kv = attention(query, grad_att, kv_blocks, (sub_len, tp))
    hd_terms = (hd_size, sub_len)
    out_far = [
        output_terms(attended, activated, w_heads, w_down, far, *hd_terms, bf16)
        for far in range(1, bl_size)
    ]
    out_own = output_terms(attended, activated, w_heads, w_down, 0, *hd_terms, f32)
    down_others, out_far, attended, slope, out_own = join(
        down_others, out_far, attended, slope, out_own
    )
    part = hd_size // 4
    parts = [range(hd_size - (g + 1) * part, hd_size - g * part) for g in range(4)]

    def over_bl(terms, ds):
        return {d: [swap(term[d], "bl", f + 1) for f, term in enumerate(terms)] for d in ds}

    def sums_of(own, received, ds, handed=()):
        return [
            ([own[d], *received[d], *(handed if d == 2 else ())], f32 if d == 0 else bf16, 1)
            for d in ds
        ]

    ((down_last,),) = add(([down_far[0], down_own[0], *down_others], bf16, 1))
    down_last, attended, slope = join(down_last, attended, slope)
    kv_others = [swap(grad_kv[d], "bh", d) for d in range(1, bh_size)]
    down_grad = collect_group(down_last)
    received = over_bl(out_far, parts[0])
    grad_pre_up, up_bias_term = backward(g_all, w_down, slope)
    up_terms = weight_terms(mlp_in, grad_pre_up)
    kv_others, down_grad, received, grad_pre_up, out_far, up_terms = join(
        kv_others, down_grad, received, grad_pre_up, out_far, up_terms
    )
    up_mine = collect_rest(up_terms)
    out = dict(zip(parts[0], add(*sums_of(out_own, received, parts[0]))))
    out, kv_others = join(out, kv_others)
    out_near = {d: hand_on(out[d][0], d) for d in parts[0]}
    middle = [*parts[1], *parts[2]]
    received = over_bl(out_far, middle)
    grad_project, qkv_bias_term = call(
        functools.partial(turn_back_kernel, bh_size),
        [((group_len, 3 * HS), bf16), ((1, 3 * HS), f32)],
        grad_query, grad_kv[0], *kv_others, *tables,
    )
    in_terms, sums = input_terms(
        x_blocks, average, inverse, grad_project, grad_pre_up, w_heads, w_up, vectors, hd_size
    )
    in_own = in_terms[:hd_size]
    in_far = [in_terms[f * hd_size : (f + 1) * hd_size] for f in range(1, bl_size)]
    out_near, received, out_far, in_far, grad_project = join(
        out_near, received, out_far, in_far, grad_project
    )
    out = add(*sums_of(out_own, received, middle, [out_near[3]] if four else []))
    out, in_far, grad_project = join(out, in_far, grad_project)
    out_near |= {d: hand_on(term, d) for d, (term,) in zip(middle, out)}
    received = over_bl(out_far, parts[3])
    received_in = over_bl(in_far, parts[0])
    heads_terms = weight_terms(attn_in, grad_project, g_all, attended)
    sums = jnp.concatenate([sums, jnp.sum(g_own.astype(f32), axis=0, keepdims=True)], axis=0)
    qkv_bias_full = lax.dynamic_update_slice(
        jnp.zeros((3, HEADS, HS), f32), qkv_bias_term.reshape(3, 1, HS), (0, t, 0)
    )
    up_bias_full = lax.dynamic_update_slice(jnp.zeros((tp, ffl), f32), up_bias_term, (t, 0))
    small_terms = jnp.concatenate(
        [
            sums.reshape(5, n_dev, rows).transpose(1, 0, 2),
            qkv_bias_full.reshape(n_dev, nq, rows),
            up_bias_full.reshape(n_dev, -1, rows),
        ],
        axis=1,
    )
    out_near, received, received_in, heads_terms, up_mine, in_far, small = join(
        out_near, received, received_in, heads_terms, up_mine, in_far, small_terms
    )
    heads_mine = collect_rest(heads_terms)
    ins = add(*sums_of(in_own, received_in, parts[0]))
    ins, up_mine, in_far = join(ins, up_mine, in_far)
    up_grad = collect_group(up_mine)
    in_near = {d: hand_on(term, d) for d, (term,) in zip(parts[0], ins)}
    received_in = over_bl(in_far, middle)
    small = exchange(small.reshape(rp, bl_size, hd_size, kinds, rows), RP, 0)
    up_grad, in_near, received_in, small, in_far = join(
        up_grad, in_near, received_in, small, in_far
    )
    ins = add(*sums_of(in_own, received_in, middle, [in_near[3]] if four else []))
    in_far, heads_mine, small = join(in_far, heads_mine, small)
    heads_grad = collect_group(heads_mine)
    received_in = over_bl(in_far, parts[3])
    down_grad = down_grad.astype(f32).transpose(1, 0, 2).reshape(rows, ff)
    up_grad = up_grad.astype(f32).transpose(1, 0, 2).reshape(rows, ff)
    small = exchange(sum(small[1:], small[0]), "hd", 1)
    heads_grad, received_in, down_grad, up_grad, ins, small = join(
        heads_grad, received_in, down_grad, up_grad, ins, small
    )
    in_near |= {d: hand_on(term, d) for d, (term,) in zip(middle, ins)}
    small = exchange(sum(small[1:], small[0]), "bl", 0)
    heads_grad = heads_grad.astype(f32)
    dense_grad = heads_grad[:, :, 3 * HS :].transpose(1, 0, 2).reshape(rows, D)
    qkv_grad = (
        heads_grad[:, :, : 3 * HS]
        .reshape(tp, rows, 3, HS)
        .transpose(1, 2, 0, 3)
        .reshape(rows, 3 * D)
    )

    def total(own, received, near):
        rest = {d: sum((x.astype(f32) for x in received[d]), own[d]) for d in received}
        near = near | {d: hand_on(rest[d].astype(bf16), d) for d in rest if d}
        straight = [d for d in range(1, hd_size) if not (four and d == 3)]
        return sum((near[d].astype(f32) for d in straight), rest[0])

    projected = total(out_own, received, out_near)
    output = (x_own.astype(f32) + projected + vectors[4:5]).astype(bf16)
    in_near, received_in, small, dense_grad, qkv_grad, output, in_own = join(
        in_near, received_in, small, dense_grad, qkv_grad, output, in_own
    )
    small = sum(small[1:], small[0])
    grad_normed = total(in_own, received_in, in_near)
    own = x_own.astype(f32)
    own_average, own_inverse = statistics(own)
    own_normed = (own - own_average) * own_inverse
    grad_hidden = g_own.astype(f32) + own_inverse * (
        grad_normed
        - jnp.mean(grad_normed, axis=1, keepdims=True)
        - own_normed * jnp.mean(grad_normed * own_normed, axis=1, keepdims=True)
    )
    return (
        output.reshape(seq_count, sub_len, D),
        grad_hidden.reshape(seq_count, sub_len, D),
        small[0],
        small[1],
        small[2],
        small[3],
        qkv_grad,
        small[5 : 5 + nq].reshape(-1),
        dense_grad,
        up_grad,
        small[5 + nq :].reshape(-1),
        down_grad,
        small[4],
    )


def solution(mesh):
    dp, blk, hd = (mesh.shape[name] for name in ("dp", "blk", "hd"))
    low = HEADS // hd
    inner = Mesh(mesh.devices.reshape(dp, blk // low, low, hd), ALL)
    token = P("dp", ("bh", "bl", "hd"), None)
    vector = P(ALL)
    matrix = P(ALL, None)
    return jax.shard_map(
        per_device,
        mesh=inner,
        in_specs=(
            token, vector, vector, vector, vector, matrix, vector,
            matrix, matrix, vector, matrix, vector, token,
        ),
        out_specs=(
            token, token, vector, vector, vector, vector, matrix, vector,
            matrix, matrix, vector, matrix, vector,
        ),
        check_vma=False,
    )
```

```python
import functools

import jax
import jax.numpy as jnp
from jax import lax
from jax.experimental import pallas as pl
from jax.experimental.pallas import tpu as pltpu
from jax.sharding import Mesh, PartitionSpec as P

D = 2048
HEADS = 8
HS = 256
ROT = 64

TP = ("bl", "hd")
RP = ("dp", "bh")
ALL = ("dp", "bh", "bl", "hd")

epsilon = 1e-05
contract_last = (((1,), (1,)), ((), ()))
f32 = jnp.float32
bf16 = jnp.bfloat16


def rotary_tables(positions):
    half_rot = ROT // 2
    frequency = 10000.0 ** (-(2.0 * jnp.arange(half_rot, dtype=f32)) / ROT)
    angles = positions[:, None] * frequency[None, :]
    cosine, sine = jnp.cos(angles), jnp.sin(angles)
    none = jnp.zeros_like(sine)
    rest = jnp.ones((positions.shape[0], 128 - ROT), f32)
    return (
        jnp.concatenate([cosine, cosine, rest], axis=1),
        jnp.concatenate([-sine, none, 0.0 * rest], axis=1),
        jnp.concatenate([none, sine, 0.0 * rest], axis=1),
    )


def mm(a, b):
    return jnp.dot(a, b, preferred_element_type=f32)


def mm_nt(a, b):
    return lax.dot_general(a, b, contract_last, preferred_element_type=f32)


class Order:
    def __init__(self, token):
        self.token = token

    def join(self, *values):
        self.token, values = lax.optimization_barrier((self.token, values))
        return values


def swap(value, axis, distance):
    size = lax.axis_size(axis)
    return lax.ppermute(value, axis, [(i, i ^ distance) for i in range(size)])


def gather_axis(value, axis):
    return [value] + [swap(value, axis, d) for d in range(1, lax.axis_size(axis))]


def gather_start(value):
    size = lax.axis_size("hd")
    return [swap(value, "hd", d) for d in range(1, 3 if size == 4 else size)]


def gather_end(value, near):
    if lax.axis_size("hd") == 4:
        near = [near[0], near[1], swap(near[1], "hd", 1)]
    return [value] + near


def gather_rest(value):
    place, size = lax.axis_index(RP), lax.axis_size(RP)
    blocks = jnp.stack([value] + [swap(value, RP, d) for d in range(1, size)])
    bit = 1
    while bit < size:
        pairs = blocks.reshape((size // (2 * bit), 2, bit) + value.shape)
        turned = jnp.stack([pairs[:, 1], pairs[:, 0]], axis=1).reshape(blocks.shape)
        blocks = jnp.where((place & bit) != 0, turned, blocks)
        bit *= 2
    return blocks


def hand_on(value, distance):
    if lax.axis_size("hd") == 4 and distance == 3:
        distance = 1
    return swap(value, "hd", distance)


def exchange(terms, axis, dim):
    place, size = lax.axis_index(axis), lax.axis_size(axis)
    pick = lambda d: lax.dynamic_index_in_dim(terms, place ^ d, dim, keepdims=False)
    return [pick(0)] + [swap(pick(d), axis, d) for d in range(1, size)]


def spread_group(shard):
    mine = lax.all_to_all(shard, TP, split_axis=0, concat_axis=0, tiled=True)
    return mine.reshape(-1, shard.shape[2])


def spread_rest(mine):
    return lax.all_gather(mine, RP, axis=0, tiled=True)


def collect_rest(terms):
    return lax.psum_scatter(terms, RP, scatter_dimension=0, tiled=True)


def collect_group(mine):
    mine = mine.reshape(lax.axis_size(TP), -1, mine.shape[1])
    return lax.all_to_all(mine, TP, split_axis=0, concat_axis=0, tiled=True)


TILE = 256
KEYS = 2048


def call(kernel, outs, *ins, scratch=(), grid=(), in_specs=None, out_specs=None):
    vmem = pl.BlockSpec(memory_space=pltpu.VMEM)
    return pl.pallas_call(
        kernel,
        grid=grid,
        out_shape=[jax.ShapeDtypeStruct(shape, dtype) for shape, dtype in outs],
        in_specs=in_specs or [vmem] * len(ins),
        out_specs=out_specs or [vmem] * len(outs),
        scratch_shapes=list(scratch),
        compiler_params=pltpu.CompilerParams(vmem_limit_bytes=58 * 2**20),
        cost_estimate=pl.CostEstimate(flops=1, bytes_accessed=1, transcendentals=0),
    )(*ins)


def tiles(count, step):
    def body(i, _):
        step(pl.ds(pl.multiple_of(i * TILE, TILE), TILE))
        return 0

    lax.fori_loop(0, count // TILE, body, 0)


def add(*groups):
    return [
        [sum((x.astype(f32) for x in arrays[1:]), arrays[0].astype(f32)).astype(dtype)]
        for arrays, dtype, _ in groups
    ]


def turn(value, tables, sign):
    own, above, below = tables
    first = value[:, :128]
    turned = first * own + sign * (
        pltpu.roll(first, 96, 1) * above + pltpu.roll(first, 32, 1) * below
    )
    return jnp.concatenate([turned, value[:, 128:]], axis=1)


def statistics(block):
    average = jnp.mean(block, axis=1, keepdims=True)
    centered = block - average
    return average, lax.rsqrt(jnp.mean(centered * centered, axis=1, keepdims=True) + epsilon)


def project_kernel(count, *refs):
    x_refs, refs = refs[:count], refs[count:]
    vec_ref, w_ref, b_ref, own_ref, above_ref, below_ref, *refs = refs
    attn_ref, mlp_ref, q_ref, kv_ref, average_ref, inverse_ref = refs
    rows = x_refs[0].shape[0]
    for start in range(0, count * rows, TILE):
        for i in range(start // rows, (start + TILE) // rows):
            at = slice(i * rows, (i + 1) * rows)
            block = x_refs[i][...].astype(f32)
            average, inverse = statistics(block)
            average_ref[at, :] = average
            inverse_ref[at, :] = inverse
            normed = (block - average) * inverse
            attn_ref[at, :] = (normed * vec_ref[0:1, :] + vec_ref[1:2, :]).astype(bf16)
            mlp_ref[at, :] = (normed * vec_ref[2:3, :] + vec_ref[3:4, :]).astype(bf16)
        at = slice(start, start + TILE)
        project = mm(attn_ref[at, :], w_ref[...]) + b_ref[...]
        tables = own_ref[at, :], above_ref[at, :], below_ref[at, :]
        query = turn(project[:, :HS], tables, 1.0).astype(bf16)
        q_ref[at, :] = (query.astype(f32) * HS**-0.5).astype(bf16)
        kv_ref[at, :HS] = turn(project[:, HS : 2 * HS], tables, 1.0).astype(bf16)
        kv_ref[at, HS:] = project[:, 2 * HS :].astype(bf16)


def cotangent_kernel(count, *refs):
    g_refs, (w_ref, g_ref, out_ref) = refs[:count], refs[count:]
    rows = g_refs[0].shape[0]
    for i in range(count):
        g_ref[i * rows : (i + 1) * rows, :] = g_refs[i][...]

    def step(at):
        out_ref[at, :] = mm(g_ref[at, :], w_ref[...]).astype(bf16)

    tiles(g_ref.shape[0], step)


def forward_kernel(mlp_ref, w_ref, b_ref, act_ref, slope_ref):
    def step(at):
        value = mm(mlp_ref[at, :], w_ref[...]) + b_ref[...]
        cdf = 0.5 * (1.0 + lax.erf(value * 0.7071067811865476))
        density = jnp.exp(-0.5 * value * value) * 0.3989422804014327
        act_ref[at, :] = (value * cdf).astype(bf16)
        slope_ref[at, :] = cdf + value * density

    tiles(mlp_ref.shape[0], step)


def forward(mlp_in, w_up, b_up):
    count, ffl = mlp_in.shape[0], w_up.shape[1]
    columns = pl.BlockSpec((count, TILE), lambda i: (0, i))
    return call(
        forward_kernel,
        [((count, ffl), bf16), ((count, ffl), f32)],
        mlp_in, w_up, b_up,
        grid=(ffl // TILE,),
        in_specs=[
            pl.BlockSpec((count, D), lambda i: (0, 0)),
            pl.BlockSpec((D, TILE), lambda i: (0, i)),
            pl.BlockSpec((1, TILE), lambda i: (0, i)),
        ],
        out_specs=[columns, columns],
    )


def backward_kernel(g_ref, w_ref, slope_ref, out_ref, sum_ref):
    grad = (mm(g_ref[...], w_ref[...]) * slope_ref[...]).astype(bf16)
    out_ref[...] = grad
    sum_ref[...] = jnp.sum(grad.astype(f32), axis=0, keepdims=True)


def backward(g_all, w_down, slope):
    count, ffl = slope.shape
    columns = pl.BlockSpec((count, TILE), lambda i: (0, i))
    return call(
        backward_kernel,
        [((count, ffl), bf16), ((1, ffl), f32)],
        g_all, w_down, slope,
        grid=(ffl // TILE,),
        in_specs=[
            pl.BlockSpec((count, D), lambda i: (0, 0)),
            pl.BlockSpec((D, TILE), lambda i: (0, i)),
            columns,
        ],
        out_specs=[columns, pl.BlockSpec((1, TILE), lambda i: (0, i))],
    )


def weight_kernel(*refs):
    pairs, out_ref = refs[:-1], refs[-1]
    start = 0
    for lhs_ref, rhs_ref in zip(pairs[::2], pairs[1::2]):
        cols = slice(start, start + rhs_ref.shape[1])
        start += rhs_ref.shape[1]
        out_ref[:, cols] = mm(lhs_ref[...].T, rhs_ref[...]).astype(bf16)


def weight_terms(*pairs):
    count = pairs[0].shape[0]
    cols = sum(rhs.shape[1] for rhs in pairs[1::2])
    specs = []
    for rhs in pairs[1::2]:
        specs.append(pl.BlockSpec((count, 2 * TILE), lambda i: (0, i)))
        specs.append(pl.BlockSpec(rhs.shape, lambda i: (0, 0)))
    return call(
        weight_kernel,
        [((D, cols), bf16)],
        *pairs,
        grid=(D // (2 * TILE),),
        in_specs=specs,
        out_specs=[pl.BlockSpec((2 * TILE, cols), lambda i: (i, 0))],
    )[0]


def weight_half_kernel(per, place_ref, lhs_ref, rhs_ref, *out_refs):
    term = mm(lhs_ref[...].T, rhs_ref[...]).astype(bf16)
    for d, out_ref in enumerate(out_refs):

        @pl.when(pl.program_id(0) // per == d)
        def _(out_ref=out_ref):
            out_ref[...] = term


def weight_half(lhs, rhs, other):
    bh = lax.axis_size("bh")
    part = D // (2 * bh)
    tile = min(TILE, part)
    per = part // tile
    place = jnp.stack([lax.axis_index("dp") ^ other, lax.axis_index("bh")]).astype(jnp.int32)
    count, cols = rhs.shape

    def lhs_at(i, place_ref):
        return (0, (place_ref[0] * bh + (place_ref[1] ^ (i // per))) * per + i % per)

    def out_at(d):
        return lambda i, place_ref: (jnp.clip(i - d * per, 0, per - 1), 0)

    return pl.pallas_call(
        functools.partial(weight_half_kernel, per),
        grid_spec=pltpu.PrefetchScalarGridSpec(
            num_scalar_prefetch=1,
            grid=(bh * per,),
            in_specs=[
                pl.BlockSpec((count, tile), lhs_at),
                pl.BlockSpec((count, cols), lambda i, place_ref: (0, 0)),
            ],
            out_specs=[pl.BlockSpec((tile, cols), out_at(d)) for d in range(bh)],
        ),
        out_shape=[jax.ShapeDtypeStruct((part, cols), bf16)] * bh,
        compiler_params=pltpu.CompilerParams(vmem_limit_bytes=58 * 2**20),
        cost_estimate=pl.CostEstimate(flops=1, bytes_accessed=1, transcendentals=0),
    )(place, lhs, rhs)


def output_kernel(att_ref, act_ref, dense_ref, down_ref, *out_refs):
    term = mm_nt(att_ref[...], dense_ref[...]) + mm_nt(act_ref[...], down_ref[...])
    rows = out_refs[0].shape[0]
    for i, out_ref in enumerate(out_refs):
        out_ref[...] = term[i * rows : (i + 1) * rows].astype(out_ref.dtype)


def output_terms(attended, activated, w_heads, w_down, part, count, rows, dtype):
    ffl, wide = activated.shape[1], 4 * TILE if count * rows <= 512 else 2 * TILE
    return call(
        output_kernel,
        [((rows, D), dtype)] * count,
        attended, activated, w_heads, w_down,
        grid=(D // wide,),
        in_specs=[
            pl.BlockSpec((count * rows, HS), lambda i: (part, 0)),
            pl.BlockSpec((count * rows, ffl), lambda i: (part, 0)),
            pl.BlockSpec((wide, HS), lambda i: (i, 3)),
            pl.BlockSpec((wide, ffl), lambda i: (i, 0)),
        ],
        out_specs=[pl.BlockSpec((rows, wide), lambda i: (0, i))] * count,
    )


def turn_back_kernel(count, *refs):
    dq_ref, refs = refs[0], refs[1:]
    term_refs, (own_ref, above_ref, below_ref, out_ref, sum_ref) = refs[:count], refs[count:]
    sum_ref[...] = jnp.zeros_like(sum_ref)

    def step(at):
        tables = own_ref[at, :], above_ref[at, :], below_ref[at, :]
        grad = term_refs[0][at, :].astype(f32)
        for ref in term_refs[1:]:
            grad += ref[at, :].astype(f32)
        grad = grad.astype(bf16)
        out_ref[at, :HS] = turn(dq_ref[at, :].astype(f32), tables, -1.0).astype(bf16)
        out_ref[at, HS : 2 * HS] = turn(grad[:, :HS].astype(f32), tables, -1.0).astype(bf16)
        out_ref[at, 2 * HS :] = grad[:, HS:]
        sum_ref[...] += jnp.sum(out_ref[at, :].astype(f32), axis=0, keepdims=True)

    tiles(dq_ref.shape[0], step)


def input_kernel(count, *refs):
    x_refs, refs = refs[:count], refs[count:]
    average_ref, inverse_ref, gp_ref, gu_ref, heads_ref, up_ref, vec_ref = refs[:7]
    out_refs, sum_ref = refs[7:-1], refs[-1]
    rows = x_refs[0].shape[0]
    sums = [0.0] * 4
    for start in range(0, count * rows, TILE):
        at = slice(start, start + TILE)
        attn = mm_nt(gp_ref[at, :], heads_ref[...])
        mlp = mm_nt(gu_ref[at, :], up_ref[...])
        block = jnp.concatenate(
            [x_refs[i][...].astype(f32) for i in range(start // rows, (start + TILE) // rows)],
            axis=0,
        )
        normed = (block - average_ref[at, :]) * inverse_ref[at, :]
        for i, term in enumerate((attn * normed, attn, mlp * normed, mlp)):
            sums[i] = sums[i] + jnp.sum(term, axis=0, keepdims=True)
        out = attn * vec_ref[0:1, :] + mlp * vec_ref[2:3, :]
        for i in range(0, TILE, rows):
            out_ref = out_refs[(start + i) // rows]
            out_ref[...] = out[i : i + rows].astype(out_ref.dtype)
    sum_ref[...] = jnp.concatenate(sums, axis=0)


def input_terms(x_blocks, average, inverse, grad_project, grad_pre_up, w_heads, w_up, vectors, own):
    count, ffl = grad_pre_up.shape
    whole = lambda rows, cols: pl.BlockSpec((rows, cols), lambda i: (0, 0))
    block = pl.BlockSpec((x_blocks[0].shape[0], TILE), lambda i: (0, i))
    *terms, sums = call(
        functools.partial(input_kernel, len(x_blocks)),
        [(x.shape, f32 if i < own else bf16) for i, x in enumerate(x_blocks)] + [((4, D), f32)],
        *x_blocks, average, inverse, grad_project, grad_pre_up, w_heads, w_up, vectors,
        grid=(D // TILE,),
        in_specs=[
            *[block] * len(x_blocks),
            whole(count, 1),
            whole(count, 1),
            whole(count, 3 * HS),
            whole(count, ffl),
            pl.BlockSpec((TILE, 3 * HS), lambda i: (i, 0)),
            pl.BlockSpec((TILE, ffl), lambda i: (i, 0)),
            pl.BlockSpec((vectors.shape[0], TILE), lambda i: (0, i)),
        ],
        out_specs=[*[block] * len(x_blocks), pl.BlockSpec((4, TILE), lambda i: (0, i))],
    )
    return terms, sums


def places(block, start, shape, dim, sizes, t):
    rows, tp = sizes
    index = start + lax.broadcasted_iota(jnp.int32, shape, dim)
    device = index // rows
    block = block ^ (device // tp)
    return (block * tp + (t ^ (device % tp))) * rows + index % rows


def attention_kernel(count, sizes, place_ref, q_ref, g_ref, *refs):
    kv_refs, (o_ref, dq_ref), refs = refs[:count], refs[count : count + 2], refs[count + 2 :]
    dkv_refs, sum_ref = refs[:-1], refs[-1]
    t, block, tile = place_ref[0], place_ref[1], 2 * TILE
    keys = jnp.concatenate([ref[:, :HS] for ref in kv_refs], axis=0)
    values = jnp.concatenate([ref[:, HS:] for ref in kv_refs], axis=0)
    keys_turned = keys.T
    values_turned = values.T
    key_places = places(block, 0, (keys.shape[0], 1), 0, sizes, t)
    sum_ref[...] = jnp.zeros_like(sum_ref)
    for start in range(0, q_ref.shape[0], tile):
        at = slice(start, start + tile)
        query = q_ref[at, :]
        grad = g_ref[at, :]
        visible = key_places <= places(block, start, (1, tile), 1, sizes, t)
        scores = jnp.where(visible, mm_nt(keys, query), -1e30)
        weights = jnp.exp(scores - jnp.max(scores, axis=0, keepdims=True))
        weights = weights * (1.0 / jnp.sum(weights, axis=0, keepdims=True))
        weights_low = weights.astype(bf16)
        result = mm(values_turned, weights_low)
        o_ref[at, :] = result.T.astype(bf16)
        sum_ref[:, HS:] += mm(weights_low, grad)
        delta = jnp.sum(result * grad.T.astype(f32), axis=0, keepdims=True)
        score_grad = (weights * (mm_nt(values, grad) - delta)).astype(bf16)
        dq_ref[at, :] = (mm(keys_turned, score_grad).T * (HS**-0.5)).astype(bf16)
        sum_ref[:, :HS] += mm(score_grad, query)
    start = 0
    for ref in dkv_refs:
        ref[...] = sum_ref[start : start + ref.shape[0], :].astype(bf16)
        start += ref.shape[0]


def long_attention_kernel(sizes, place_ref, q_ref, g_ref, kv_ref, o_ref, dq_ref, dkv_ref, sum_ref):
    blocks = kv_ref.shape[0] // KEYS
    t, block = place_ref[0], place_ref[1]
    sum_ref[...] = jnp.zeros_like(sum_ref)

    def step(at):
        query = q_ref[at, :]
        grad = g_ref[at, :]
        query_places = places(block, at.start, (1, TILE), 1, sizes, t)

        def scores_of(j):
            here = pl.ds(pl.multiple_of(j * KEYS, KEYS), KEYS)
            visible = places(block, j * KEYS, (KEYS, 1), 0, sizes, t) <= query_places
            return here, jnp.where(visible, mm_nt(kv_ref[here, :HS], query), -1e30)

        def first(j, state):
            top, total = state
            _, scores = scores_of(j)
            higher = jnp.maximum(top, jnp.max(scores, axis=0, keepdims=True))
            now = jnp.sum(jnp.exp(scores - higher), axis=0, keepdims=True)
            return higher, total * jnp.exp(top - higher) + now

        row = (1, TILE)
        top, total = lax.fori_loop(
            0, blocks, first, (jnp.full(row, -1e30, f32), jnp.zeros(row, f32))
        )
        inverse = 1.0 / total

        def second(j, result):
            here, scores = scores_of(j)
            weights = jnp.exp(scores - top) * inverse
            return result + mm(kv_ref[here, HS:].T, weights.astype(bf16))

        result = lax.fori_loop(0, blocks, second, jnp.zeros((HS, TILE), f32))
        o_ref[at, :] = result.T.astype(bf16)
        delta = jnp.sum(result * grad.T.astype(f32), axis=0, keepdims=True)

        def third(j, result):
            here, scores = scores_of(j)
            weights = jnp.exp(scores - top) * inverse
            weight_grad = mm_nt(kv_ref[here, HS:], grad)
            score_grad = (weights * (weight_grad - delta)).astype(bf16)
            sum_ref[here, HS:] += mm(weights.astype(bf16), grad)
            sum_ref[here, :HS] += mm(score_grad, query)
            return result + mm(kv_ref[here, :HS].T, score_grad)

        result = lax.fori_loop(0, blocks, third, jnp.zeros((HS, TILE), f32))
        dq_ref[at, :] = (result.T * (HS**-0.5)).astype(bf16)

    tiles(q_ref.shape[0], step)
    dkv_ref[...] = sum_ref[...].astype(bf16)


def attention(query, grad, kv_blocks, sizes):
    place = jnp.stack([lax.axis_index(TP), lax.axis_index("bh")]).astype(jnp.int32)
    count, total = len(kv_blocks), sum(block.shape[0] for block in kv_blocks)
    low = (query.shape, bf16)
    scratch = [pltpu.VMEM((total, 2 * HS), f32)]
    vmem = pl.BlockSpec(memory_space=pltpu.VMEM)
    smem = pl.BlockSpec(memory_space=pltpu.SMEM)
    if total <= KEYS:
        attended, grad_query, *grad_kv = call(
            functools.partial(attention_kernel, count, sizes),
            [low, low] + [(block.shape, bf16) for block in kv_blocks],
            place, query, grad, *kv_blocks,
            scratch=scratch,
            in_specs=[smem] + [vmem] * (2 + count),
        )
        return attended, grad_query, grad_kv
    kv_all = jnp.concatenate(kv_blocks, axis=0)
    attended, grad_query, grad_kv = call(
        functools.partial(long_attention_kernel, sizes),
        [low, low, (kv_all.shape, bf16)],
        place, query, grad, kv_all,
        scratch=scratch,
        in_specs=[smem] + [vmem] * 3,
    )
    return attended, grad_query, jnp.split(grad_kv, count, axis=0)


def per_device(
    hidden_in,
    gain_attn,
    shift_attn,
    gain_mlp,
    shift_mlp,
    qkv_weight,
    qkv_bias,
    dense_weight,
    up_weight,
    up_bias,
    down_weight,
    out_bias,
    cotangent,
):
    seq_count, sub_len, _ = hidden_in.shape
    tp, rp = lax.axis_size(TP), lax.axis_size(RP)
    n_dev = lax.axis_size(ALL)
    t = lax.axis_index(TP)
    bh, bh_size, bl_size = lax.axis_index("bh"), lax.axis_size("bh"), lax.axis_size("bl")
    rows = qkv_weight.shape[0]
    ff = up_weight.shape[1]
    ffl = ff // tp
    group_len = sub_len * tp

    vmem = pl.BlockSpec(memory_space=pltpu.VMEM)
    x_own = hidden_in.reshape(sub_len, D)
    join = Order(out_bias).join
    g_own = cotangent.reshape(sub_len, D)
    smalls = jnp.concatenate(
        [
            vector.reshape(-1, rows)
            for vector in (
                gain_attn, shift_attn, gain_mlp, shift_mlp, out_bias, qkv_bias, up_bias
            )
        ],
        axis=0,
    )
    kinds = smalls.shape[0]
    count = kinds * rows
    smalls = jnp.pad(smalls.reshape(1, count), ((0, 7), (0, 4 * HS - count)))
    heads_own = jnp.concatenate(
        [
            qkv_weight.reshape(rows, 3, HEADS, HS).transpose(2, 0, 1, 3).reshape(HEADS, rows, 3 * HS),
            dense_weight.reshape(rows, HEADS, HS).transpose(1, 0, 2),
        ],
        axis=2,
    )
    heads_own = jnp.concatenate(
        [heads_own, jnp.broadcast_to(smalls[None], (tp,) + smalls.shape)], axis=1
    )
    up_own = up_weight.reshape(rows, tp, ffl).transpose(1, 0, 2)
    down_own = down_weight.reshape(rows, tp, ffl).transpose(1, 0, 2)

    x_near = gather_start(x_own)
    x_side = gather_axis(x_own, "bl")
    g_side = gather_axis(g_own, "bl")
    x_near, x_side, g_side, heads_own, up_own, down_own = join(
        x_near, x_side, g_side, heads_own, up_own, down_own
    )
    m_heads = lax.all_to_all(heads_own, TP, split_axis=0, concat_axis=0, tiled=True)
    x_rows = [x_side, gather_axis(x_near[0], "bl")]
    x_second = x_near[1]
    x_left = gather_axis(x_second[: sub_len // 2], "bl")[1:]
    x_near = gather_end(x_own, x_near)
    row = jnp.arange(group_len, dtype=jnp.int32)
    inside = ((row // sub_len) ^ t) * sub_len + row % sub_len
    query_places = bh * group_len + inside
    tables = rotary_tables(query_places.astype(f32))
    x_near, x_rows, x_left, m_heads, up_own, g_late, tables, down_own, x_second = join(
        x_near, x_rows, x_left, m_heads, up_own, g_own, tables, down_own, x_second
    )
    x_right = gather_axis(x_second[sub_len // 2 :], "bl")[1:]
    w_heads = spread_rest(m_heads[:, :rows].reshape(tp * rows, -1))
    x_rows += [None] + [gather_axis(block, "bl") for block in x_near[3:]]
    g_first = swap(g_late, "hd", 1)
    m_up = spread_group(up_own)
    smalls = gather_rest(m_heads[:, rows, :count]).reshape(n_dev, kinds, rows).astype(f32)
    vectors = smalls[:, :5].transpose(1, 0, 2).reshape(5, D)
    nq = qkv_bias.shape[0] // rows
    b_qkv = smalls[:, 5 : 5 + nq].reshape(3, HEADS, HS)
    b_up = smalls[:, 5 + nq :].reshape(tp, ffl)
    b_qkv = lax.dynamic_index_in_dim(b_qkv, t, 1, keepdims=False).reshape(1, 3 * HS)
    b_up = lax.dynamic_index_in_dim(b_up, t, 0, keepdims=True)

    x_rows, x_right, g_first, m_up, g_late, down_own, vectors, b_qkv, b_up = join(
        x_rows, x_right, g_first, m_up, g_late, down_own, vectors, b_qkv, b_up
    )
    x_rows[2] = [x_second] + [
        jnp.concatenate(halves, axis=0) for halves in zip(x_left, x_right)
    ]
    w_up = spread_rest(m_up)
    x_blocks = [row[far] for far in range(bl_size) for row in x_rows]
    g_rows = [g_side, gather_axis(g_first, "bl")]
    hd_size = lax.axis_size("hd")
    four = hd_size == 4
    g_near = [g_first] + [swap(g_late, "hd", d) for d in range(2, 3 if hd_size == 4 else hd_size)]
    attn_in, mlp_in, query, kv, average, inverse = call(
        functools.partial(project_kernel, tp),
        [
            ((group_len, D), bf16),
            ((group_len, D), bf16),
            ((group_len, HS), bf16),
            ((group_len, 2 * HS), bf16),
            ((group_len, 1), f32),
            ((group_len, 1), f32),
        ],
        *x_blocks, vectors, w_heads, b_qkv, *tables,
        grid=(1,),
        in_specs=[vmem] * (tp + 1) + [pl.BlockSpec((D, 3 * HS), lambda i: (0, 0))] + [vmem] * 4,
    )
    g_rows, g_near, kv, mlp_in, g_late, down_own = join(
        g_rows, g_near, kv, mlp_in, g_late, down_own
    )
    g_near = gather_end(g_late, g_near)
    g_rows += [gather_axis(block, "bl") for block in g_near[2:3]]
    g_rows, g_near, down_own, mlp_in = join(g_rows, g_near, down_own, mlp_in)
    g_rows += [gather_axis(block, "bl") for block in g_near[3:]]
    kv_blocks = gather_axis(kv, "bh")
    m_down = spread_group(down_own)
    activated, slope = forward(mlp_in, w_up, b_up)
    g_rows, kv_blocks, m_down, activated, slope = join(g_rows, kv_blocks, m_down, activated, slope)
    w_down = spread_rest(m_down)
    g_blocks = [row[far] for far in range(bl_size) for row in g_rows]
    g_all, grad_att = call(
        functools.partial(cotangent_kernel, tp),
        [((group_len, D), bf16), ((group_len, HS), bf16)],
        *g_blocks, w_heads,
        grid=(1,),
        in_specs=[vmem] * tp + [pl.BlockSpec((D, HS), lambda i: (0, 3))],
    )
    down_far = weight_half(g_all, activated, 1)
    down_far, grad_att, g_all = join(down_far, grad_att, g_all)
    down_far = [swap(terms, "dp", 1) for terms in reversed(down_far)][::-1]
    down_own = weight_half(g_all, activated, 0)
    down_far, down_own, grad_att = join(down_far, down_own, grad_att)
    down_sent = add(*[([down_far[d], down_own[d]], bf16, 1) for d in range(1, bh_size)])
    down_sent, grad_att = join(down_sent, grad_att)
    down_others = [swap(sent[0], "bh", d + 1) for d, sent in enumerate(down_sent)]
    attended, grad_query, grad_kv = attention(query, grad_att, kv_blocks, (sub_len, tp))
    hd_terms = (hd_size, sub_len)
    out_far = [
        output_terms(attended, activated, w_heads, w_down, far, *hd_terms, bf16)
        for far in range(1, bl_size)
    ]
    out_own = output_terms(attended, activated, w_heads, w_down, 0, *hd_terms, f32)
    down_others, out_far, attended, slope, out_own = join(
        down_others, out_far, attended, slope, out_own
    )
    part = hd_size // 4
    parts = [range(hd_size - (g + 1) * part, hd_size - g * part) for g in range(4)]

    def over_bl(terms, ds):
        return {d: [swap(term[d], "bl", f + 1) for f, term in enumerate(terms)] for d in ds}

    def sums_of(own, received, ds, handed=()):
        return [
            ([own[d], *received[d], *(handed if d == 2 else ())], f32 if d == 0 else bf16, 1)
            for d in ds
        ]

    ((down_last,),) = add(([down_far[0], down_own[0], *down_others], bf16, 1))
    down_last, attended, slope = join(down_last, attended, slope)
    kv_others = [swap(grad_kv[d], "bh", d) for d in range(1, bh_size)]
    down_grad = collect_group(down_last)
    received = over_bl(out_far, parts[0])
    grad_pre_up, up_bias_term = backward(g_all, w_down, slope)
    up_terms = weight_terms(mlp_in, grad_pre_up)
    kv_others, down_grad, received, grad_pre_up, out_far, up_terms = join(
        kv_others, down_grad, received, grad_pre_up, out_far, up_terms
    )
    up_mine = collect_rest(up_terms)
    out = dict(zip(parts[0], add(*sums_of(out_own, received, parts[0]))))
    out, kv_others = join(out, kv_others)
    out_near = {d: hand_on(out[d][0], d) for d in parts[0]}
    middle = [*parts[1], *parts[2]]
    received = over_bl(out_far, middle)
    grad_project, qkv_bias_term = call(
        functools.partial(turn_back_kernel, bh_size),
        [((group_len, 3 * HS), bf16), ((1, 3 * HS), f32)],
        grad_query, grad_kv[0], *kv_others, *tables,
    )
    in_terms, sums = input_terms(
        x_blocks, average, inverse, grad_project, grad_pre_up, w_heads, w_up, vectors, hd_size
    )
    in_own = in_terms[:hd_size]
    in_far = [in_terms[f * hd_size : (f + 1) * hd_size] for f in range(1, bl_size)]
    out_near, received, out_far, in_far, grad_project = join(
        out_near, received, out_far, in_far, grad_project
    )
    out = add(*sums_of(out_own, received, middle, [out_near[3]] if four else []))
    out, in_far, grad_project = join(out, in_far, grad_project)
    out_near |= {d: hand_on(term, d) for d, (term,) in zip(middle, out)}
    received = over_bl(out_far, parts[3])
    received_in = over_bl(in_far, parts[0])
    heads_terms = weight_terms(attn_in, grad_project, g_all, attended)
    sums = jnp.concatenate([sums, jnp.sum(g_own.astype(f32), axis=0, keepdims=True)], axis=0)
    qkv_bias_full = lax.dynamic_update_slice(
        jnp.zeros((3, HEADS, HS), f32), qkv_bias_term.reshape(3, 1, HS), (0, t, 0)
    )
    up_bias_full = lax.dynamic_update_slice(jnp.zeros((tp, ffl), f32), up_bias_term, (t, 0))
    small_terms = jnp.concatenate(
        [
            sums.reshape(5, n_dev, rows).transpose(1, 0, 2),
            qkv_bias_full.reshape(n_dev, nq, rows),
            up_bias_full.reshape(n_dev, -1, rows),
        ],
        axis=1,
    )
    out_near, received, received_in, heads_terms, up_mine, in_far, small = join(
        out_near, received, received_in, heads_terms, up_mine, in_far, small_terms
    )
    heads_mine = collect_rest(heads_terms)
    ins = add(*sums_of(in_own, received_in, parts[0]))
    ins, up_mine, in_far = join(ins, up_mine, in_far)
    up_grad = collect_group(up_mine)
    in_near = {d: hand_on(term, d) for d, (term,) in zip(parts[0], ins)}
    received_in = over_bl(in_far, middle)
    small = exchange(small.reshape(rp, bl_size, hd_size, kinds, rows), RP, 0)
    up_grad, in_near, received_in, small, in_far = join(
        up_grad, in_near, received_in, small, in_far
    )
    ins = add(*sums_of(in_own, received_in, middle, [in_near[3]] if four else []))
    in_far, heads_mine, small = join(in_far, heads_mine, small)
    heads_grad = collect_group(heads_mine)
    received_in = over_bl(in_far, parts[3])
    down_grad = down_grad.astype(f32).transpose(1, 0, 2).reshape(rows, ff)
    up_grad = up_grad.astype(f32).transpose(1, 0, 2).reshape(rows, ff)
    small = exchange(sum(small[1:], small[0]), "hd", 1)
    heads_grad, received_in, down_grad, up_grad, ins, small = join(
        heads_grad, received_in, down_grad, up_grad, ins, small
    )
    in_near |= {d: hand_on(term, d) for d, (term,) in zip(middle, ins)}
    small = exchange(sum(small[1:], small[0]), "bl", 0)
    heads_grad = heads_grad.astype(f32)
    dense_grad = heads_grad[:, :, 3 * HS :].transpose(1, 0, 2).reshape(rows, D)
    qkv_grad = (
        heads_grad[:, :, : 3 * HS]
        .reshape(tp, rows, 3, HS)
        .transpose(1, 2, 0, 3)
        .reshape(rows, 3 * D)
    )

    def total(own, received, near):
        rest = {d: sum((x.astype(f32) for x in received[d]), own[d]) for d in received}
        near = near | {d: hand_on(rest[d].astype(bf16), d) for d in rest if d}
        straight = [d for d in range(1, hd_size) if not (four and d == 3)]
        return sum((near[d].astype(f32) for d in straight), rest[0])

    projected = total(out_own, received, out_near)
    output = (x_own.astype(f32) + projected + vectors[4:5]).astype(bf16)
    small = sum(small[1:], small[0])
    smalls = [small[i] for i in range(5)]
    smalls += [small[5 : 5 + nq].reshape(-1), small[5 + nq :].reshape(-1)]
    in_near, received_in, smalls, dense_grad, qkv_grad, output, in_own = join(
        in_near, received_in, smalls, dense_grad, qkv_grad, output, in_own
    )
    grad_normed = total(in_own, received_in, in_near)
    own = x_own.astype(f32)
    own_average, own_inverse = statistics(own)
    own_normed = (own - own_average) * own_inverse
    grad_hidden = g_own.astype(f32) + own_inverse * (
        grad_normed
        - jnp.mean(grad_normed, axis=1, keepdims=True)
        - own_normed * jnp.mean(grad_normed * own_normed, axis=1, keepdims=True)
    )
    return (
        output.reshape(seq_count, sub_len, D),
        grad_hidden.reshape(seq_count, sub_len, D),
        *smalls[:4],
        qkv_grad,
        smalls[5],
        dense_grad,
        up_grad,
        smalls[6],
        down_grad,
        smalls[4],
    )


def solution(mesh):
    dp, blk, hd = (mesh.shape[name] for name in ("dp", "blk", "hd"))
    low = HEADS // hd
    inner = Mesh(mesh.devices.reshape(dp, blk // low, low, hd), ALL)
    token = P("dp", ("bh", "bl", "hd"), None)
    vector = P(ALL)
    matrix = P(ALL, None)
    return jax.shard_map(
        per_device,
        mesh=inner,
        in_specs=(
            token, vector, vector, vector, vector, matrix, vector,
            matrix, matrix, vector, matrix, vector, token,
        ),
        out_specs=(
            token, token, vector, vector, vector, vector, matrix, vector,
            matrix, matrix, vector, matrix, vector,
        ),
        check_vma=False,
    )
```

```python
import functools

import jax
import jax.numpy as jnp
from jax import lax
from jax.experimental import pallas as pl
from jax.experimental.pallas import tpu as pltpu
from jax.sharding import Mesh, PartitionSpec as P

D = 2048
HEADS = 8
HS = 256
ROT = 64

TP = ("bl", "hd")
RP = ("dp", "bh")
ALL = ("dp", "bh", "bl", "hd")

epsilon = 1e-05
contract_last = (((1,), (1,)), ((), ()))
f32 = jnp.float32
bf16 = jnp.bfloat16


def rotary_tables(positions):
    half_rot = ROT // 2
    frequency = 10000.0 ** (-(2.0 * jnp.arange(half_rot, dtype=f32)) / ROT)
    angles = positions[:, None] * frequency[None, :]
    cosine, sine = jnp.cos(angles), jnp.sin(angles)
    none = jnp.zeros_like(sine)
    rest = jnp.ones((positions.shape[0], 128 - ROT), f32)
    return (
        jnp.concatenate([cosine, cosine, rest], axis=1),
        jnp.concatenate([-sine, none, 0.0 * rest], axis=1),
        jnp.concatenate([none, sine, 0.0 * rest], axis=1),
    )


def mm(a, b):
    return jnp.dot(a, b, preferred_element_type=f32)


def mm_nt(a, b):
    return lax.dot_general(a, b, contract_last, preferred_element_type=f32)


class Order:
    def __init__(self, token):
        self.token = token

    def join(self, *values):
        self.token, values = lax.optimization_barrier((self.token, values))
        return values


def swap(value, axis, distance):
    size = lax.axis_size(axis)
    return lax.ppermute(value, axis, [(i, i ^ distance) for i in range(size)])


def gather_axis(value, axis):
    return [value] + [swap(value, axis, d) for d in range(1, lax.axis_size(axis))]


def gather_start(value):
    size = lax.axis_size("hd")
    return [swap(value, "hd", d) for d in range(1, 3 if size == 4 else size)]


def gather_end(value, near):
    if lax.axis_size("hd") == 4:
        near = [near[0], near[1], swap(near[1], "hd", 1)]
    return [value] + near


def gather_rest(value):
    place, size = lax.axis_index(RP), lax.axis_size(RP)
    blocks = jnp.stack([value] + [swap(value, RP, d) for d in range(1, size)])
    bit = 1
    while bit < size:
        pairs = blocks.reshape((size // (2 * bit), 2, bit) + value.shape)
        turned = jnp.stack([pairs[:, 1], pairs[:, 0]], axis=1).reshape(blocks.shape)
        blocks = jnp.where((place & bit) != 0, turned, blocks)
        bit *= 2
    return blocks


def hand_on(value, distance):
    if lax.axis_size("hd") == 4 and distance == 3:
        distance = 1
    return swap(value, "hd", distance)


def exchange(terms, axis, dim):
    place, size = lax.axis_index(axis), lax.axis_size(axis)
    pick = lambda d: lax.dynamic_index_in_dim(terms, place ^ d, dim, keepdims=False)
    return [pick(0)] + [swap(pick(d), axis, d) for d in range(1, size)]


def spread_group(shard):
    mine = lax.all_to_all(shard, TP, split_axis=0, concat_axis=0, tiled=True)
    return mine.reshape(-1, shard.shape[2])


def spread_rest(mine):
    return lax.all_gather(mine, RP, axis=0, tiled=True)


def collect_rest(terms):
    return lax.psum_scatter(terms, RP, scatter_dimension=0, tiled=True)


def collect_group(mine):
    mine = mine.reshape(lax.axis_size(TP), -1, mine.shape[1])
    return lax.all_to_all(mine, TP, split_axis=0, concat_axis=0, tiled=True)


TILE = 256
KEYS = 2048


def call(kernel, outs, *ins, scratch=(), grid=(), in_specs=None, out_specs=None):
    vmem = pl.BlockSpec(memory_space=pltpu.VMEM)
    return pl.pallas_call(
        kernel,
        grid=grid,
        out_shape=[jax.ShapeDtypeStruct(shape, dtype) for shape, dtype in outs],
        in_specs=in_specs or [vmem] * len(ins),
        out_specs=out_specs or [vmem] * len(outs),
        scratch_shapes=list(scratch),
        compiler_params=pltpu.CompilerParams(vmem_limit_bytes=58 * 2**20),
        cost_estimate=pl.CostEstimate(flops=1, bytes_accessed=1, transcendentals=0),
    )(*ins)


def tiles(count, step):
    def body(i, _):
        step(pl.ds(pl.multiple_of(i * TILE, TILE), TILE))
        return 0

    lax.fori_loop(0, count // TILE, body, 0)


def add(*groups):
    return [
        [sum((x.astype(f32) for x in arrays[1:]), arrays[0].astype(f32)).astype(dtype)]
        for arrays, dtype, _ in groups
    ]


def turn(value, tables, sign):
    own, above, below = tables
    first = value[:, :128]
    turned = first * own + sign * (
        pltpu.roll(first, 96, 1) * above + pltpu.roll(first, 32, 1) * below
    )
    return jnp.concatenate([turned, value[:, 128:]], axis=1)


def statistics(block):
    average = jnp.mean(block, axis=1, keepdims=True)
    centered = block - average
    return average, lax.rsqrt(jnp.mean(centered * centered, axis=1, keepdims=True) + epsilon)


def project_kernel(count, *refs):
    x_refs, refs = refs[:count], refs[count:]
    vec_ref, w_ref, b_ref, own_ref, above_ref, below_ref, *refs = refs
    attn_ref, mlp_ref, q_ref, kv_ref, average_ref, inverse_ref = refs
    rows = x_refs[0].shape[0]
    for start in range(0, count * rows, TILE):
        for i in range(start // rows, (start + TILE) // rows):
            at = slice(i * rows, (i + 1) * rows)
            block = x_refs[i][...].astype(f32)
            average, inverse = statistics(block)
            average_ref[at, :] = average
            inverse_ref[at, :] = inverse
            normed = (block - average) * inverse
            attn_ref[at, :] = (normed * vec_ref[0:1, :] + vec_ref[1:2, :]).astype(bf16)
            mlp_ref[at, :] = (normed * vec_ref[2:3, :] + vec_ref[3:4, :]).astype(bf16)
        at = slice(start, start + TILE)
        project = mm(attn_ref[at, :], w_ref[...]) + b_ref[...]
        tables = own_ref[at, :], above_ref[at, :], below_ref[at, :]
        query = turn(project[:, :HS], tables, 1.0).astype(bf16)
        q_ref[at, :] = (query.astype(f32) * HS**-0.5).astype(bf16)
        kv_ref[at, :HS] = turn(project[:, HS : 2 * HS], tables, 1.0).astype(bf16)
        kv_ref[at, HS:] = project[:, 2 * HS :].astype(bf16)


def cotangent_kernel(count, *refs):
    g_refs, (w_ref, g_ref, out_ref) = refs[:count], refs[count:]
    rows = g_refs[0].shape[0]
    for i in range(count):
        g_ref[i * rows : (i + 1) * rows, :] = g_refs[i][...]

    out_ref[...] = mm(g_ref[...], w_ref[...]).astype(bf16)


def forward_kernel(mlp_ref, w_ref, b_ref, act_ref, slope_ref):
    def step(at):
        value = mm(mlp_ref[at, :], w_ref[...]) + b_ref[...]
        cdf = 0.5 * (1.0 + lax.erf(value * 0.7071067811865476))
        density = jnp.exp(-0.5 * value * value) * 0.3989422804014327
        act_ref[at, :] = (value * cdf).astype(bf16)
        slope_ref[at, :] = cdf + value * density

    tiles(mlp_ref.shape[0], step)


def forward(mlp_in, w_up, b_up):
    count, ffl = mlp_in.shape[0], w_up.shape[1]
    columns = pl.BlockSpec((count, TILE), lambda i: (0, i))
    return call(
        forward_kernel,
        [((count, ffl), bf16), ((count, ffl), f32)],
        mlp_in, w_up, b_up,
        grid=(ffl // TILE,),
        in_specs=[
            pl.BlockSpec((count, D), lambda i: (0, 0)),
            pl.BlockSpec((D, TILE), lambda i: (0, i)),
            pl.BlockSpec((1, TILE), lambda i: (0, i)),
        ],
        out_specs=[columns, columns],
    )


def backward_kernel(g_ref, w_ref, slope_ref, out_ref, sum_ref):
    grad = (mm(g_ref[...], w_ref[...]) * slope_ref[...]).astype(bf16)
    out_ref[...] = grad
    sum_ref[...] = jnp.sum(grad.astype(f32), axis=0, keepdims=True)


def backward(g_all, w_down, slope):
    count, ffl = slope.shape
    columns = pl.BlockSpec((count, TILE), lambda i: (0, i))
    return call(
        backward_kernel,
        [((count, ffl), bf16), ((1, ffl), f32)],
        g_all, w_down, slope,
        grid=(ffl // TILE,),
        in_specs=[
            pl.BlockSpec((count, D), lambda i: (0, 0)),
            pl.BlockSpec((D, TILE), lambda i: (0, i)),
            columns,
        ],
        out_specs=[columns, pl.BlockSpec((1, TILE), lambda i: (0, i))],
    )


def weight_kernel(*refs):
    pairs, out_ref = refs[:-1], refs[-1]
    start = 0
    for lhs_ref, rhs_ref in zip(pairs[::2], pairs[1::2]):
        cols = slice(start, start + rhs_ref.shape[1])
        start += rhs_ref.shape[1]
        out_ref[:, cols] = mm(lhs_ref[...].T, rhs_ref[...]).astype(bf16)


def weight_terms(*pairs):
    count = pairs[0].shape[0]
    cols = sum(rhs.shape[1] for rhs in pairs[1::2])
    specs = []
    for rhs in pairs[1::2]:
        specs.append(pl.BlockSpec((count, 2 * TILE), lambda i: (0, i)))
        specs.append(pl.BlockSpec(rhs.shape, lambda i: (0, 0)))
    return call(
        weight_kernel,
        [((D, cols), bf16)],
        *pairs,
        grid=(D // (2 * TILE),),
        in_specs=specs,
        out_specs=[pl.BlockSpec((2 * TILE, cols), lambda i: (i, 0))],
    )[0]


def weight_half_kernel(per, place_ref, lhs_ref, rhs_ref, *out_refs):
    term = mm(lhs_ref[...].T, rhs_ref[...]).astype(bf16)
    for d, out_ref in enumerate(out_refs):

        @pl.when(pl.program_id(0) // per == d)
        def _(out_ref=out_ref):
            out_ref[...] = term


def weight_half(lhs, rhs, other):
    bh = lax.axis_size("bh")
    part = D // (2 * bh)
    tile = min(TILE, part)
    per = part // tile
    place = jnp.stack([lax.axis_index("dp") ^ other, lax.axis_index("bh")]).astype(jnp.int32)
    count, cols = rhs.shape

    def lhs_at(i, place_ref):
        return (0, (place_ref[0] * bh + (place_ref[1] ^ (i // per))) * per + i % per)

    def out_at(d):
        return lambda i, place_ref: (jnp.clip(i - d * per, 0, per - 1), 0)

    return pl.pallas_call(
        functools.partial(weight_half_kernel, per),
        grid_spec=pltpu.PrefetchScalarGridSpec(
            num_scalar_prefetch=1,
            grid=(bh * per,),
            in_specs=[
                pl.BlockSpec((count, tile), lhs_at),
                pl.BlockSpec((count, cols), lambda i, place_ref: (0, 0)),
            ],
            out_specs=[pl.BlockSpec((tile, cols), out_at(d)) for d in range(bh)],
        ),
        out_shape=[jax.ShapeDtypeStruct((part, cols), bf16)] * bh,
        compiler_params=pltpu.CompilerParams(vmem_limit_bytes=58 * 2**20),
        cost_estimate=pl.CostEstimate(flops=1, bytes_accessed=1, transcendentals=0),
    )(place, lhs, rhs)


def output_kernel(att_ref, act_ref, dense_ref, down_ref, *out_refs):
    term = mm_nt(att_ref[...], dense_ref[...]) + mm_nt(act_ref[...], down_ref[...])
    rows = out_refs[0].shape[0]
    for i, out_ref in enumerate(out_refs):
        out_ref[...] = term[i * rows : (i + 1) * rows].astype(out_ref.dtype)


def output_terms(attended, activated, w_heads, w_down, part, count, rows, dtype):
    ffl, wide = activated.shape[1], 4 * TILE if count * rows <= 512 else 2 * TILE
    return call(
        output_kernel,
        [((rows, D), dtype)] * count,
        attended, activated, w_heads, w_down,
        grid=(D // wide,),
        in_specs=[
            pl.BlockSpec((count * rows, HS), lambda i: (part, 0)),
            pl.BlockSpec((count * rows, ffl), lambda i: (part, 0)),
            pl.BlockSpec((wide, HS), lambda i: (i, 3)),
            pl.BlockSpec((wide, ffl), lambda i: (i, 0)),
        ],
        out_specs=[pl.BlockSpec((rows, wide), lambda i: (0, i))] * count,
    )


def turn_back_kernel(count, *refs):
    dq_ref, refs = refs[0], refs[1:]
    term_refs, (own_ref, above_ref, below_ref, out_ref, sum_ref) = refs[:count], refs[count:]
    sum_ref[...] = jnp.zeros_like(sum_ref)

    def step(at):
        tables = own_ref[at, :], above_ref[at, :], below_ref[at, :]
        grad = term_refs[0][at, :].astype(f32)
        for ref in term_refs[1:]:
            grad += ref[at, :].astype(f32)
        grad = grad.astype(bf16)
        out_ref[at, :HS] = turn(dq_ref[at, :].astype(f32), tables, -1.0).astype(bf16)
        out_ref[at, HS : 2 * HS] = turn(grad[:, :HS].astype(f32), tables, -1.0).astype(bf16)
        out_ref[at, 2 * HS :] = grad[:, HS:]
        sum_ref[...] += jnp.sum(out_ref[at, :].astype(f32), axis=0, keepdims=True)

    tiles(dq_ref.shape[0], step)


def input_kernel(count, *refs):
    x_refs, refs = refs[:count], refs[count:]
    average_ref, inverse_ref, gp_ref, gu_ref, heads_ref, up_ref, vec_ref = refs[:7]
    out_refs, sum_ref = refs[7:-1], refs[-1]
    rows = x_refs[0].shape[0]
    sums = [0.0] * 4
    for start in range(0, count * rows, TILE):
        at = slice(start, start + TILE)
        attn = mm_nt(gp_ref[at, :], heads_ref[...])
        mlp = mm_nt(gu_ref[at, :], up_ref[...])
        block = jnp.concatenate(
            [x_refs[i][...].astype(f32) for i in range(start // rows, (start + TILE) // rows)],
            axis=0,
        )
        normed = (block - average_ref[at, :]) * inverse_ref[at, :]
        for i, term in enumerate((attn * normed, attn, mlp * normed, mlp)):
            sums[i] = sums[i] + jnp.sum(term, axis=0, keepdims=True)
        out = attn * vec_ref[0:1, :] + mlp * vec_ref[2:3, :]
        for i in range(0, TILE, rows):
            out_ref = out_refs[(start + i) // rows]
            out_ref[...] = out[i : i + rows].astype(out_ref.dtype)
    sum_ref[...] = jnp.concatenate(sums, axis=0)


def input_terms(x_blocks, average, inverse, grad_project, grad_pre_up, w_heads, w_up, vectors, own):
    count, ffl = grad_pre_up.shape
    whole = lambda rows, cols: pl.BlockSpec((rows, cols), lambda i: (0, 0))
    block = pl.BlockSpec((x_blocks[0].shape[0], TILE), lambda i: (0, i))
    *terms, sums = call(
        functools.partial(input_kernel, len(x_blocks)),
        [(x.shape, f32 if i < own else bf16) for i, x in enumerate(x_blocks)] + [((4, D), f32)],
        *x_blocks, average, inverse, grad_project, grad_pre_up, w_heads, w_up, vectors,
        grid=(D // TILE,),
        in_specs=[
            *[block] * len(x_blocks),
            whole(count, 1),
            whole(count, 1),
            whole(count, 3 * HS),
            whole(count, ffl),
            pl.BlockSpec((TILE, 3 * HS), lambda i: (i, 0)),
            pl.BlockSpec((TILE, ffl), lambda i: (i, 0)),
            pl.BlockSpec((vectors.shape[0], TILE), lambda i: (0, i)),
        ],
        out_specs=[*[block] * len(x_blocks), pl.BlockSpec((4, TILE), lambda i: (0, i))],
    )
    return terms, sums


def places(block, start, shape, dim, sizes, t):
    rows, tp = sizes
    index = start + lax.broadcasted_iota(jnp.int32, shape, dim)
    device = index // rows
    block = block ^ (device // tp)
    return (block * tp + (t ^ (device % tp))) * rows + index % rows


def attention_kernel(count, sizes, place_ref, q_ref, g_ref, *refs):
    kv_refs, (o_ref, dq_ref), refs = refs[:count], refs[count : count + 2], refs[count + 2 :]
    dkv_refs, sum_ref = refs[:-1], refs[-1]
    t, block, tile = place_ref[0], place_ref[1], 2 * TILE
    keys = jnp.concatenate([ref[:, :HS] for ref in kv_refs], axis=0)
    values = jnp.concatenate([ref[:, HS:] for ref in kv_refs], axis=0)
    keys_turned = keys.T
    values_turned = values.T
    key_places = places(block, 0, (keys.shape[0], 1), 0, sizes, t)
    sum_ref[...] = jnp.zeros_like(sum_ref)
    for start in range(0, q_ref.shape[0], tile):
        at = slice(start, start + tile)
        query = q_ref[at, :]
        grad = g_ref[at, :]
        visible = key_places <= places(block, start, (1, tile), 1, sizes, t)
        scores = jnp.where(visible, mm_nt(keys, query), -1e30)
        weights = jnp.exp(scores - jnp.max(scores, axis=0, keepdims=True))
        weights = weights * (1.0 / jnp.sum(weights, axis=0, keepdims=True))
        weights_low = weights.astype(bf16)
        result = mm(values_turned, weights_low)
        o_ref[at, :] = result.T.astype(bf16)
        sum_ref[:, HS:] += mm(weights_low, grad)
        delta = jnp.sum(result * grad.T.astype(f32), axis=0, keepdims=True)
        score_grad = (weights * (mm_nt(values, grad) - delta)).astype(bf16)
        dq_ref[at, :] = (mm(keys_turned, score_grad).T * (HS**-0.5)).astype(bf16)
        sum_ref[:, :HS] += mm(score_grad, query)
    start = 0
    for ref in dkv_refs:
        ref[...] = sum_ref[start : start + ref.shape[0], :].astype(bf16)
        start += ref.shape[0]


def long_attention_kernel(sizes, place_ref, q_ref, g_ref, kv_ref, o_ref, dq_ref, dkv_ref, sum_ref):
    blocks = kv_ref.shape[0] // KEYS
    t, block = place_ref[0], place_ref[1]
    sum_ref[...] = jnp.zeros_like(sum_ref)

    def step(at):
        query = q_ref[at, :]
        grad = g_ref[at, :]
        query_places = places(block, at.start, (1, TILE), 1, sizes, t)

        def scores_of(j):
            here = pl.ds(pl.multiple_of(j * KEYS, KEYS), KEYS)
            visible = places(block, j * KEYS, (KEYS, 1), 0, sizes, t) <= query_places
            return here, jnp.where(visible, mm_nt(kv_ref[here, :HS], query), -1e30)

        def first(j, state):
            top, total = state
            _, scores = scores_of(j)
            higher = jnp.maximum(top, jnp.max(scores, axis=0, keepdims=True))
            now = jnp.sum(jnp.exp(scores - higher), axis=0, keepdims=True)
            return higher, total * jnp.exp(top - higher) + now

        row = (1, TILE)
        top, total = lax.fori_loop(
            0, blocks, first, (jnp.full(row, -1e30, f32), jnp.zeros(row, f32))
        )
        inverse = 1.0 / total

        def second(j, result):
            here, scores = scores_of(j)
            weights = jnp.exp(scores - top) * inverse
            return result + mm(kv_ref[here, HS:].T, weights.astype(bf16))

        result = lax.fori_loop(0, blocks, second, jnp.zeros((HS, TILE), f32))
        o_ref[at, :] = result.T.astype(bf16)
        delta = jnp.sum(result * grad.T.astype(f32), axis=0, keepdims=True)

        def third(j, result):
            here, scores = scores_of(j)
            weights = jnp.exp(scores - top) * inverse
            weight_grad = mm_nt(kv_ref[here, HS:], grad)
            score_grad = (weights * (weight_grad - delta)).astype(bf16)
            sum_ref[here, HS:] += mm(weights.astype(bf16), grad)
            sum_ref[here, :HS] += mm(score_grad, query)
            return result + mm(kv_ref[here, :HS].T, score_grad)

        result = lax.fori_loop(0, blocks, third, jnp.zeros((HS, TILE), f32))
        dq_ref[at, :] = (result.T * (HS**-0.5)).astype(bf16)

    tiles(q_ref.shape[0], step)
    dkv_ref[...] = sum_ref[...].astype(bf16)


def attention(query, grad, kv_blocks, sizes):
    place = jnp.stack([lax.axis_index(TP), lax.axis_index("bh")]).astype(jnp.int32)
    count, total = len(kv_blocks), sum(block.shape[0] for block in kv_blocks)
    low = (query.shape, bf16)
    scratch = [pltpu.VMEM((total, 2 * HS), f32)]
    vmem = pl.BlockSpec(memory_space=pltpu.VMEM)
    smem = pl.BlockSpec(memory_space=pltpu.SMEM)
    if total <= KEYS:
        attended, grad_query, *grad_kv = call(
            functools.partial(attention_kernel, count, sizes),
            [low, low] + [(block.shape, bf16) for block in kv_blocks],
            place, query, grad, *kv_blocks,
            scratch=scratch,
            in_specs=[smem] + [vmem] * (2 + count),
        )
        return attended, grad_query, grad_kv
    kv_all = jnp.concatenate(kv_blocks, axis=0)
    attended, grad_query, grad_kv = call(
        functools.partial(long_attention_kernel, sizes),
        [low, low, (kv_all.shape, bf16)],
        place, query, grad, kv_all,
        scratch=scratch,
        in_specs=[smem] + [vmem] * 3,
    )
    return attended, grad_query, jnp.split(grad_kv, count, axis=0)


def per_device(
    hidden_in,
    gain_attn,
    shift_attn,
    gain_mlp,
    shift_mlp,
    qkv_weight,
    qkv_bias,
    dense_weight,
    up_weight,
    up_bias,
    down_weight,
    out_bias,
    cotangent,
):
    seq_count, sub_len, _ = hidden_in.shape
    tp, rp = lax.axis_size(TP), lax.axis_size(RP)
    n_dev = lax.axis_size(ALL)
    t = lax.axis_index(TP)
    bh, bh_size, bl_size = lax.axis_index("bh"), lax.axis_size("bh"), lax.axis_size("bl")
    rows = qkv_weight.shape[0]
    ff = up_weight.shape[1]
    ffl = ff // tp
    group_len = sub_len * tp

    vmem = pl.BlockSpec(memory_space=pltpu.VMEM)
    x_own = hidden_in.reshape(sub_len, D)
    join = Order(out_bias).join
    g_own = cotangent.reshape(sub_len, D)
    smalls = jnp.concatenate(
        [
            vector.reshape(-1, rows)
            for vector in (
                gain_attn, shift_attn, gain_mlp, shift_mlp, out_bias, qkv_bias, up_bias
            )
        ],
        axis=0,
    )
    kinds = smalls.shape[0]
    count = kinds * rows
    smalls = jnp.pad(smalls.reshape(1, count), ((0, 7), (0, 4 * HS - count)))
    heads_own = jnp.concatenate(
        [
            qkv_weight.reshape(rows, 3, HEADS, HS).transpose(2, 0, 1, 3).reshape(HEADS, rows, 3 * HS),
            dense_weight.reshape(rows, HEADS, HS).transpose(1, 0, 2),
        ],
        axis=2,
    )
    heads_own = jnp.concatenate(
        [heads_own, jnp.broadcast_to(smalls[None], (tp,) + smalls.shape)], axis=1
    )
    up_own = up_weight.reshape(rows, tp, ffl).transpose(1, 0, 2)
    down_own = down_weight.reshape(rows, tp, ffl).transpose(1, 0, 2)

    x_near = gather_start(x_own)
    x_side = gather_axis(x_own, "bl")
    g_side = gather_axis(g_own, "bl")
    x_near, x_side, g_side, heads_own, up_own, down_own = join(
        x_near, x_side, g_side, heads_own, up_own, down_own
    )
    m_heads = lax.all_to_all(heads_own, TP, split_axis=0, concat_axis=0, tiled=True)
    x_rows = [x_side, gather_axis(x_near[0], "bl")]
    x_second = x_near[1]
    x_left = gather_axis(x_second[: sub_len // 2], "bl")[1:]
    x_near = gather_end(x_own, x_near)
    row = jnp.arange(group_len, dtype=jnp.int32)
    inside = ((row // sub_len) ^ t) * sub_len + row % sub_len
    query_places = bh * group_len + inside
    tables = rotary_tables(query_places.astype(f32))
    x_near, x_rows, x_left, m_heads, up_own, g_late, tables, down_own, x_second = join(
        x_near, x_rows, x_left, m_heads, up_own, g_own, tables, down_own, x_second
    )
    x_right = gather_axis(x_second[sub_len // 2 :], "bl")[1:]
    w_heads = spread_rest(m_heads[:, :rows].reshape(tp * rows, -1))
    x_rows += [None] + [gather_axis(block, "bl") for block in x_near[3:]]
    g_first = swap(g_late, "hd", 1)
    m_up = spread_group(up_own)
    smalls = gather_rest(m_heads[:, rows, :count]).reshape(n_dev, kinds, rows).astype(f32)
    vectors = smalls[:, :5].transpose(1, 0, 2).reshape(5, D)
    nq = qkv_bias.shape[0] // rows
    b_qkv = smalls[:, 5 : 5 + nq].reshape(3, HEADS, HS)
    b_up = smalls[:, 5 + nq :].reshape(tp, ffl)
    b_qkv = lax.dynamic_index_in_dim(b_qkv, t, 1, keepdims=False).reshape(1, 3 * HS)
    b_up = lax.dynamic_index_in_dim(b_up, t, 0, keepdims=True)

    x_rows, x_right, g_first, m_up, g_late, down_own, vectors, b_qkv, b_up = join(
        x_rows, x_right, g_first, m_up, g_late, down_own, vectors, b_qkv, b_up
    )
    x_rows[2] = [x_second] + [
        jnp.concatenate(halves, axis=0) for halves in zip(x_left, x_right)
    ]
    w_up = spread_rest(m_up)
    x_blocks = [row[far] for far in range(bl_size) for row in x_rows]
    g_rows = [g_side, gather_axis(g_first, "bl")]
    hd_size = lax.axis_size("hd")
    four = hd_size == 4
    g_near = [g_first] + [swap(g_late, "hd", d) for d in range(2, 3 if hd_size == 4 else hd_size)]
    attn_in, mlp_in, query, kv, average, inverse = call(
        functools.partial(project_kernel, tp),
        [
            ((group_len, D), bf16),
            ((group_len, D), bf16),
            ((group_len, HS), bf16),
            ((group_len, 2 * HS), bf16),
            ((group_len, 1), f32),
            ((group_len, 1), f32),
        ],
        *x_blocks, vectors, w_heads, b_qkv, *tables,
        grid=(1,),
        in_specs=[vmem] * (tp + 1) + [pl.BlockSpec((D, 3 * HS), lambda i: (0, 0))] + [vmem] * 4,
    )
    g_rows, g_near, kv, mlp_in, g_late, down_own = join(
        g_rows, g_near, kv, mlp_in, g_late, down_own
    )
    g_near = gather_end(g_late, g_near)
    g_rows += [gather_axis(block, "bl") for block in g_near[2:3]]
    g_rows, g_near, down_own, mlp_in = join(g_rows, g_near, down_own, mlp_in)
    g_rows += [gather_axis(block, "bl") for block in g_near[3:]]
    kv_blocks = gather_axis(kv, "bh")
    m_down = spread_group(down_own)
    activated, slope = forward(mlp_in, w_up, b_up)
    g_rows, kv_blocks, m_down, activated, slope = join(g_rows, kv_blocks, m_down, activated, slope)
    w_down = spread_rest(m_down)
    g_blocks = [row[far] for far in range(bl_size) for row in g_rows]
    g_all, grad_att = call(
        functools.partial(cotangent_kernel, tp),
        [((group_len, D), bf16), ((group_len, HS), bf16)],
        *g_blocks, w_heads,
        grid=(1,),
        in_specs=[vmem] * tp + [pl.BlockSpec((D, HS), lambda i: (0, 3))],
    )
    down_far = weight_half(g_all, activated, 1)
    down_far, grad_att, g_all = join(down_far, grad_att, g_all)
    down_far = [swap(terms, "dp", 1) for terms in reversed(down_far)][::-1]
    down_own = weight_half(g_all, activated, 0)
    down_far, down_own, grad_att = join(down_far, down_own, grad_att)
    down_sent = add(*[([down_far[d], down_own[d]], bf16, 1) for d in range(1, bh_size)])
    down_sent, grad_att = join(down_sent, grad_att)
    down_others = [swap(sent[0], "bh", d + 1) for d, sent in enumerate(down_sent)]
    attended, grad_query, grad_kv = attention(query, grad_att, kv_blocks, (sub_len, tp))
    hd_terms = (hd_size, sub_len)
    out_far = [
        output_terms(attended, activated, w_heads, w_down, far, *hd_terms, bf16)
        for far in range(1, bl_size)
    ]
    out_own = output_terms(attended, activated, w_heads, w_down, 0, *hd_terms, f32)
    down_others, out_far, attended, slope, out_own = join(
        down_others, out_far, attended, slope, out_own
    )
    part = hd_size // 4
    parts = [range(hd_size - (g + 1) * part, hd_size - g * part) for g in range(4)]

    def over_bl(terms, ds):
        return {d: [swap(term[d], "bl", f + 1) for f, term in enumerate(terms)] for d in ds}

    def sums_of(own, received, ds, handed=()):
        return [
            ([own[d], *received[d], *(handed if d == 2 else ())], f32 if d == 0 else bf16, 1)
            for d in ds
        ]

    ((down_last,),) = add(([down_far[0], down_own[0], *down_others], bf16, 1))
    down_last, attended, slope = join(down_last, attended, slope)
    kv_others = [swap(grad_kv[d], "bh", d) for d in range(1, bh_size)]
    down_grad = collect_group(down_last)
    received = over_bl(out_far, parts[0])
    grad_pre_up, up_bias_term = backward(g_all, w_down, slope)
    up_terms = weight_terms(mlp_in, grad_pre_up)
    kv_others, down_grad, received, grad_pre_up, out_far, up_terms = join(
        kv_others, down_grad, received, grad_pre_up, out_far, up_terms
    )
    up_mine = collect_rest(up_terms)
    out = dict(zip(parts[0], add(*sums_of(out_own, received, parts[0]))))
    out, kv_others = join(out, kv_others)
    out_near = {d: hand_on(out[d][0], d) for d in parts[0]}
    middle = [*parts[1], *parts[2]]
    received = over_bl(out_far, middle)
    grad_project, qkv_bias_term = call(
        functools.partial(turn_back_kernel, bh_size),
        [((group_len, 3 * HS), bf16), ((1, 3 * HS), f32)],
        grad_query, grad_kv[0], *kv_others, *tables,
    )
    in_terms, sums = input_terms(
        x_blocks, average, inverse, grad_project, grad_pre_up, w_heads, w_up, vectors, hd_size
    )
    in_own = in_terms[:hd_size]
    in_far = [in_terms[f * hd_size : (f + 1) * hd_size] for f in range(1, bl_size)]
    out_near, received, out_far, in_far, grad_project = join(
        out_near, received, out_far, in_far, grad_project
    )
    out = add(*sums_of(out_own, received, middle, [out_near[3]] if four else []))
    out, in_far, grad_project = join(out, in_far, grad_project)
    out_near |= {d: hand_on(term, d) for d, (term,) in zip(middle, out)}
    received = over_bl(out_far, parts[3])
    received_in = over_bl(in_far, parts[0])
    heads_terms = weight_terms(attn_in, grad_project, g_all, attended)
    sums = jnp.concatenate([sums, jnp.sum(g_own.astype(f32), axis=0, keepdims=True)], axis=0)
    qkv_bias_full = lax.dynamic_update_slice(
        jnp.zeros((3, HEADS, HS), f32), qkv_bias_term.reshape(3, 1, HS), (0, t, 0)
    )
    up_bias_full = lax.dynamic_update_slice(jnp.zeros((tp, ffl), f32), up_bias_term, (t, 0))
    small_terms = jnp.concatenate(
        [
            sums.reshape(5, n_dev, rows).transpose(1, 0, 2),
            qkv_bias_full.reshape(n_dev, nq, rows),
            up_bias_full.reshape(n_dev, -1, rows),
        ],
        axis=1,
    )
    out_near, received, received_in, heads_terms, up_mine, in_far, small = join(
        out_near, received, received_in, heads_terms, up_mine, in_far, small_terms
    )
    heads_mine = collect_rest(heads_terms)
    ins = add(*sums_of(in_own, received_in, parts[0]))
    ins, up_mine, in_far = join(ins, up_mine, in_far)
    up_grad = collect_group(up_mine)
    in_near = {d: hand_on(term, d) for d, (term,) in zip(parts[0], ins)}
    received_in = over_bl(in_far, middle)
    small = exchange(small.reshape(rp, bl_size, hd_size, kinds, rows), RP, 0)
    up_grad, in_near, received_in, small, in_far = join(
        up_grad, in_near, received_in, small, in_far
    )
    ins = add(*sums_of(in_own, received_in, middle, [in_near[3]] if four else []))
    in_far, heads_mine, small = join(in_far, heads_mine, small)
    heads_grad = collect_group(heads_mine)
    received_in = over_bl(in_far, parts[3])
    down_grad = down_grad.astype(f32).transpose(1, 0, 2).reshape(rows, ff)
    up_grad = up_grad.astype(f32).transpose(1, 0, 2).reshape(rows, ff)
    small = exchange(sum(small[1:], small[0]), "hd", 1)
    heads_grad, received_in, down_grad, up_grad, ins, small = join(
        heads_grad, received_in, down_grad, up_grad, ins, small
    )
    in_near |= {d: hand_on(term, d) for d, (term,) in zip(middle, ins)}
    small = exchange(sum(small[1:], small[0]), "bl", 0)
    heads_grad = heads_grad.astype(f32)
    dense_grad = heads_grad[:, :, 3 * HS :].transpose(1, 0, 2).reshape(rows, D)
    qkv_grad = (
        heads_grad[:, :, : 3 * HS]
        .reshape(tp, rows, 3, HS)
        .transpose(1, 2, 0, 3)
        .reshape(rows, 3 * D)
    )

    def total(own, received, near):
        rest = {d: sum((x.astype(f32) for x in received[d]), own[d]) for d in received}
        near = near | {d: hand_on(rest[d].astype(bf16), d) for d in rest if d}
        straight = [d for d in range(1, hd_size) if not (four and d == 3)]
        return sum((near[d].astype(f32) for d in straight), rest[0])

    projected = total(out_own, received, out_near)
    output = (x_own.astype(f32) + projected + vectors[4:5]).astype(bf16)
    small = sum(small[1:], small[0])
    smalls = [small[i] for i in range(5)]
    smalls += [small[5 : 5 + nq].reshape(-1), small[5 + nq :].reshape(-1)]
    in_near, received_in, smalls, dense_grad, qkv_grad, output, in_own = join(
        in_near, received_in, smalls, dense_grad, qkv_grad, output, in_own
    )
    grad_normed = total(in_own, received_in, in_near)
    own = x_own.astype(f32)
    own_average, own_inverse = statistics(own)
    own_normed = (own - own_average) * own_inverse
    grad_hidden = g_own.astype(f32) + own_inverse * (
        grad_normed
        - jnp.mean(grad_normed, axis=1, keepdims=True)
        - own_normed * jnp.mean(grad_normed * own_normed, axis=1, keepdims=True)
    )
    return (
        output.reshape(seq_count, sub_len, D),
        grad_hidden.reshape(seq_count, sub_len, D),
        *smalls[:4],
        qkv_grad,
        smalls[5],
        dense_grad,
        up_grad,
        smalls[6],
        down_grad,
        smalls[4],
    )


def solution(mesh):
    dp, blk, hd = (mesh.shape[name] for name in ("dp", "blk", "hd"))
    low = HEADS // hd
    inner = Mesh(mesh.devices.reshape(dp, blk // low, low, hd), ALL)
    token = P("dp", ("bh", "bl", "hd"), None)
    vector = P(ALL)
    matrix = P(ALL, None)
    return jax.shard_map(
        per_device,
        mesh=inner,
        in_specs=(
            token, vector, vector, vector, vector, matrix, vector,
            matrix, matrix, vector, matrix, vector, token,
        ),
        out_specs=(
            token, token, vector, vector, vector, vector, matrix, vector,
            matrix, matrix, vector, matrix, vector,
        ),
        check_vma=False,
    )
```
